128 devices in a mesh: clip: 32 (over y_lo, x, z), stripe: 4 (over y_hi, core).
Axes of the slice: x: 4, y: 4 (y_hi: 2, y_lo: 2; y = y_hi * 2 + y_lo), z: 4, core: 2. Of those that a mesh axis runs over, the one named last changes fastest.
Arguments:
- clip_tokens: bfloat16 [32, 4, 256, 768], P('clip', None, 'stripe'), may hold values from -6 to 6
- timesteps: int32 [32], P('clip'), may hold values from 0 to 999
- loss_weight: float32 [32], P('clip'), may hold values from 0.2 to 5
- cotangent: bfloat16 [32, 4, 256, 768], P('clip', None, 'stripe'), may hold values from -6 to 6
- w_mod: bfloat16 [2, 768, 4608], P(None, None, 'stripe'), may hold values from -0.21875 to 0.21875
- b_mod: bfloat16 [2, 4608], P(None, 'stripe'), may hold values from -3 to 3
- w_qkv: bfloat16 [2, 768, 2304], P(None, 'stripe'), may hold values from -0.21875 to 0.21875
- w_out: bfloat16 [2, 768, 768], P(None, 'stripe'), may hold values from -0.625 to 0.625
- w_up: bfloat16 [2, 768, 3072], P(None, 'stripe'), may hold values from -0.21875 to 0.21875
- b_up: bfloat16 [2, 3072], P(None, 'stripe'), may hold values from -3 to 3
- w_down: bfloat16 [2, 3072, 768], P(None, 'stripe'), may hold values from -0.109375 to 0.109375
Outputs:
- block_output: bfloat16 [32, 4, 256, 768], P('clip', None, 'stripe')
- grad_input: float32 [32, 4, 256, 768], P('clip', None, 'stripe')
- grad_w_mod: float32 [2, 768, 4608], P(None, None, 'stripe')
- grad_b_mod: float32 [2, 4608], P(None, 'stripe')
- grad_w_qkv: float32 [2, 768, 2304], P(None, 'stripe')
- grad_w_out: float32 [2, 768, 768], P(None, 'stripe')
- grad_w_up: float32 [2, 768, 3072], P(None, 'stripe')
- grad_b_up: float32 [2, 3072], P(None, 'stripe')
- grad_w_down: float32 [2, 3072, 768], P(None, 'stripe')
The draws below stay inside these ranges and needn't reach their ends.
All inputs are finite; a program needn't handle non-finite values.
Results may differ from the reference program's by a relative error of at most 0.033.
Values may be sent and summed in bfloat16 or wider, within the bound.
A program may use at most 192 MiB of HBM per device.

```python
import math
import jax
import jax.numpy as jnp
import numpy as np
from jax import lax

D = 768
HEAD = 64
FF = 3072
FRAMES = 4
PATCHES = 256
LAYERS = 2
STEPS = 1000
CLIPS = 32


def set_ends(drawn, key, least, high):
    index_at = [jax.random.randint(jax.random.fold_in(key, axis), (), 0, length) for axis, length in enumerate(drawn.shape)]
    main_axis = drawn.shape.index(max(drawn.shape))
    neighbour = index_at[:main_axis] + [(index_at[main_axis] + 1) % drawn.shape[main_axis]] + index_at[main_axis + 1:]
    return drawn.at[tuple(index_at)].set(least).at[tuple(neighbour)].set(high)


def shard_levels(rng, shape, pieces, least, top_value):
    def one(position, shards_of):
        draws = jax.random.uniform(jax.random.fold_in(jax.random.fold_in(rng, 6), position), (shards_of,), jnp.float32, least / len(pieces), top_value / len(pieces))
        return jnp.repeat(jnp.exp(draws), shape[position] // shards_of).reshape((-1,) + (1,) * (len(shape) - position - 1))

    gain = one(*pieces[0])
    for cut in pieces[1:]:
        gain = gain * one(*cut)
    return gain


def rank_bounds(number_of, lean):
    weights = [(1 << 20) // math.isqrt(rank ** lean) + 1 for rank in range(1, number_of + 1)]
    deviation = 1 + sum(weights) // (1 << 30)
    return np.cumsum(np.array([max(1, weight // deviation) for weight in weights]))


def ranked(stream_key, shape, amount, slope):
    grid = rank_bounds(amount, slope)
    lot = jax.random.randint(jax.random.fold_in(stream_key, 1), shape, 0, int(grid[amount - 1]))
    standing = jnp.searchsorted(jnp.asarray(grid, jnp.int32), lot, side="right")
    return jax.random.permutation(jax.random.fold_in(stream_key, 2), amount)[standing].astype(jnp.int32)


def gaussian(own_key, dims, scale, most, cuts=(), kind=jnp.bfloat16):
    drawn = jax.random.normal(own_key, dims, jnp.float32) * scale
    if len(cuts) > 0:
        drawn = shard_levels(own_key, dims, cuts, -0.22, 0.18) * drawn
    return jnp.clip(drawn, min=-most, max=most).astype(kind)


def setup_inputs(seed: int = 0) -> dict:
    key_of = jax.random.split(jax.random.key(seed), 12)
    return {
        "clip_tokens": gaussian(key_of[0], (CLIPS, FRAMES, PATCHES, D), 1.0, 6.0, ((0, 32), (2, 4))),
        "timesteps": set_ends(ranked(key_of[1], (CLIPS,), STEPS, 2), jax.random.fold_in(key_of[1], 3), 0, STEPS - 1).astype(jnp.int32),
        "loss_weight": jnp.clip(jnp.exp(math.log(5.0) - 3.218876 * jax.random.uniform(key_of[2], (CLIPS,), jnp.float32) ** shard_levels(key_of[2], (CLIPS,), ((0, 32),), -0.2, 0.2)), 0.2, 5.0),
        "cotangent": gaussian(key_of[3], (CLIPS, FRAMES, PATCHES, D), 1.0, 6.0, ((0, 32), (2, 4))),
        "w_mod": gaussian(key_of[4], (LAYERS, D, 6 * D), D ** -0.5, 0.21875, ((2, 4),)),
        "b_mod": gaussian(key_of[5], (LAYERS, 6 * D), 0.5, 3.0, ((1, 4),)),
        "w_qkv": gaussian(key_of[6], (LAYERS, D, 3 * D), D ** -0.5, 0.21875, ((1, 4),)),
        "w_out": gaussian(key_of[7], (LAYERS, D, D), (D // 8) ** -0.5, 0.625, ((1, 4),)),
        "w_up": gaussian(key_of[8], (LAYERS, D, FF), D ** -0.5, 0.21875, ((1, 4),)),
        "b_up": gaussian(key_of[9], (LAYERS, FF), 0.5, 3.0, ((1, 4),)),
        "w_down": gaussian(key_of[10], (LAYERS, FF, D), FF ** -0.5, 0.109375, ((1, 4),)),
    }


@jax.custom_vjp
def low(v):
    return lax.optimization_barrier(v.astype(jnp.bfloat16)).astype(jnp.float32)

@jax.custom_vjp
def low_back(v):
    return v

def low_keep(v):
    return (low(v), None)

def low_pass(kept, grad):
    return (grad,)

def back_keep(v):
    return (v, None)

def back_low(kept, grad):
    return (low(grad),)
low.defvjp(low_keep, low_pass)
low_back.defvjp(back_keep, back_low)
spatial_forms = ('fqhe,fkhe->fhqk', 'fhqk,fkhe->fqhe')
temporal_forms = ('qphe,kphe->phqk', 'phqk,kphe->qphe')
highest = lax.Precision.HIGHEST

def norm_rows(values):
    centred = values - lax.optimization_barrier(jnp.mean(values, axis=-1, keepdims=True))
    spread = lax.optimization_barrier(jnp.mean(centred * centred, axis=-1, keepdims=True))
    return centred * lax.rsqrt(spread + 1e-06)

def modulate(values, shift, scale):
    return norm_rows(values) * (1.0 + scale) + shift

def gelu_tanh(values):
    return 0.5 * values * (1.0 + jnp.tanh(0.7978845608028654 * (values + 0.044715 * values * values * values)))

def silu_plain(values):
    return values / (1.0 + jnp.exp(-values))

def sinusoid(steps, width):
    half = width // 2
    freqs = jnp.exp(-math.log(10000.0) * jnp.arange(half).astype(jnp.float32) / half)
    angles = steps.astype(jnp.float32)[:, None] * freqs[None, :]
    return jnp.concatenate([jnp.cos(angles), jnp.sin(angles)], axis=1)

def attention(query, key, value, forms):
    scale = HEAD ** (-0.5)
    raw = low_back(jnp.einsum(forms[0], query, key, precision=highest))
    scores = raw * scale
    top = lax.optimization_barrier(jnp.max(scores, axis=-1, keepdims=True))
    expo = jnp.exp(scores - top)
    probs = low(expo / lax.optimization_barrier(jnp.sum(expo, axis=-1, keepdims=True)))
    return jnp.einsum(forms[1], probs, value, precision=highest)

def block(rows, embed, params, layer):
    w_mod, b_mod, w_qkv, w_out, w_up, b_up, w_down = [p[layer] for p in params]
    mod = jnp.dot(embed[None, :], w_mod, precision=highest)[0] + b_mod
    shift1, scale1, gate1, shift2, scale2, gate2 = jnp.split(mod, 6)
    width = rows.shape[1]
    heads = width // HEAD
    normed1 = low(modulate(rows, shift1, scale1))
    qkv = low_back(low(jnp.dot(normed1, w_qkv, precision=highest)))
    per_frame = rows.shape[0] // FRAMES
    query = qkv[:, :width].reshape(FRAMES, per_frame, heads, HEAD)
    key = qkv[:, width:2 * width].reshape(FRAMES, per_frame, heads, HEAD)
    value = qkv[:, 2 * width:].reshape(FRAMES, per_frame, heads, HEAD)
    forms = spatial_forms if layer % 2 == 0 else temporal_forms
    attended = attention(query, key, value, forms).reshape(rows.shape[0], width)
    attended = low_back(low(attended))
    branch = low_back(jnp.dot(attended, w_out, precision=highest))
    mid = rows + gate1 * branch
    normed2 = low(modulate(mid, shift2, scale2))
    pre = low_back(jnp.dot(normed2, w_up, precision=highest) + b_up)
    hidden = low(gelu_tanh(pre))
    mlp = low_back(jnp.dot(hidden, w_down, precision=highest))
    return mid + gate2 * mlp

def add_trees(left, right):
    return jax.tree.map(jnp.add, left, right)

def reference(clip_tokens, timesteps, loss_weight, cotangent, w_mod, b_mod, w_qkv, w_out, w_up, b_up, w_down):
    params = tuple((p.astype(jnp.float32) for p in (w_mod, b_mod, w_qkv, w_out, w_up, b_up, w_down)))
    embeds = low(silu_plain(sinusoid(timesteps, D)))

    def per_clip(totals, item):
        tokens, embed, weight, cot = item
        start = tokens.reshape(FRAMES * PATCHES, D).astype(jnp.float32)

        def forward(rows, weights):
            for layer in range(LAYERS):
                rows = block(rows, embed, weights, layer)
            return rows
        result, pull = jax.vjp(forward, start, params)
        grad_rows, grad_params = pull(cot.reshape(FRAMES * PATCHES, D).astype(jnp.float32) * weight)
        totals = add_trees(totals, grad_params)
        return (totals, (result.astype(jnp.bfloat16).reshape(FRAMES, PATCHES, D), grad_rows.reshape(FRAMES, PATCHES, D)))
    zeros = jax.tree.map(jnp.zeros_like, params)
    totals, (outputs, grads) = lax.scan(per_clip, zeros, (clip_tokens, embeds, loss_weight, cotangent))
    return (outputs, grads, totals[0], totals[1], totals[2], totals[3], totals[4], totals[5], totals[6])
```

```python
import functools
import math

import jax
import jax.numpy as jnp
from jax import lax
from jax.experimental import pallas as pl
from jax.experimental.pallas import tpu as pltpu
from jax.sharding import PartitionSpec as P

HEAD = 64
MESH = pl.DeviceIdType.MESH
bf16 = jnp.bfloat16
f32 = jnp.float32
spatial_forms = ("fqhe,fkhe->fhqk", "fhqk,fkhe->fqhe", "fhqk,fqhe->fkhe")
temporal_forms = ("qphe,kphe->phqk", "phqk,kphe->qphe", "phqk,qphe->kphe")


class Place:
    def __init__(self):
        clip, stripe = lax.axis_index("clip"), lax.axis_index("stripe")
        self.clip, self.stripe = clip, stripe
        self.ylo = lax.div(clip, 16)
        self.x = lax.rem(lax.div(clip, 4), 4)
        self.z = lax.rem(clip, 4)
        self.yhi = lax.div(stripe, 2)
        self.core = lax.rem(stripe, 2)

    def at_x(self, x):
        return (self.ylo * 16 + x * 4 + self.z, self.stripe)

    def at_z(self, z):
        return (self.ylo * 16 + self.x * 4 + z, self.stripe)

    def ring(self, axis, step):
        there = lax.rem((self.x if axis == 0 else self.z) + step, 4)
        return (self.at_x(there) if axis == 0 else self.at_z(there)), there

    def on_ring(self, axis):
        return self.x if axis == 0 else self.z

    def sibling(self):
        return (self.clip, self.yhi * 2 + 1 - self.core)

    def mirror(self):
        return ((1 - self.ylo) * 16 + self.x * 4 + self.z, (1 - self.yhi) * 2 + self.core)

    def twin(self):
        return ((1 - self.ylo) * 16 + self.x * 4 + self.z, self.stripe)

    def in_group(self, step):
        there = lax.rem(self.stripe + step, 4)
        return (self.clip, there), there


def enter(devices):
    barrier = pltpu.get_barrier_semaphore()
    for device in devices:
        pl.semaphore_signal(barrier, inc=1, device_id=device, device_id_type=MESH)
    pl.semaphore_wait(barrier, len(devices))


class Sems:
    def __init__(self, send, recv):
        self.send, self.recv, self.used = send, recv, 0

    def copy(self, src, dst, device):
        at = self.used
        self.used += 1
        return pltpu.make_async_remote_copy(
            src_ref=src,
            dst_ref=dst,
            send_sem=self.send.at[at],
            recv_sem=self.recv.at[at],
            device_id=device,
            device_id_type=MESH,
        )


def rows_at(start, size, grain):
    return pl.ds(pl.multiple_of(start * grain, grain), size)


def gather_matrix(place, sems, own, full):
    rows, columns = own.shape
    quarter, half = rows // 4, columns // 2
    other = (1 - place.yhi) * 2 + place.core
    parts = []
    for axis in range(2):
        parts.append((axis, pl.ds(axis * half, half)))
    state = {}

    def begin():
        first = []
        for axis, cols in parts:
            mine = rows_at(place.on_ring(axis), quarter, quarter)
            first.append(
                sems.copy(own.at[mine, cols], full.at[place.stripe, mine, cols], place.mirror())
            )
        state["side"] = sems.copy(own, full.at[place.stripe], place.sibling())
        for copy in first:
            copy.start()
        state["side"].start()
        state["first"] = first

    def spread():
        state["ring"] = []
        for axis, cols in parts:
            state["first"][axis].wait()
            mine = rows_at(place.on_ring(axis), quarter, quarter)
            piece = full.at[other, mine, cols]
            for step in (1, 3, 2):
                device, _ = place.ring(axis, step)
                copy = sems.copy(piece, piece, device)
                copy.start()
                state["ring"].append(copy)

    def share():
        state["last"] = []
        for axis, cols in parts:
            for copy in state["ring"][axis * 3 : axis * 3 + 3]:
                copy.wait()
            piece = full.at[other, :, cols]
            copy = sems.copy(piece, piece, place.sibling())
            copy.start()
            state["last"].append(copy)

    def end():
        state["side"].wait()
        for copy in state["last"]:
            copy.wait()

    return begin, spread, share, end


def gather_kernel(
    small, tokens, w_qkv, w_out, w_up, w_down, all_small, frame, q_all, o_all, u_all, d_all,
    send, recv, local
):
    place = Place()
    peers = [place.sibling(), place.mirror()]
    peers += [place.ring(axis, step)[0] for axis in range(2) for step in (1, 2, 3)]
    peers += [(place.clip, lax.rem(place.stripe + 2, 4)), (place.clip, 3 - place.stripe)]
    enter(peers)
    sems = Sems(send, recv)
    quick = []
    for step in (1, 2, 3):
        device, there = place.in_group(step)
        quick.append(sems.copy(small, all_small.at[place.stripe], device))
        quick.append(sems.copy(tokens.at[there], frame.at[place.stripe], device))
    for copy in quick:
        copy.start()
    kept = [
        pltpu.make_async_copy(small, all_small.at[place.stripe], local.at[0]),
        pltpu.make_async_copy(tokens.at[place.stripe], frame.at[place.stripe], local.at[1]),
    ]
    plans = []
    for layer in range(2):
        for member, (own, full) in enumerate(
            ((w_qkv, q_all), (w_out, o_all), (w_up, u_all), (w_down, d_all))
        ):
            plans.append(gather_matrix(place, sems, own.at[layer], full.at[layer]))
            kept.append(
                pltpu.make_async_copy(
                    own.at[layer], full.at[layer, place.stripe], local.at[2 + layer * 4 + member]
                )
            )
    for plan in plans:
        plan[0]()
    for copy in kept:
        copy.start()
    for at in range(len(plans) + 2):
        if at < len(plans):
            plans[at][1]()
        if 0 <= at - 1 < len(plans):
            plans[at - 1][2]()
        if 0 <= at - 2 < len(plans):
            plans[at - 2][3]()
    for copy in quick + kept:
        copy.wait()


def gather(small, tokens, w_qkv, w_out, w_up, w_down):
    anywhere = pl.BlockSpec(memory_space=pl.ANY)
    shapes = [(4, *small.shape), tokens.shape]
    shapes += [(2, 4, *w.shape[1:]) for w in (w_qkv, w_out, w_up, w_down)]
    types = [f32] + [bf16] * 5
    return pl.pallas_call(
        gather_kernel,
        out_shape=[jax.ShapeDtypeStruct(s, t) for s, t in zip(shapes, types)],
        in_specs=[anywhere] * 6,
        out_specs=[anywhere] * 6,
        scratch_shapes=[
            pltpu.SemaphoreType.DMA((94,)),
            pltpu.SemaphoreType.DMA((94,)),
            pltpu.SemaphoreType.DMA((10,)),
        ],
        compiler_params=pltpu.CompilerParams(collective_id=0, has_side_effects=True),
        name="gather_weights",
    )(small, tokens, w_qkv, w_out, w_up, w_down)


def exchange_kernel(source, result, send, recv, local):
    place = Place()
    enter([place.in_group(step)[0] for step in (1, 2, 3)])
    sems = Sems(send, recv)
    copies = []
    for step in (2, 1, 3):
        device, there = place.in_group(step)
        copies.append(sems.copy(source.at[there], result.at[place.stripe], device))
    for copy in copies:
        copy.start()
    kept = pltpu.make_async_copy(source.at[place.stripe], result.at[place.stripe], local)
    kept.start()
    for copy in copies:
        copy.wait()
    kept.wait()


def exchange(blocks, collective_id):
    anywhere = pl.BlockSpec(memory_space=pl.ANY)
    return pl.pallas_call(
        exchange_kernel,
        out_shape=jax.ShapeDtypeStruct(blocks.shape, blocks.dtype),
        in_specs=[anywhere],
        out_specs=anywhere,
        scratch_shapes=[
            pltpu.SemaphoreType.DMA((3,)),
            pltpu.SemaphoreType.DMA((3,)),
            pltpu.SemaphoreType.DMA,
        ],
        compiler_params=pltpu.CompilerParams(collective_id=collective_id, has_side_effects=True),
        name="exchange_rows",
    )(blocks)


CHUNKS = 6
STAGES = 8


def add_into(out, *terms, rows=64):
    height = out.shape[0]
    rows = min(rows, height)

    @pl.loop(0, height // rows)
    def _(step):
        at = pl.ds(pl.multiple_of(step * rows, rows), rows)
        total = terms[0][at, :].astype(f32)
        for term in terms[1:]:
            total = total + term[at, :].astype(f32)
        out[at, :] = total.astype(out.dtype)


class Reduce:
    def __init__(self, place, bufs, outs):
        self.place, self.bufs, self.outs = place, bufs, outs
        self.flight = {}

    def sems(self, k, base):
        send, recv = self.bufs["send"], self.bufs["recv"]
        sems = Sems(send.at[k % 2], recv.at[k % 2])
        sems.used = base
        return sems

    def go(self, key, copies):
        for copy in copies:
            copy.start()
        self.flight[key] = copies

    def land(self, key):
        for copy in self.flight.pop(key):
            copy.wait()

    def cols(self, axis):
        return pl.ds(axis * 384, 384)

    def step(self, stage, k):
        place, b, bufs = self.place, k % 2, self.bufs
        sib_core = 1 - place.core
        if stage == 0:
            sems = self.sems(k, 0)
            grads = bufs["grads"].at[k]
            own = [
                pltpu.make_async_copy(
                    grads.at[2 * h + place.core], bufs["part"].at[b, h], bufs["local"].at[b, h]
                )
                for h in range(2)
            ]
            for copy in own:
                copy.start()
            self.flight["own", k] = own
            self.go(
                (0, k),
                [
                    sems.copy(grads.at[2 * h + sib_core], bufs["side"].at[b, h], place.sibling())
                    for h in range(2)
                ],
            )
        elif stage == 1:
            self.land((0, k))
            self.land(("own", k))
            for h in range(2):
                part = bufs["part"].at[b, h]
                add_into(part, part, bufs["side"].at[b, h])
            sems = self.sems(k, 2)
            copies = []
            for step in (1, 3, 2):
                for axis in range(2):
                    device, there = place.ring(axis, step)
                    piece = bufs["part"].at[b, :, rows_at(there, 192, 192), self.cols(axis)]
                    copies.append(sems.copy(piece, bufs["ring"].at[b, axis, step - 1], device))
            self.go((1, k), copies)
        elif stage == 2:
            self.land((1, k))
            for axis in range(2):
                mine = rows_at(place.on_ring(axis), 192, 192)
                for h in range(2):
                    add_into(
                        bufs["sums"].at[b, h, axis],
                        bufs["part"].at[b, h, mine, self.cols(axis)],
                        *[bufs["ring"].at[b, axis, step, h] for step in range(3)],
                    )
            sems = self.sems(k, 8)
            self.go(
                (2, k),
                [sems.copy(bufs["sums"].at[b, 1 - place.yhi], bufs["cross"].at[b], place.mirror())],
            )
        elif stage == 3:
            self.land((2, k))
            sems = self.sems(k, 9)
            copies = []
            for axis in range(2):
                ours = bufs["ours"].at[b, axis]
                add_into(ours, bufs["sums"].at[b, place.yhi, axis], bufs["cross"].at[b, axis])
            for step in (1, 3, 2):
                for axis in range(2):
                    device, there = place.ring(1 - axis, step)
                    piece = bufs["ours"].at[b, axis, rows_at(there, 48, 48)]
                    copies.append(sems.copy(piece, bufs["ring2"].at[b, axis, step - 1], device))
            self.go((3, k), copies)
        elif stage == 4:
            self.land((3, k))
            for axis in range(2):
                mine = rows_at(place.on_ring(1 - axis), 48, 48)
                add_into(
                    bufs["small"].at[b, axis],
                    bufs["ours"].at[b, axis, mine],
                    *[bufs["ring2"].at[b, axis, step] for step in range(3)],
                    rows=48,
                )
            sems = self.sems(k, 15)
            self.go((4, k), [sems.copy(bufs["small"].at[b], bufs["twin"].at[b], place.twin())])
        elif stage == 5:
            self.land((4, k))
            sems = self.sems(k, 16)
            copies = []
            pieces = []
            for axis in range(2):
                start = place.on_ring(axis) * 192 + place.on_ring(1 - axis) * 48
                piece = bufs["final"].at[k, rows_at(start // 16, 48, 16), self.cols(axis)]
                add_into(piece, bufs["small"].at[b, axis], bufs["twin"].at[b, axis], rows=48)
                pieces.append(piece)
            for step in (1, 3, 2):
                for axis in range(2):
                    device, _ = place.ring(1 - axis, step)
                    copies.append(sems.copy(pieces[axis], pieces[axis], device))
            self.go((5, k), copies)
        elif stage == 6:
            self.land((5, k))
            sems = self.sems(k, 22)
            copies = []
            for step in (1, 3, 2):
                for axis in range(2):
                    device, _ = place.ring(axis, step)
                    mine = rows_at(place.on_ring(axis), 192, 192)
                    piece = bufs["final"].at[k, mine, self.cols(axis)]
                    copies.append(sems.copy(piece, piece, device))
            self.go((6, k), copies)
        else:
            self.land((6, k))
            copies = []
            layer, member = 1 - k // 3, k % 3
            out_qkv, out_out, out_up, out_down = self.outs
            for j in range(4):
                block = bufs["final"].at[k, pl.ds(j * 192, 192)]
                wide = pl.ds(j * 768, 768)
                if member == 0:
                    to = out_down.at[layer, pl.ds(j * 192, 192)]
                elif member == 1:
                    to = out_up.at[layer, :, wide]
                elif j < 3:
                    to = out_qkv.at[layer, :, wide]
                else:
                    to = out_out.at[layer]
                copies.append(pltpu.make_async_copy(block, to, bufs["store"].at[k, j]))
            self.go(("store", k), copies)


class ReduceSmall:
    def __init__(self, place, bufs, send, recv, out):
        self.place, self.bufs, self.out = place, bufs, out
        self.sems = Sems(send, recv)

    def go(self, copies):
        for copy in copies:
            copy.start()
        self.flight = copies

    def land(self):
        for copy in self.flight:
            copy.wait()

    def step(self, stage):
        place, bufs, sems = self.place, self.bufs, self.sems
        if stage == 0:
            copies = []
            for step in (1, 2, 3):
                device, there = place.in_group(step)
                copies.append(sems.copy(bufs["in"].at[there], bufs["land"].at[step - 1], device))
            self.go(copies)
        elif stage == 1:
            self.land()
            total = bufs["in"][place.stripe]
            for step in range(3):
                total = total + bufs["land"][step]
            mine = bufs["all"].at[place.ylo, place.x, place.z]
            mine[...] = total.astype(bf16)
            self.go([sems.copy(mine, mine, place.ring(0, step)[0]) for step in (1, 2, 3)])
        elif stage == 2:
            self.land()
            mine = bufs["all"].at[place.ylo, :, place.z]
            self.go([sems.copy(mine, mine, place.ring(1, step)[0]) for step in (1, 2, 3)])
        elif stage == 3:
            self.land()
            mine = bufs["all"].at[place.ylo]
            self.go([sems.copy(mine, mine, place.twin())])
        elif stage == 4:
            self.land()


REDUCE_SCRATCH = {
    "part": ((2, 2, 768, 768), bf16),
    "side": ((2, 2, 768, 768), bf16),
    "ring": ((2, 2, 3, 2, 192, 384), bf16),
    "sums": ((2, 2, 2, 192, 384), bf16),
    "cross": ((2, 2, 192, 384), bf16),
    "ours": ((2, 2, 192, 384), bf16),
    "ring2": ((2, 2, 3, 48, 384), bf16),
    "small": ((2, 2, 48, 384), bf16),
    "twin": ((2, 2, 48, 384), bf16),
    "final": ((CHUNKS, 768, 768), bf16),
}
REDUCE_SEMS = {"send": (2, 28), "recv": (2, 28), "local": (2, 2), "store": (CHUNKS, 4)}


def reduce_peers(place):
    peers = [place.sibling(), place.mirror(), place.twin()]
    peers += [place.ring(axis, step)[0] for axis in range(2) for step in (1, 2, 3)]
    peers += [(place.clip, lax.rem(place.stripe + 2, 4)), (place.clip, 3 - place.stripe)]
    return peers


def reduce_kernel(grads, small_in, out_qkv, out_out, out_up, out_down, small_out, *scratch):
    place = Place()
    names = list(REDUCE_SCRATCH) + list(REDUCE_SEMS)
    bufs = dict(zip(names, scratch))
    land, everything, small_send, small_recv = scratch[len(names) :]
    bufs["grads"] = grads
    enter(reduce_peers(place))
    reduce = Reduce(place, bufs, (out_qkv, out_out, out_up, out_down))
    small = ReduceSmall(
        place, {"in": small_in, "land": land, "all": small_out}, small_send, small_recv, small_out
    )
    for slot in range(CHUNKS + STAGES - 1):
        for stage in reversed(range(STAGES)):
            if 0 <= slot - stage < CHUNKS:
                reduce.step(stage, slot - stage)
        if slot < 5:
            small.step(slot)
    for k in range(CHUNKS):
        reduce.land(("store", k))


def reduce_all(grads, small):
    anywhere = pl.BlockSpec(memory_space=pl.ANY)
    vmem = pl.BlockSpec(memory_space=pltpu.VMEM)
    scratch = [pltpu.VMEM(*spec) for spec in REDUCE_SCRATCH.values()]
    scratch += [pltpu.SemaphoreType.DMA(shape) for shape in REDUCE_SEMS.values()]
    scratch += [
        pltpu.VMEM((3, 16, 384), f32),
        pltpu.VMEM((8, 128), f32),
        pltpu.SemaphoreType.DMA((10,)),
        pltpu.SemaphoreType.DMA((10,)),
    ]
    shapes = [(2, 192, 2304), (2, 192, 768), (2, 192, 3072), (2, 768, 768), (2, 4, 4, 16, 384)]
    return pl.pallas_call(
        reduce_kernel,
        out_shape=[jax.ShapeDtypeStruct(s, bf16) for s in shapes],
        in_specs=[anywhere, vmem],
        out_specs=[anywhere] * 4 + [vmem],
        scratch_shapes=scratch,
        compiler_params=pltpu.CompilerParams(
            collective_id=4, has_side_effects=True, vmem_limit_bytes=56 * 2**20
        ),
        name="reduce_gradients",
    )(grads, small)


def norm_rows(values):
    centred = values - jnp.mean(values, axis=-1, keepdims=True)
    spread = jnp.mean(centred * centred, axis=-1, keepdims=True)
    return centred * lax.rsqrt(spread + 1e-06)


def modulate(values, shift, scale):
    return norm_rows(values) * (1.0 + scale) + shift


def gelu_tanh(values):
    return (
        0.5
        * values
        * (1.0 + jnp.tanh(0.7978845608028654 * (values + 0.044715 * values * values * values)))
    )


def silu_plain(values):
    return values / (1.0 + jnp.exp(-values))


def sinusoid(steps, width):
    half = width // 2
    freqs = jnp.exp(-math.log(10000.0) * jnp.arange(half).astype(f32) / half)
    angles = steps.astype(f32)[:, None] * freqs[None, :]
    return jnp.concatenate([jnp.cos(angles), jnp.sin(angles)], axis=1)


def trans_dot(left, right):
    return lax.dot_general(left, right, (((0,), (0,)), ((), ())), preferred_element_type=f32)


def right_dot(left, right):
    return lax.dot_general(left, right, (((1,), (1,)), ((), ())), preferred_element_type=f32)


def forward_block(rows, mod, weights, spatial):
    w_qkv, w_out, w_up, b_up, w_down = weights
    shift1, scale1, gate1, shift2, scale2, gate2 = jnp.split(mod, 6)
    width = rows.shape[1]
    heads = width // HEAD
    frames = 1 if spatial else 4
    per_frame = rows.shape[0] // frames
    normed1 = modulate(rows, shift1, scale1).astype(bf16)
    qkv = jnp.dot(normed1, w_qkv, preferred_element_type=f32).astype(bf16)
    forms = spatial_forms if spatial else temporal_forms
    query, key, value = (
        qkv[:, i * width : (i + 1) * width].reshape(frames, per_frame, heads, HEAD)
        for i in range(3)
    )
    scale = HEAD ** (-0.5)
    scores = jnp.einsum(forms[0], query, key, preferred_element_type=f32) * scale
    top = jnp.max(scores, axis=-1, keepdims=True)
    total = jnp.sum(jnp.exp(scores - top), axis=-1, keepdims=True)
    log_total = top + jnp.log(total)
    probs = jnp.exp(scores - log_total).astype(bf16)
    attended = jnp.einsum(forms[1], probs, value, preferred_element_type=f32)
    attended = attended.reshape(rows.shape[0], width).astype(bf16)
    branch = jnp.dot(attended, w_out, preferred_element_type=f32)
    mid = rows + gate1 * branch
    normed2 = modulate(mid, shift2, scale2).astype(bf16)
    pre = jnp.dot(normed2, w_up, preferred_element_type=f32) + b_up
    hidden = gelu_tanh(pre).astype(bf16)
    mlp = jnp.dot(hidden, w_down, preferred_element_type=f32)
    saved = (
        rows, normed1, query, key, value, log_total, attended, branch, mid, normed2, pre, hidden,
        mlp
    )
    return (mid + gate2 * mlp, saved)


def backward_block(grad_out, mod, weights, saved, spatial):
    w_qkv, w_out, w_up, b_up, w_down = weights
    (
        rows, normed1, query, key, value, log_total, attended, branch, mid, normed2, pre, hidden,
        mlp
    ) = saved
    shift1, scale1, gate1, shift2, scale2, gate2 = jnp.split(mod, 6)
    width = rows.shape[1]
    forms = spatial_forms if spatial else temporal_forms
    grad_gate2 = jnp.sum(grad_out * mlp, axis=0)
    grad_mlp = (gate2 * grad_out).astype(bf16)
    grad_hidden = right_dot(grad_mlp, w_down)
    gelu_pull = jax.vjp(gelu_tanh, pre)[1]
    grad_pre = gelu_pull(grad_hidden)[0].astype(bf16)
    second_pull = jax.vjp(modulate, mid, shift2, scale2)[1]
    grad_mid, grad_shift2, grad_scale2 = second_pull(right_dot(grad_pre, w_up))
    grad_mid = grad_out + grad_mid
    grad_gate1 = jnp.sum(grad_mid * branch, axis=0)
    grad_branch = (gate1 * grad_mid).astype(bf16)
    grad_att = right_dot(grad_branch, w_out).astype(bf16).reshape(query.shape)
    scale = HEAD ** (-0.5)
    scores = jnp.einsum(forms[0], query, key, preferred_element_type=f32) * scale
    soft = jnp.exp(scores - log_total)
    grad_probs = jnp.einsum(forms[0], grad_att, value, preferred_element_type=f32)
    centre = jnp.sum(soft * grad_probs, axis=-1, keepdims=True)
    grad_scores = (soft * (grad_probs - centre) * scale).astype(bf16)
    grad_query = jnp.einsum(forms[1], grad_scores, key, preferred_element_type=f32)
    probs = soft.astype(bf16)
    grad_key = jnp.einsum(forms[2], grad_scores, query, preferred_element_type=f32)
    grad_value = jnp.einsum(forms[2], probs, grad_att, preferred_element_type=f32)
    grad_qkv = jnp.concatenate(
        [g.reshape(-1, width) for g in (grad_query, grad_key, grad_value)], axis=1
    ).astype(bf16)
    first_pull = jax.vjp(modulate, rows, shift1, scale1)[1]
    grad_rows, grad_shift1, grad_scale1 = first_pull(right_dot(grad_qkv, w_qkv))
    grad_rows = grad_mid + grad_rows
    grad_mod = jnp.concatenate(
        [grad_shift1, grad_scale1, grad_gate1, grad_shift2, grad_scale2, grad_gate2]
    )

    def wide(grad):
        blocks = grad.shape[1] // 768
        return grad.astype(bf16).reshape(4, 192, blocks, 768).transpose(0, 2, 1, 3).reshape(
            4, 192 * blocks, 768
        )

    chunks = [
        trans_dot(hidden, grad_mlp).astype(bf16).reshape(4, 768, 768),
        wide(trans_dot(normed2, grad_pre)),
        jnp.concatenate(
            [
                wide(trans_dot(normed1, grad_qkv)),
                wide(trans_dot(attended, grad_branch)),
            ],
            axis=1,
        ),
    ]
    grad_b_up = jnp.sum(grad_pre.astype(f32), axis=0)
    return (grad_rows, grad_mod, grad_b_up, chunks)


def shards(
    clip_tokens, timesteps, loss_weight, cotangent, w_mod, b_mod, w_qkv, w_out, w_up, b_up, w_down
):
    width = clip_tokens.shape[3]
    embed = silu_plain(sinusoid(timesteps, width)).astype(bf16)
    mod_part = jnp.einsum("d,ldm->lm", embed[0], w_mod, preferred_element_type=f32) + b_mod.astype(
        f32
    )
    small = jnp.concatenate([b_up.astype(f32).reshape(4, 384), mod_part.reshape(6, 384)])
    small = jnp.pad(small, ((0, 6), (0, 0)))
    all_small, frame, *full = gather(small, clip_tokens[0], w_qkv, w_out, w_up, w_down)
    b_ups = all_small[:, 0:4].reshape(4, 2, 768).transpose(1, 0, 2).reshape(2, 3072)
    mods = all_small[:, 4:10].reshape(4, 2, 1152).transpose(1, 0, 2).reshape(2, 4608)
    weights = [
        (
            full[0][layer].reshape(768, 2304),
            full[1][layer].reshape(768, 768),
            full[2][layer].reshape(768, 3072),
            b_ups[layer],
            full[3][layer].reshape(3072, 768),
        )
        for layer in range(2)
    ]
    rows, saved0 = forward_block(frame.reshape(256, width).astype(f32), mods[0], weights[0], True)
    rows = exchange(rows.astype(bf16).reshape(4, 64, width), 1).reshape(256, width).astype(f32)
    rows, saved1 = forward_block(rows, mods[1], weights[1], False)
    block_output = rows.astype(bf16).reshape(clip_tokens.shape)
    grad = cotangent.reshape(-1, width).astype(f32) * loss_weight[0]
    grad, mod1, b_up1, chunks1 = backward_block(grad, mods[1], weights[1], saved1, False)
    grad = exchange(grad.astype(bf16).reshape(4, 64, width), 2).reshape(256, width).astype(f32)
    grad, mod0, b_up0, chunks0 = backward_block(grad, mods[0], weights[0], saved0, True)
    grad = exchange(grad.astype(bf16).reshape(4, 64, width), 3)
    grad_input = grad.astype(f32).reshape(clip_tokens.shape)

    b_part = jnp.stack([b_up0, b_up1]).reshape(2, 4, 768).transpose(1, 0, 2).reshape(4, 4, 384)
    m_part = jnp.stack([mod0, mod1]).reshape(2, 4, 1152).transpose(1, 0, 2).reshape(4, 6, 384)
    e_part = jnp.broadcast_to(0.25 * embed.astype(f32).reshape(1, 2, 384), (4, 2, 384))
    small = jnp.concatenate([b_part, m_part, e_part, jnp.zeros((4, 4, 384), f32)], axis=1)
    *sums, everyone = reduce_all(jnp.stack(chunks1 + chunks0), small)
    everyone = everyone.reshape(32, 16, 384)
    b_all = everyone[:, 0:4].astype(f32).sum(0).reshape(2, 768)
    m_all = everyone[:, 4:10].reshape(32, 2, 1152)
    e_all = everyone[:, 10:12].reshape(32, 768)
    grad_w_mod = jnp.einsum("cd,clm->ldm", e_all, m_all, preferred_element_type=f32)
    return (
        block_output,
        grad_input,
        grad_w_mod,
        m_all.astype(f32).sum(0),
        sums[0].astype(f32),
        sums[1].astype(f32),
        sums[2].astype(f32),
        b_all,
        sums[3].astype(f32),
    )


def solution(mesh):
    placed = (
        P("clip", None, "stripe", None),
        P("clip"),
        P("clip"),
        P("clip", None, "stripe", None),
        P(None, None, "stripe"),
        P(None, "stripe"),
        P(None, "stripe", None),
        P(None, "stripe", None),
        P(None, "stripe", None),
        P(None, "stripe"),
        P(None, "stripe", None),
    )
    return jax.shard_map(
        shards,
        mesh=mesh,
        in_specs=placed,
        out_specs=(
            P("clip", None, "stripe", None),
            P("clip", None, "stripe", None),
            P(None, None, "stripe"),
            P(None, "stripe"),
            P(None, "stripe", None),
            P(None, "stripe", None),
            P(None, "stripe", None),
            P(None, "stripe"),
            P(None, "stripe", None),
        ),
        check_vma=False,
    )
```

```python
import math
from types import SimpleNamespace
from typing import Any, NamedTuple

import jax
import jax.numpy as jnp
from jax import lax
from jax.experimental import pallas as pl
from jax.experimental.pallas import tpu as pltpu
from jax.sharding import PartitionSpec as P

HEAD = 64
MESH = pl.DeviceIdType.MESH
bf16 = jnp.bfloat16
f32 = jnp.float32
WIDTH = 768
ROWS = 256


class Place:
    def __init__(self):
        clip, stripe = lax.axis_index("clip"), lax.axis_index("stripe")
        self.clip, self.stripe = clip, stripe
        self.ylo = lax.div(clip, 16)
        self.x = lax.rem(lax.div(clip, 4), 4)
        self.z = lax.rem(clip, 4)
        self.yhi = lax.div(stripe, 2)
        self.core = lax.rem(stripe, 2)

    def at_x(self, x):
        return (self.ylo * 16 + x * 4 + self.z, self.stripe)

    def at_z(self, z):
        return (self.ylo * 16 + self.x * 4 + z, self.stripe)

    def ring(self, axis, step):
        there = lax.rem((self.x if axis == 0 else self.z) + step, 4)
        return (self.at_x(there) if axis == 0 else self.at_z(there)), there

    def on_ring(self, axis):
        return self.x if axis == 0 else self.z

    def sibling(self):
        return (self.clip, self.yhi * 2 + 1 - self.core)

    def mirror(self):
        return ((1 - self.ylo) * 16 + self.x * 4 + self.z, (1 - self.yhi) * 2 + self.core)

    def twin(self):
        return ((1 - self.ylo) * 16 + self.x * 4 + self.z, self.stripe)

    def in_group(self, step):
        there = lax.rem(self.stripe + step, 4)
        return (self.clip, there), there


def enter(devices):
    barrier = pltpu.get_barrier_semaphore()
    for device in devices:
        pl.semaphore_signal(barrier, inc=1, device_id=device, device_id_type=MESH)
    pl.semaphore_wait(barrier, len(devices))


class Sems:
    def __init__(self, send, recv):
        self.send, self.recv, self.used = send, recv, 0

    def copy(self, src, dst, device):
        at = self.used
        self.used += 1
        return pltpu.make_async_remote_copy(
            src_ref=src,
            dst_ref=dst,
            send_sem=self.send.at[at],
            recv_sem=self.recv.at[at],
            device_id=device,
            device_id_type=MESH,
        )


def rows_at(start, size, grain):
    return pl.ds(pl.multiple_of(start * grain, grain), size)


class Buf:
    def __init__(self, shape, dtype, space=pltpu.VMEM, array=None):
        self.shape, self.dtype, self.space, self.array = shape, dtype, space, array


def given(array, space=pltpu.VMEM):
    return Buf(array.shape, array.dtype, space, array)


def dma(*shape):
    return pltpu.SemaphoreType.DMA(shape)


def call_kernel(body, collective_id, ins, outs, scratch):
    leaves, trees = zip(*(jax.tree.flatten(part) for part in (ins, outs, scratch)))
    ends = [len(leaves[0]), len(leaves[0]) + len(leaves[1])]

    def kernel(*refs):
        parts = (refs[: ends[0]], refs[ends[0] : ends[1]], refs[ends[1] :])
        groups = [jax.tree.unflatten(tree, part) for tree, part in zip(trees, parts)]
        body(SimpleNamespace(**groups[0], **groups[1], **groups[2]))

    results = pl.pallas_call(
        kernel,
        out_shape=[jax.ShapeDtypeStruct(b.shape, b.dtype) for b in leaves[1]],
        in_specs=[pl.BlockSpec(memory_space=b.space) for b in leaves[0]],
        out_specs=[pl.BlockSpec(memory_space=b.space) for b in leaves[1]],
        scratch_shapes=[
            pltpu.VMEM(b.shape, b.dtype) if isinstance(b, Buf) else b for b in leaves[2]
        ],
        compiler_params=pltpu.CompilerParams(
            collective_id=collective_id,
            has_side_effects=collective_id is not None,
            vmem_limit_bytes=62 * 2**20,
        ),
        name=body.__name__,
    )(*[b.array for b in leaves[0]])
    return SimpleNamespace(**jax.tree.unflatten(trees[1], results))


CHUNKS = 6
STAGES = 10
SIDE = 384


def add_into(out, *terms, rows=64):
    height = out.shape[0]
    rows = math.gcd(rows, height)

    @pl.loop(0, height // rows)
    def _(step):
        at = pl.ds(pl.multiple_of(step * rows, rows), rows)
        total = terms[0][at, :].astype(f32)
        for term in terms[1:]:
            total = total + term[at, :].astype(f32)
        out[at, :] = total.astype(out.dtype)


class Reduce:
    def __init__(self, place, bufs, outs):
        self.place, self.bufs, self.outs = place, bufs, outs
        self.flight = {}

    def go(self, key, *plans):
        k, stage = key
        sems = Sems(self.bufs.send.at[k % 2], self.bufs.recv.at[k % 2])
        sems.used = (0, 2, 6, 10, 11, 17, 18, 24, 28)[stage]
        copies = [sems.copy(*plan) for plan in plans]
        for copy in copies:
            copy.start()
        self.flight[key] = copies

    def land(self, *key):
        for copy in self.flight.pop(key):
            copy.wait()

    def cols(self, axis):
        return pl.ds(axis * SIDE, SIDE)

    def own(self, k, axis, step, half=None):
        there = self.place.ring(axis, step)[1] * 192
        size = 192
        if half is not None:
            there, size = there + 96 * half, 96
        rows = rows_at(there // 32, size, 32)
        return self.bufs.grads.at[k % 2, :, self.place.core, rows, self.cols(axis)]

    def step(self, stage, k):
        place, b, bufs = self.place, k % 2, self.bufs
        here = k, stage
        if stage > 0:
            self.land(k, stage - 1)
        if stage == 0:
            other = 1 - place.core
            self.go(
                here,
                *[
                    (bufs.grads.at[b, h, other], bufs.side.at[b, h], place.sibling())
                    for h in range(2)
                ],
            )
        elif stage == 1:
            for h in range(2):
                part = bufs.grads.at[b, h, place.core]
                add_into(part, part, bufs.side.at[b, h])
            self.go(
                here,
                *[
                    (
                        self.own(k, axis, 2, way),
                        bufs.relay.at[b, axis, way],
                        place.ring(axis, 1 + 2 * way)[0],
                    )
                    for axis in range(2)
                    for way in range(2)
                ],
            )
        elif stage == 2:
            plans = []
            for axis in range(2):
                for way in range(2):
                    for h in range(2):
                        half = self.own(k, axis, 1 + 2 * way, way).at[h]
                        add_into(half, half, bufs.relay.at[b, axis, way, h], rows=96)
                    device, _ = place.ring(axis, 1 + 2 * way)
                    piece = self.own(k, axis, 1 + 2 * way)
                    plans.append((piece, bufs.ring.at[b, axis, way], device))
            self.go(here, *plans)
        elif stage == 3:
            for axis in range(2):
                for h in range(2):
                    add_into(
                        bufs.sums.at[b, h, axis],
                        self.own(k, axis, 0).at[h],
                        *[bufs.ring.at[b, axis, way, h] for way in range(2)],
                    )
            self.go(
                here, (bufs.sums.at[b, 1 - place.yhi], bufs.cross.at[b], place.mirror())
            )
        elif stage == 4:
            for axis in range(2):
                ours = bufs.ours.at[b, axis]
                add_into(ours, bufs.sums.at[b, place.yhi, axis], bufs.cross.at[b, axis])
            plans = []
            for step in (1, 3, 2):
                for axis in range(2):
                    device, there = place.ring(1 - axis, step)
                    piece = bufs.ours.at[b, axis, rows_at(there, 48, 48)]
                    plans.append((piece, bufs.ring2.at[b, axis, step - 1], device))
            self.go(here, *plans)
        elif stage == 5:
            for axis in range(2):
                mine = rows_at(place.on_ring(1 - axis), 48, 48)
                add_into(
                    bufs.small.at[b, axis],
                    bufs.ours.at[b, axis, mine],
                    *[bufs.ring2.at[b, axis, step] for step in range(3)],
                    rows=48,
                )
            self.go(here, (bufs.small.at[b], bufs.twin.at[b], place.twin()))
        elif stage == 6:
            plans = []
            for axis in range(2):
                start = place.on_ring(axis) * 12 + place.on_ring(1 - axis) * 3
                piece = bufs.final.at[k, rows_at(start, 48, 16), self.cols(axis)]
                add_into(piece, bufs.small.at[b, axis], bufs.twin.at[b, axis], rows=48)
                for step in (1, 3, 2):
                    plans.append((piece, piece, place.ring(1 - axis, step)[0]))
            self.go(here, *plans)
        elif stage == 7:
            plans = []
            for axis in range(2):
                mine = rows_at(place.on_ring(axis), 192, 192)
                piece = bufs.final.at[k, mine, self.cols(axis)]
                for step in (1, 3):
                    plans.append((piece, piece, place.ring(axis, step)[0]))
            self.go(here, *plans)
        elif stage == 8:
            plans = []
            for axis in range(2):
                for way in range(2):
                    came = place.ring(axis, 3 - 2 * way)[1]
                    rows = rows_at(came * 2 + way, 96, 96)
                    piece = bufs.final.at[k, rows, self.cols(axis)]
                    plans.append((piece, piece, place.ring(axis, 1 + 2 * way)[0]))
            self.go(here, *plans)
        else:
            copies = []
            layer, member = 1 - k // 3, k % 3
            for j in range(4):
                block = bufs.final.at[k, pl.ds(j * 192, 192)]
                wide = pl.ds(j * 768, 768)
                if member == 0:
                    to = self.outs.down.at[layer, pl.ds(j * 192, 192)]
                elif member == 1:
                    to = self.outs.up.at[layer, :, wide]
                elif j < 3:
                    to = self.outs.qkv.at[layer, :, wide]
                else:
                    to = self.outs.out.at[layer]
                copies.append(pltpu.make_async_copy(block, to, bufs.store.at[k, j]))
            for copy in copies:
                copy.start()
            self.flight[here] = copies


class ReduceSmall:
    def __init__(self, place, bufs):
        self.place, self.bufs = place, bufs
        self.sems = Sems(bufs.little_send, bufs.little_recv)

    def go(self, copies):
        for copy in copies:
            copy.start()
        self.flight = copies

    def land(self):
        for copy in self.flight:
            copy.wait()

    def step(self, stage):
        place, bufs, sems = self.place, self.bufs, self.sems
        if stage == 0:
            copies = []
            for step in (1, 2, 3):
                device, there = place.in_group(step)
                copies.append(sems.copy(bufs.pack.at[there], bufs.pack_land.at[step - 1], device))
            self.go(copies)
        elif stage == 1:
            self.land()
            total = bufs.pack[place.stripe]
            for step in range(3):
                total = total + bufs.pack_land[step]
            mine = bufs.everyone.at[place.ylo, place.x, place.z]
            mine[...] = total.astype(bf16)
            self.go([sems.copy(mine, mine, place.ring(0, step)[0]) for step in (1, 2, 3)])
        elif stage == 2:
            self.land()
            mine = bufs.everyone.at[place.ylo, :, place.z]
            self.go([sems.copy(mine, mine, place.ring(1, step)[0]) for step in (1, 2, 3)])
        elif stage == 3:
            self.land()
            mine = bufs.everyone.at[place.ylo]
            self.go([sems.copy(mine, mine, place.twin())])
        elif stage == 4:
            self.land()


class Gather:
    STEPS = ("begin", "spread", "relay", "share", "end")

    def __init__(self, place, sems, own, full, local_sem):
        self.place, self.sems, self.own, self.full = place, sems, own, full
        rows, columns = own.shape
        self.quarter, self.half = rows // 4, columns // 2
        self.other = (1 - place.yhi) * 2 + place.core
        self.kept = pltpu.make_async_copy(own, full.at[place.stripe], local_sem)

    def parts(self):
        for axis in range(2):
            mine = rows_at(self.place.on_ring(axis), self.quarter, self.quarter)
            yield axis, mine, pl.ds(axis * self.half, self.half)

    def go(self, plans):
        copies = [self.sems.copy(*plan) for plan in plans]
        for copy in copies:
            copy.start()
        return copies

    def begin(self):
        place = self.place
        plans = []
        for _, mine, cols in self.parts():
            there = self.full.at[place.stripe, mine, cols]
            plans.append((self.own.at[mine, cols], there, place.mirror()))
        plans.append((self.own, self.full.at[place.stripe], place.sibling()))
        *self.first, self.side = self.go(plans)
        self.kept.start()

    def spread(self):
        plans = []
        for axis, mine, cols in self.parts():
            self.first[axis].wait()
            piece = self.full.at[self.other, mine, cols]
            plans += [(piece, piece, self.place.ring(axis, step)[0]) for step in (1, 3)]
        self.rings = self.go(plans)

    def relay(self):
        for copy in self.rings:
            copy.wait()
        plans = []
        cut = -(-self.half // 256) * 128
        for axis, _, _ in self.parts():
            for way in range(2):
                came = self.place.ring(axis, 3 - 2 * way)[1]
                start, size = (0, cut) if way == 0 else (cut, self.half - cut)
                piece = self.full.at[
                    self.other,
                    rows_at(came, self.quarter, self.quarter),
                    pl.ds(axis * self.half + start, size),
                ]
                plans.append((piece, piece, self.place.ring(axis, 1 + 2 * way)[0]))
        self.relays = self.go(plans)

    def share(self):
        for copy in self.relays:
            copy.wait()
        piece = self.full.at[self.other]
        self.last = self.go([(piece, piece, self.place.sibling())])

    def end(self):
        self.kept.wait()
        self.side.wait()
        for copy in self.last:
            copy.wait()


def trans_dot(left, right):
    return lax.dot_general(left, right, (((0,), (0,)), ((), ())), preferred_element_type=f32)


def right_dot(left, right):
    return lax.dot_general(left, right, (((1,), (1,)), ((), ())), preferred_element_type=f32)


def dot(left, right):
    return jnp.dot(left, right, preferred_element_type=f32)


def norm_rows(values):
    centred = values - jnp.mean(values, axis=-1, keepdims=True)
    spread = jnp.mean(centred * centred, axis=-1, keepdims=True)
    rate = lax.rsqrt(spread + 1e-06)
    return centred * rate, rate


def norm_pull(grad, normed, rate):
    along = jnp.mean(grad * normed, axis=-1, keepdims=True)
    return rate * (grad - jnp.mean(grad, axis=-1, keepdims=True) - normed * along)


def over_rows(values):
    return jnp.sum(values, axis=0, keepdims=True)


def gelu_and_slope(v):
    square = v * v
    t = jnp.tanh(0.7978845608028654 * (v + 0.044715 * (square * v)))
    half = 0.5 * (1.0 + t)
    inner = 0.7978845608028654 * (1.0 + 0.134145 * square)
    return v * half, half + 0.5 * v * (1.0 - t * t) * inner


class Small:
    def __init__(self, ref):
        self.ref = ref

    def spot(self, layer, member, half):
        unit = 2 * member + half
        return unit // 3, 4 + 3 * layer + unit % 3

    def mod(self, layer, member):
        spots = [self.spot(layer, member, half) for half in range(2)]
        return jnp.concatenate([self.ref[s, r : r + 1, :] for s, r in spots], axis=1)

    def put_mod(self, layer, member, value):
        for half in range(2):
            s, r = self.spot(layer, member, half)
            self.ref[s, r : r + 1, :] = value[:, half * 384 : (half + 1) * 384]

    def bias(self, layer, s):
        return jnp.concatenate(
            [self.ref[s, 2 * layer + half : 2 * layer + half + 1, :] for half in range(2)], axis=1
        )

    def put_bias(self, layer, s, value):
        for half in range(2):
            r = 2 * layer + half
            self.ref[s, r : r + 1, :] = value[:, half * 384 : (half + 1) * 384]


def frame_major():
    for group in range(2):
        for frame in range(4):
            start = group * 128 + frame * 32
            yield slice(start, start + 32), frame, slice(group * 32, group * 32 + 32)


def head_mask(half):
    lane = lax.broadcasted_iota(jnp.int32, (1, 128), 1)
    return (lane >= 64 * half) & (lane < 64 * half + 64)


def same_patch():
    row = lax.broadcasted_iota(jnp.int32, (128, 128), 0)
    col = lax.broadcasted_iota(jnp.int32, (128, 128), 1)
    return lax.rem(row, 32) == lax.rem(col, 32)


def attend(qkv, attended, probs, spatial):
    size = ROWS if spatial else 128

    @pl.loop(0, 6)
    def _(pair):
        def cols(member):
            return pl.ds(pl.multiple_of(member * WIDTH + pair * 128, 128), 128)

        for group in range(ROWS // size):
            here = slice(group * size, (group + 1) * size)
            query, key, value = (qkv[here, cols(member)] for member in range(3))
            query = query * jnp.asarray(HEAD**-0.5, bf16)
            outs = []
            for half in range(2):
                picked = jnp.where(head_mask(half), query, jnp.zeros_like(query))
                scores = right_dot(picked, key)
                if not spatial:
                    scores = jnp.where(same_patch(), scores, -1e30)
                expo = jnp.exp(scores - jnp.max(scores, axis=-1, keepdims=True))
                weight = (expo * (1.0 / jnp.sum(expo, axis=-1, keepdims=True))).astype(bf16)
                probs[pair * 2 + half, here, 0:size] = weight
                outs.append(dot(weight, value))
            attended[here, cols(0)] = jnp.where(head_mask(0), outs[0], outs[1]).astype(bf16)


def attend_back(qkv, probs, grad_att, grad_qkv, spatial):
    size = ROWS if spatial else 128
    scale = HEAD**-0.5

    @pl.loop(0, 6)
    def _(pair):
        def cols(member):
            return pl.ds(pl.multiple_of(member * WIDTH + pair * 128, 128), 128)

        for group in range(ROWS // size):
            here = slice(group * size, (group + 1) * size)
            query, key, value = (qkv[here, cols(member)] for member in range(3))
            grad = grad_att[here, cols(0)]
            found = []
            for half in range(2):
                picked = jnp.where(head_mask(half), grad, jnp.zeros_like(grad))
                weight = probs[pair * 2 + half, here, 0:size]
                wide = weight.astype(f32)
                pull = wide * right_dot(picked, value)
                centre = jnp.sum(pull, axis=-1, keepdims=True)
                grad_scores = ((pull - wide * centre) * scale).astype(bf16)
                found.append(
                    (
                        dot(grad_scores, key),
                        trans_dot(grad_scores, query),
                        trans_dot(weight, grad),
                    )
                )
            for member in range(3):
                both = jnp.where(head_mask(0), found[0][member], found[1][member])
                grad_qkv[here, cols(member)] = both.astype(bf16)


class Weights(NamedTuple):
    qkv: Any
    out: Any
    up: Any
    down: Any


class Saved(NamedTuple):
    normed1: Any
    unit1: Any
    rate1: Any
    qkv: Any
    probs: Any
    attended: Any
    branch: Any
    unit2: Any
    rate2: Any
    normed2: Any
    slope: Any
    hidden: Any
    mlp: Any


FULL = Weights((4, 192, 2304), (4, 192, 768), (4, 192, 3072), (4, 768, 768))
SAVED = Saved(
    normed1=Buf((ROWS, WIDTH), bf16),
    unit1=Buf((ROWS, WIDTH), bf16),
    rate1=Buf((ROWS, 128), f32),
    qkv=Buf((ROWS, 3 * WIDTH), bf16),
    probs=Buf((12, ROWS, ROWS), bf16),
    attended=Buf((ROWS, WIDTH), bf16),
    branch=Buf((ROWS, WIDTH), bf16),
    unit2=Buf((ROWS, WIDTH), bf16),
    rate2=Buf((ROWS, 128), f32),
    normed2=Buf((ROWS, WIDTH), bf16),
    slope=Buf((ROWS, 4 * WIDTH), bf16),
    hidden=Buf((ROWS, 4 * WIDTH), bf16),
    mlp=Buf((ROWS, WIDTH), bf16),
)


class Keep:
    def __init__(self, near, far, layer, sem, inward):
        copies = []
        for at, (a, b) in enumerate(zip(near, far)):
            a, b = (b.at[layer], a) if inward else (a, b.at[layer])
            copies.append(pltpu.make_async_copy(a, b, sem.at[at]))
        self.copies = Saved(*copies)

    def start(self, pick):
        for copy in pick(self.copies):
            copy.start()

    def wait(self, pick):
        for copy in pick(self.copies):
            copy.wait()


def spread_lanes(value):
    return jnp.broadcast_to(value, (ROWS, 128))


def whole(ref, cols=slice(None)):
    value = ref[:, :, cols]
    return value.reshape(value.shape[0] * value.shape[1], value.shape[2])


def forward_block(layer, rows, mid, near, keep, small, weights, pump):
    unit, rate = norm_rows(rows[...])
    near.unit1[...] = unit.astype(bf16)
    near.rate1[...] = spread_lanes(rate)
    shift, scale = small.mod(layer, 0), small.mod(layer, 1)
    near.normed1[...] = (unit * (1.0 + scale) + shift).astype(bf16)
    keep.start(lambda k: (k.unit1, k.rate1, k.normed1))
    pump(0)
    for j in range(3):
        cols = slice(j * WIDTH, (j + 1) * WIDTH)
        near.qkv[:, cols] = dot(near.normed1[...], whole(weights.qkv, cols)).astype(bf16)
    keep.start(lambda k: (k.qkv,))
    pump(1)
    attend(near.qkv, near.attended, near.probs, layer == 0)
    keep.start(lambda k: (k.probs, k.attended))
    pump(2)
    branch = dot(near.attended[...], whole(weights.out))
    near.branch[...] = branch.astype(bf16)
    mid[...] = rows[...] + small.mod(layer, 2) * branch
    pump(3)
    unit, rate = norm_rows(mid[...])
    near.unit2[...] = unit.astype(bf16)
    near.rate2[...] = spread_lanes(rate)
    shift, scale = small.mod(layer, 3), small.mod(layer, 4)
    near.normed2[...] = (unit * (1.0 + scale) + shift).astype(bf16)
    keep.start(lambda k: (k.branch, k.unit2, k.rate2, k.normed2))
    pump(4)
    for j in range(4):
        if j == 2:
            pump(5)
        cols = slice(j * WIDTH, (j + 1) * WIDTH)
        pre = dot(near.normed2[...], whole(weights.up, cols)) + small.bias(layer, j)
        hidden, slope = gelu_and_slope(pre)
        near.hidden[:, cols] = hidden.astype(bf16)
        near.slope[:, cols] = slope.astype(bf16)
    keep.start(lambda k: (k.hidden, k.slope))
    pump(6)
    mlp = dot(near.hidden[...], whole(weights.down))
    near.mlp[...] = mlp.astype(bf16)
    keep.start(lambda k: (k.mlp,))
    rows[...] = mid[...] + small.mod(layer, 5) * mlp


def group_peers(place):
    return [place.in_group(step)[0] for step in (1, 2, 3)]


def ring_peers(place):
    return [place.ring(axis, step)[0] for axis in range(2) for step in (1, 2, 3)]


class Swap:
    def __init__(self, place, sems, source, result, local_sem):
        self.copies = []
        for step in (2, 1, 3):
            device, there = place.in_group(step)
            self.copies.append(sems.copy(source.at[there], result.at[place.stripe], device))
        mine = place.stripe
        self.copies.append(pltpu.make_async_copy(source.at[mine], result.at[mine], local_sem))

    def start(self):
        for copy in self.copies:
            copy.start()

    def wait(self):
        for copy in self.copies:
            copy.wait()


def forward_blocks(refs):
    place = Place()
    enter(group_peers(place) + [place.mirror()] + ring_peers(place))
    sems = Sems(refs.send, refs.recv)
    local = refs.local
    greet = []
    for step in (1, 2, 3):
        device, _ = place.in_group(step)
        greet.append(sems.copy(refs.small, refs.small_all.at[place.stripe], device))
    mine = refs.small_all.at[place.stripe]
    greet.append(pltpu.make_async_copy(refs.small, mine, local.at[0]))
    for copy in greet:
        copy.start()
    swap = Swap(place, sems, refs.tokens, refs.frame, local.at[1])
    swap.start()

    g, outward = [], []
    for layer in range(2):
        for own, full, far in zip(refs.shards, refs.full, refs.far):
            at = len(g)
            g.append(Gather(place, sems, own.at[layer], full.at[layer], local.at[2 + at]))
            outward.append(
                pltpu.make_async_copy(full.at[layer], far.at[layer], local.at[10 + at])
            )
    for one in g:
        one.begin()

    def end(at):
        g[at].end()
        outward[at].start()

    def pump(layer, part):
        if (layer, part) == (0, 0):
            g[0].spread(), g[1].spread(), g[0].relay(), g[1].relay(), g[0].share()
            end(0)
        elif (layer, part) == (0, 1):
            g[2].spread(), g[1].share()
        elif (layer, part) == (0, 2):
            g[2].relay(), g[3].spread()
            end(1)
        elif (layer, part) == (0, 3):
            g[2].share()
        elif (layer, part) == (0, 4):
            g[4].spread(), g[3].relay()
            end(2)
        elif (layer, part) == (0, 5):
            g[5].spread(), g[4].relay(), g[3].share()
        elif (layer, part) == (0, 6):
            g[6].spread(), g[5].relay(), g[4].share()
            end(3)
        elif (layer, part) == (0, 7):
            g[7].spread(), g[6].relay(), g[5].share()
        elif (layer, part) == (1, 0):
            g[6].share()
            end(4)
        elif (layer, part) == (1, 1):
            g[7].relay()
            end(5)
        elif (layer, part) == (1, 2):
            g[7].share()
        elif (layer, part) == (1, 4):
            end(6)
        elif (layer, part) == (1, 6):
            end(7)

    for copy in greet:
        copy.wait()
    swap.wait()
    small = Small(refs.small_all)
    rows = refs.rows
    for j in range(4):
        rows[j * 64 : (j + 1) * 64, :] = refs.frame[j].astype(f32)
    keeps = []
    for layer in range(2):
        keep = Keep(refs.near[layer], refs.saved, layer, refs.keep.at[layer], False)
        keeps.append(keep)
        weights = Weights(*[full.at[layer] for full in refs.full])

        def at_part(part, layer=layer):
            pump(layer, part)

        forward_block(layer, rows, refs.mid, refs.near[layer], keep, small, weights, at_part)
        if layer == 0:
            for j in range(4):
                refs.turn[j] = rows[j * 64 : (j + 1) * 64, :].astype(bf16)
            swap = Swap(place, sems, refs.turn, refs.turned, local.at[18])
            swap.start()
            pump(0, 7)
            swap.wait()
            for here, f, patches in frame_major():
                rows[here, :] = refs.turned[f, patches, :].astype(f32)
    for here, f, patches in frame_major():
        refs.block_output[f, patches, :] = rows[here, :].astype(bf16)
    for copy in outward:
        copy.wait()
    for keep in keeps:
        keep.wait(lambda k: k)


def run_forward(small, tokens, shards):
    ins = dict(
        small=given(small),
        tokens=given(tokens),
        shards=Weights(*[given(w, pl.ANY) for w in shards]),
    )
    outs = dict(
        small_all=Buf((4, 16, 384), f32),
        block_output=Buf(tokens.shape, bf16),
        far=Weights(*[Buf((2, *shape), bf16, pl.ANY) for shape in FULL]),
        saved=Saved(*[Buf((2, *b.shape), b.dtype, pl.ANY) for b in SAVED]),
    )
    scratch = dict(
        full=Weights(*[Buf((2, *shape), bf16) for shape in FULL]),
        near=(SAVED, SAVED),
        rows=Buf((ROWS, WIDTH), f32),
        mid=Buf((ROWS, WIDTH), f32),
        frame=Buf(tokens.shape, bf16),
        turn=Buf(tokens.shape, bf16),
        turned=Buf(tokens.shape, bf16),
        send=dma(110),
        recv=dma(110),
        local=dma(20),
        keep=dma(2, len(SAVED)),
    )
    return call_kernel(forward_blocks, 0, ins, outs, scratch)


def backward_block(layer, grad, refs, small, pack, weights, at):
    near, grads, work, gpre, back, gqkv = (
        refs.near, refs.grads, refs.work, refs.gpre, refs.back, refs.gqkv
    )
    at.have(lambda k: (k.mlp, k.hidden))
    pack.put_mod(layer, 5, over_rows(grad[...] * near.mlp[...].astype(f32)))
    work[...] = (small.mod(layer, 5) * grad[...]).astype(bf16)
    b = at.before()
    for s in range(4):
        cols = slice(s * WIDTH, (s + 1) * WIDTH)
        grads[b, s // 2, s % 2] = trans_dot(near.hidden[:, cols], work[...]).astype(bf16)
    at.after()
    at.have(lambda k: (k.slope,), lambda w: (w.down,))
    for j in range(4):
        cols = slice(j * WIDTH, (j + 1) * WIDTH)
        pre = (right_dot(work[...], weights.down[j]) * near.slope[:, cols].astype(f32)).astype(bf16)
        gpre[:, cols] = pre
        pack.put_bias(layer, j, over_rows(pre.astype(f32)))
    at.done(lambda k: (k.mlp, k.hidden, k.slope), lambda w: (w.down,))
    at.middle()
    at.have(lambda k: (k.unit2, k.rate2, k.normed2), lambda w: (w.up,))
    back[...] = right_dot(gpre[...], whole(weights.up))
    b = at.before()
    for j in range(4):
        found = trans_dot(near.normed2[...], gpre[:, j * WIDTH : (j + 1) * WIDTH]).astype(bf16)
        for s in range(4):
            rows = slice(j * 192, (j + 1) * 192)
            grads[b, s // 2, s % 2, rows, :] = found[s * 192 : (s + 1) * 192, :]
    at.after()
    pack.put_mod(layer, 3, over_rows(back[...]))
    unit = near.unit2[...].astype(f32)
    pack.put_mod(layer, 4, over_rows(back[...] * unit))
    rate = near.rate2[:, 0:1]
    grad[...] += norm_pull(back[...] * (1.0 + small.mod(layer, 4)), unit, rate)
    at.done(lambda k: (k.unit2, k.rate2, k.normed2), lambda w: (w.up,))
    at.have(lambda k: (k.branch,), lambda w: (w.out,))
    pack.put_mod(layer, 2, over_rows(grad[...] * near.branch[...].astype(f32)))
    work[...] = (small.mod(layer, 2) * grad[...]).astype(bf16)
    refs.gatt[...] = right_dot(work[...], whole(weights.out)).astype(bf16)
    at.middle()
    at.have(lambda k: (k.qkv, k.probs))
    attend_back(near.qkv, near.probs, refs.gatt, gqkv, layer == 0)
    at.done(lambda k: (k.branch, k.qkv, k.probs), lambda w: (w.out,))
    at.have(lambda k: (k.normed1, k.attended))
    b = at.before()
    for j in range(4):
        if j < 3:
            found = trans_dot(near.normed1[...], gqkv[:, j * WIDTH : (j + 1) * WIDTH])
        else:
            found = trans_dot(near.attended[...], work[...])
        found = found.astype(bf16)
        for s in range(4):
            rows = slice(j * 192, (j + 1) * 192)
            grads[b, s // 2, s % 2, rows, :] = found[s * 192 : (s + 1) * 192, :]
    at.after()
    at.have(lambda k: (k.unit1, k.rate1), lambda w: (w.qkv,))
    back[...] = right_dot(gqkv[...], whole(weights.qkv))
    pack.put_mod(layer, 0, over_rows(back[...]))
    unit = near.unit1[...].astype(f32)
    pack.put_mod(layer, 1, over_rows(back[...] * unit))
    rate = near.rate1[:, 0:1]
    grad[...] += norm_pull(back[...] * (1.0 + small.mod(layer, 1)), unit, rate)
    at.done(lambda k: (k.normed1, k.attended, k.unit1, k.rate1), lambda w: (w.qkv,))


class Progress:
    def __init__(self, reduce, keeps, fetches):
        self.reduce, self.keeps, self.fetches = reduce, keeps, fetches
        self.tick, self.layer = 0, 1

    def have(self, saved, weights=lambda w: ()):
        self.keeps[self.layer].wait(saved)
        for copy in weights(self.fetches[self.layer]):
            copy.wait()

    def done(self, saved, weights=lambda w: ()):
        if self.layer == 1:
            self.keeps[0].start(saved)
            for copy in weights(self.fetches[0]):
                copy.start()

    def move(self, first):
        for k in range(CHUNKS):
            stage = self.tick - 2 * k
            if first <= stage < STAGES:
                self.reduce.step(stage, k)

    def before(self):
        self.move(1)
        return self.tick // 2 % 2

    def after(self):
        self.reduce.step(0, self.tick // 2)
        self.tick += 1

    def middle(self):
        self.move(0)
        self.tick += 1

    def last(self):
        return self.tick >= 2 * (CHUNKS - 1) + STAGES


def backward_blocks(refs):
    place = Place()
    enter(group_peers(place) + [place.mirror(), place.twin()] + ring_peers(place))
    keeps = [Keep(refs.near, refs.saved, layer, refs.keep.at[layer], True) for layer in range(2)]
    fetches = []
    for layer in range(2):
        copies = [
            pltpu.make_async_copy(far.at[layer], near, refs.fetch.at[layer, at])
            for at, (far, near) in enumerate(zip(refs.far, refs.weights))
        ]
        fetches.append(Weights(*copies))
    keeps[1].start(lambda k: (k.mlp, k.hidden, k.slope))
    fetches[1].down.start()
    keeps[1].start(lambda k: (k.unit2, k.rate2, k.normed2, k.branch))
    fetches[1].up.start()
    fetches[1].out.start()
    keeps[1].start(lambda k: (k.qkv, k.probs, k.normed1, k.attended, k.unit1, k.rate1))
    fetches[1].qkv.start()

    grad = refs.grad
    weight = refs.loss_weight[0]
    for here, f, patches in frame_major():
        grad[here, :] = refs.cotangent[f, patches, :].astype(f32) * weight
    small, pack = Small(refs.small_all), Small(refs.pack)
    refs.pack[...] = refs.base[...]

    reduce = Reduce(place, refs, refs.sums_out)
    little = ReduceSmall(place, refs)
    at = Progress(reduce, keeps, fetches)
    swap_sems = Sems(refs.swap_send, refs.swap_recv)
    for layer in (1, 0):
        at.layer = layer
        backward_block(layer, grad, refs, small, pack, refs.weights, at)
        turn = refs.turn.at[layer]
        if layer == 1:
            for here, f, patches in frame_major():
                turn[f, patches, :] = grad[here, :].astype(bf16)
            swap = Swap(place, swap_sems, turn, refs.turned, refs.swap_local.at[0])
            swap.start()
            at.middle()
            swap.wait()
            for j in range(4):
                grad[j * 64 : (j + 1) * 64, :] = refs.turned[j].astype(f32)
        else:
            for j in range(4):
                turn[j] = grad[j * 64 : (j + 1) * 64, :].astype(bf16)
            swap = Swap(place, swap_sems, turn, refs.grad_input, refs.swap_local.at[1])
            swap.start()
    for stage in range(5):
        little.step(stage)
        at.middle()
    while not at.last():
        at.middle()
    swap.wait()
    for k in range(CHUNKS):
        reduce.land(k, STAGES - 1)


def run_backward(forward, cotangent, loss_weight, base):
    ins = dict(
        cotangent=given(cotangent),
        loss_weight=given(loss_weight, pltpu.SMEM),
        base=given(base),
        small_all=given(forward.small_all),
        far=Weights(*[given(w, pl.ANY) for w in forward.far]),
        saved=Saved(*[given(w, pl.ANY) for w in forward.saved]),
    )
    outs = dict(
        grad_input=Buf(cotangent.shape, bf16),
        everyone=Buf((2, 4, 4, 16, 384), bf16),
        sums_out=Weights(
            *[
                Buf(shape, bf16, pl.ANY)
                for shape in ((2, 192, 2304), (2, 192, 768), (2, 192, 3072), (2, 768, 768))
            ]
        ),
    )
    scratch = dict(
        grads=Buf((2, 2, 2, 768, 768), bf16),
        side=Buf((2, 2, 768, 768), bf16),
        relay=Buf((2, 2, 2, 2, 96, SIDE), bf16),
        ring=Buf((2, 2, 2, 2, 192, SIDE), bf16),
        sums=Buf((2, 2, 2, 192, SIDE), bf16),
        cross=Buf((2, 2, 192, SIDE), bf16),
        ours=Buf((2, 2, 192, SIDE), bf16),
        ring2=Buf((2, 2, 3, 48, SIDE), bf16),
        small=Buf((2, 2, 48, SIDE), bf16),
        twin=Buf((2, 2, 48, SIDE), bf16),
        final=Buf((CHUNKS, 768, 768), bf16),
        near=SAVED,
        weights=Weights(*[Buf(shape, bf16) for shape in FULL]),
        grad=Buf((ROWS, WIDTH), f32),
        back=Buf((ROWS, WIDTH), f32),
        work=Buf((ROWS, WIDTH), bf16),
        gatt=Buf((ROWS, WIDTH), bf16),
        gpre=Buf((ROWS, 4 * WIDTH), bf16),
        gqkv=Buf((ROWS, 3 * WIDTH), bf16),
        turn=Buf((2, *cotangent.shape), bf16),
        turned=Buf(cotangent.shape, bf16),
        pack=Buf((4, 16, 384), f32),
        pack_land=Buf((3, 16, 384), f32),
        send=dma(2, 32),
        recv=dma(2, 32),
        store=dma(CHUNKS, 4),
        keep=dma(2, len(SAVED)),
        fetch=dma(2, len(FULL)),
        little_send=dma(10),
        little_recv=dma(10),
        swap_send=dma(6),
        swap_recv=dma(6),
        swap_local=dma(2),
    )
    return call_kernel(backward_blocks, 4, ins, outs, scratch)


def finish(refs):
    copies = []

    def load(far, near):
        copies.append(pltpu.make_async_copy(far, near, refs.sems.at[len(copies)]))
        copies[-1].start()
        return copies[-1]

    loads = [load(far, near) for far, near in zip(refs.sums_in, refs.near)]
    stores = []
    everyone = refs.everyone[...].astype(f32)
    embed = jnp.concatenate([everyone[:, 10, :], everyone[:, 11, :]], axis=1).astype(bf16)
    for layer in range(2):
        for part in range(3):
            cols = pl.ds(part * 384, 384)
            change = everyone[:, 4 + 3 * layer + part, :]
            refs.b_mod[layer : layer + 1, cols] = over_rows(change)
            refs.mod[layer, :, cols] = trans_dot(embed, change.astype(bf16))
        stores.append(load(refs.mod.at[layer], refs.w_mod.at[layer]))
        for half in range(2):
            value = over_rows(everyone[:, 2 * layer + half, :])
            refs.b_up[layer : layer + 1, pl.ds(half * 384, 384)] = value
    refs.grad_input[...] = refs.grad[...].astype(f32)
    for at in (3, 2, 0, 1):
        loads[at].wait()
        near, wide, far = refs.near[at], refs.wide[at], refs.sums_out[at]
        for layer in range(2):
            rows = near.shape[1]

            @pl.loop(0, rows // 32)
            def _(step, layer=layer, near=near, wide=wide):
                here = pl.ds(pl.multiple_of(step * 32, 32), 32)
                wide[layer, here, :] = near[layer, here, :].astype(f32)

            stores.append(load(wide.at[layer], far.at[layer]))
    for copy in stores:
        copy.wait()


def run_finish(back):
    ins = dict(
        everyone=given(back.everyone.reshape(32, 16, 384)),
        grad=given(back.grad_input),
        sums_in=Weights(*[given(w, pl.ANY) for w in back.sums_out]),
    )
    shapes = [w.shape for w in back.sums_out]
    outs = dict(
        grad_input=Buf(back.grad_input.shape, f32),
        w_mod=Buf((2, 768, 1152), f32, pl.ANY),
        b_mod=Buf((2, 1152), f32),
        b_up=Buf((2, 768), f32),
        sums_out=Weights(*[Buf(shape, f32, pl.ANY) for shape in shapes]),
    )
    scratch = dict(
        near=Weights(*[Buf(shape, bf16) for shape in shapes]),
        wide=Weights(*[Buf(shape, f32) for shape in shapes]),
        mod=Buf((2, 768, 1152), f32),
        sems=dma(16),
    )
    return call_kernel(finish, None, ins, outs, scratch)


def silu_plain(values):
    return values / (1.0 + jnp.exp(-values))


def sinusoid(steps, width):
    half = width // 2
    freqs = jnp.exp(-math.log(10000.0) * jnp.arange(half).astype(f32) / half)
    angles = steps.astype(f32)[:, None] * freqs[None, :]
    return jnp.concatenate([jnp.cos(angles), jnp.sin(angles)], axis=1)


def shards(
    clip_tokens, timesteps, loss_weight, cotangent, w_mod, b_mod, w_qkv, w_out, w_up, b_up, w_down
):
    embed = silu_plain(sinusoid(timesteps, WIDTH)).astype(bf16)
    mod_part = jnp.einsum("d,ldm->lm", embed[0], w_mod, preferred_element_type=f32) + b_mod.astype(
        f32
    )
    small = jnp.concatenate([b_up.astype(f32).reshape(4, 384), mod_part.reshape(6, 384)])
    small = jnp.pad(small, ((0, 6), (0, 0)))
    base = jnp.broadcast_to(0.25 * embed.astype(f32).reshape(1, 2, 384), (4, 2, 384))
    base = jnp.pad(base, ((0, 0), (10, 4), (0, 0)))
    forward = run_forward(small, clip_tokens[0], (w_qkv, w_out, w_up, w_down))
    back = run_backward(forward, cotangent[0], loss_weight, base)
    end = run_finish(back)
    sums = end.sums_out
    return (
        forward.block_output[None], end.grad_input[None], end.w_mod, end.b_mod, sums.qkv,
        sums.out, sums.up, end.b_up, sums.down
    )


def solution(mesh):
    rows = P("clip", None, "stripe", None)
    middle, last, clips = P(None, "stripe", None), P(None, None, "stripe"), P("clip")
    vector = P(None, "stripe")
    weights = (last, vector, middle, middle, middle, vector, middle)
    return jax.shard_map(
        shards,
        mesh=mesh,
        in_specs=(rows, clips, clips, rows, *weights),
        out_specs=(rows, rows, *weights),
        check_vma=False,
    )
```

```python
import math
from types import SimpleNamespace
from typing import Any, NamedTuple

import jax
import jax.numpy as jnp
from jax import lax
from jax.experimental import pallas as pl
from jax.experimental.pallas import tpu as pltpu
from jax.sharding import PartitionSpec as P

HEAD = 64
MESH = pl.DeviceIdType.MESH
bf16 = jnp.bfloat16
f32 = jnp.float32
WIDTH = 768
ROWS = 256


class Place:
    def __init__(self):
        clip, stripe = lax.axis_index("clip"), lax.axis_index("stripe")
        self.clip, self.stripe = clip, stripe
        self.ylo = lax.div(clip, 16)
        self.x = lax.rem(lax.div(clip, 4), 4)
        self.z = lax.rem(clip, 4)
        self.yhi = lax.div(stripe, 2)
        self.core = lax.rem(stripe, 2)

    def at_x(self, x):
        return (self.ylo * 16 + x * 4 + self.z, self.stripe)

    def at_z(self, z):
        return (self.ylo * 16 + self.x * 4 + z, self.stripe)

    def ring(self, axis, step):
        there = lax.rem((self.x if axis == 0 else self.z) + step, 4)
        return (self.at_x(there) if axis == 0 else self.at_z(there)), there

    def along(self, axis, step):
        x = lax.rem(self.x + step * (1 - axis), 4)
        z = lax.rem(self.z + step * axis, 4)
        return (self.ylo * 16 + x * 4 + z, self.stripe), x + (z - x) * axis

    def on_ring(self, axis):
        return self.x if axis == 0 else self.z

    def sibling(self):
        return (self.clip, self.yhi * 2 + 1 - self.core)

    def mirror(self):
        return ((1 - self.ylo) * 16 + self.x * 4 + self.z, (1 - self.yhi) * 2 + self.core)

    def twin(self):
        return ((1 - self.ylo) * 16 + self.x * 4 + self.z, self.stripe)

    def in_group(self, step):
        there = lax.rem(self.stripe + step, 4)
        return (self.clip, there), there


def enter(devices):
    barrier = pltpu.get_barrier_semaphore()
    for device in devices:
        pl.semaphore_signal(barrier, inc=1, device_id=device, device_id_type=MESH)
    pl.semaphore_wait(barrier, len(devices))


class Sems:
    def __init__(self, send, recv):
        self.send, self.recv, self.used = send, recv, 0

    def copy(self, src, dst, device):
        at = self.used
        self.used += 1
        return pltpu.make_async_remote_copy(
            src_ref=src,
            dst_ref=dst,
            send_sem=self.send.at[at],
            recv_sem=self.recv.at[at],
            device_id=device,
            device_id_type=MESH,
        )


def rows_at(start, size, grain):
    return pl.ds(pl.multiple_of(start * grain, grain), size)


class Buf:
    def __init__(self, shape, dtype, space=pltpu.VMEM, array=None):
        self.shape, self.dtype, self.space, self.array = shape, dtype, space, array


def given(array, space=pltpu.VMEM):
    return Buf(array.shape, array.dtype, space, array)


def dma(*shape):
    return pltpu.SemaphoreType.DMA(shape)


def call_kernel(body, collective_id, ins, outs, scratch):
    leaves, trees = zip(*(jax.tree.flatten(part) for part in (ins, outs, scratch)))
    ends = [len(leaves[0]), len(leaves[0]) + len(leaves[1])]

    def kernel(*refs):
        parts = (refs[: ends[0]], refs[ends[0] : ends[1]], refs[ends[1] :])
        groups = [jax.tree.unflatten(tree, part) for tree, part in zip(trees, parts)]
        body(SimpleNamespace(**groups[0], **groups[1], **groups[2]))

    results = pl.pallas_call(
        kernel,
        out_shape=[jax.ShapeDtypeStruct(b.shape, b.dtype) for b in leaves[1]],
        in_specs=[pl.BlockSpec(memory_space=b.space) for b in leaves[0]],
        out_specs=[pl.BlockSpec(memory_space=b.space) for b in leaves[1]],
        scratch_shapes=[
            pltpu.VMEM(b.shape, b.dtype) if isinstance(b, Buf) else b for b in leaves[2]
        ],
        compiler_params=pltpu.CompilerParams(
            collective_id=collective_id,
            has_side_effects=collective_id is not None,
            vmem_limit_bytes=62 * 2**20,
        ),
        name=body.__name__,
    )(*[b.array for b in leaves[0]])
    return SimpleNamespace(**jax.tree.unflatten(trees[1], results))


CHUNKS = 6
STAGES = 10
SIDE = 384


def add_into(out, *terms, rows=64):
    if len(terms) == 2 and all(t.dtype == out.dtype for t in terms):

        @pl.loop(0, out.shape[0] // 96)
        def _(step):
            at = pl.ds(pl.multiple_of(step * 96, 96), 96)
            out[at, :] = terms[0][at, :] + terms[1][at, :]

        return
    height = out.shape[0]
    rows = math.gcd(rows, height)

    @pl.loop(0, height // rows)
    def _(step):
        at = pl.ds(pl.multiple_of(step * rows, rows), rows)
        total = terms[0][at, :].astype(f32)
        for term in terms[1:]:
            total = total + term[at, :].astype(f32)
        out[at, :] = total.astype(out.dtype)


class Reduce:
    def __init__(self, place, bufs, outs):
        self.place, self.bufs, self.outs = place, bufs, outs
        self.flight = {}

    def go(self, key, *plans):
        k, stage = key
        sems = Sems(self.bufs.send.at[k % 2], self.bufs.recv.at[k % 2])
        sems.used = (0, 2, 6, 10, 11, 17, 18, 24, 28)[stage]
        copies = [sems.copy(*plan) for plan in plans]
        for copy in copies:
            copy.start()
        self.flight[key] = copies

    def land(self, *key):
        for copy in self.flight.pop(key):
            copy.wait()

    def cols(self, axis):
        return pl.ds(axis * SIDE, SIDE)

    def own(self, k, axis, step, half=None):
        there = self.place.ring(axis, step)[1] * 192
        size = 192
        if half is not None:
            there, size = there + 96 * half, 96
        rows = rows_at(there // 32, size, 32)
        return self.bufs.grads.at[k % 2, :, self.place.core, rows, self.cols(axis)]

    def step(self, stage, k):
        place, b, bufs = self.place, k % 2, self.bufs
        here = k, stage
        if stage > 0:
            self.land(k, stage - 1)
        if stage == 0:
            other = 1 - place.core
            self.go(
                here,
                *[
                    (bufs.grads.at[b, h, other], bufs.side.at[b, h], place.sibling())
                    for h in range(2)
                ],
            )
        elif stage == 1:
            for h in range(2):
                part = bufs.grads.at[b, h, place.core]
                add_into(part, part, bufs.side.at[b, h])
            self.go(
                here,
                *[
                    (
                        self.own(k, axis, 2, way),
                        bufs.relay.at[b, axis, way],
                        place.ring(axis, 1 + 2 * way)[0],
                    )
                    for axis in range(2)
                    for way in range(2)
                ],
            )
        elif stage == 2:
            plans = []
            for axis in range(2):
                for way in range(2):
                    for h in range(2):
                        half = self.own(k, axis, 1 + 2 * way, way).at[h]
                        add_into(half, half, bufs.relay.at[b, axis, way, h], rows=96)
                    device, _ = place.ring(axis, 1 + 2 * way)
                    piece = self.own(k, axis, 1 + 2 * way)
                    plans.append((piece, bufs.ring.at[b, axis, way], device))
            self.go(here, *plans)
        elif stage == 3:
            for axis in range(2):
                for h in range(2):
                    add_into(
                        bufs.sums.at[b, h, axis],
                        self.own(k, axis, 0).at[h],
                        *[bufs.ring.at[b, axis, way, h] for way in range(2)],
                    )
            self.go(
                here, (bufs.sums.at[b, 1 - place.yhi], bufs.cross.at[b], place.mirror())
            )
        elif stage == 4:
            for axis in range(2):
                ours = bufs.ours.at[b, axis]
                add_into(ours, bufs.sums.at[b, place.yhi, axis], bufs.cross.at[b, axis])
            plans = []
            for step in (1, 3, 2):
                for axis in range(2):
                    device, there = place.ring(1 - axis, step)
                    piece = bufs.ours.at[b, axis, rows_at(there, 48, 48)]
                    plans.append((piece, bufs.ring2.at[b, axis, step - 1], device))
            self.go(here, *plans)
        elif stage == 5:
            for axis in range(2):
                mine = rows_at(place.on_ring(1 - axis), 48, 48)
                add_into(
                    bufs.small.at[b, axis],
                    bufs.ours.at[b, axis, mine],
                    *[bufs.ring2.at[b, axis, step] for step in range(3)],
                    rows=48,
                )
            self.go(here, (bufs.small.at[b], bufs.twin.at[b], place.twin()))
        elif stage == 6:
            plans = []
            for axis in range(2):
                start = place.on_ring(axis) * 12 + place.on_ring(1 - axis) * 3
                piece = bufs.final.at[k, rows_at(start, 48, 16), self.cols(axis)]
                piece[...] = bufs.small[b, axis] + bufs.twin[b, axis]
                for step in (1, 3, 2):
                    plans.append((piece, piece, place.ring(1 - axis, step)[0]))
            self.go(here, *plans)
        elif stage == 7:
            plans = []
            for axis in range(2):
                mine = rows_at(place.on_ring(axis), 192, 192)
                piece = bufs.final.at[k, mine, self.cols(axis)]
                for step in (1, 3):
                    plans.append((piece, piece, place.ring(axis, step)[0]))
            self.go(here, *plans)
        elif stage == 8:
            plans = []
            for axis in range(2):
                for way in range(2):
                    came = place.ring(axis, 3 - 2 * way)[1]
                    rows = rows_at(came * 2 + way, 96, 96)
                    piece = bufs.final.at[k, rows, self.cols(axis)]
                    plans.append((piece, piece, place.ring(axis, 1 + 2 * way)[0]))
            self.go(here, *plans)
        else:
            copies = []
            layer, member = 1 - k // 3, k % 3
            for j in range(4):
                block = bufs.final.at[k, pl.ds(j * 192, 192)]
                wide = pl.ds(j * 768, 768)
                if member == 0:
                    to = self.outs.down.at[layer, pl.ds(j * 192, 192)]
                elif member == 1:
                    to = self.outs.up.at[layer, :, wide]
                elif j < 3:
                    to = self.outs.qkv.at[layer, :, wide]
                else:
                    to = self.outs.out.at[layer]
                copies.append(pltpu.make_async_copy(block, to, bufs.store.at[k, j]))
            for copy in copies:
                copy.start()
            self.flight[here] = copies

    def end(self):
        for key in list(self.flight):
            self.land(*key)


class ReduceSmall:
    def __init__(self, place, bufs):
        self.place, self.bufs = place, bufs
        self.sems = Sems(bufs.little_send, bufs.little_recv)

    def go(self, copies):
        for copy in copies:
            copy.start()
        self.flight = copies

    def land(self):
        for copy in self.flight:
            copy.wait()

    def step(self, stage):
        place, bufs, sems = self.place, self.bufs, self.sems
        if stage == 0:
            copies = []
            for step in (1, 2, 3):
                device, there = place.in_group(step)
                copies.append(sems.copy(bufs.pack.at[there], bufs.pack_land.at[step - 1], device))
            self.go(copies)
        elif stage == 1:
            self.land()
            total = bufs.pack[place.stripe]
            for step in range(3):
                total = total + bufs.pack_land[step]
            mine = bufs.everyone.at[place.ylo, place.x, place.z]
            mine[...] = total.astype(bf16)
            self.go([sems.copy(mine, mine, place.ring(0, step)[0]) for step in (1, 2, 3)])
        elif stage == 2:
            self.land()
            mine = bufs.everyone.at[place.ylo, :, place.z]
            self.go([sems.copy(mine, mine, place.ring(1, step)[0]) for step in (1, 2, 3)])
        elif stage == 3:
            self.land()
            mine = bufs.everyone.at[place.ylo]
            self.go([sems.copy(mine, mine, place.twin())])
        elif stage == 4:
            self.land()


class Gather:
    STEPS = ("begin", "fetched", "passed", "relay", "share", "end")

    def __init__(self, place, sems, own, full, local_sem):
        self.place, self.sems, self.own, self.full = place, sems, own, full
        rows, columns = own.shape
        self.quarter, self.half = rows // 4, columns // 2
        self.other = (1 - place.yhi) * 2 + place.core
        self.kept = pltpu.make_async_copy(own, full.at[place.stripe], local_sem)
        self.rings, self.relays = [], []

    def spot(self, axis, step=0, start=0, size=None):
        rows = rows_at(self.place.along(axis, step)[1], self.quarter, self.quarter)
        cols = pl.ds(pl.multiple_of(axis * self.half + start, 128), size or self.half)
        return rows, cols

    def go(self, plans):
        copies = [self.sems.copy(*plan) for plan in plans]
        for copy in copies:
            copy.start()
        return copies

    def begin(self):
        place = self.place
        spot = self.spot(1 - place.ylo)
        self.first, self.side = self.go(
            [
                (self.own.at[spot], self.full.at[(place.stripe, *spot)], place.mirror()),
                (self.own, self.full.at[place.stripe], place.sibling()),
            ]
        )
        self.kept.start()

    def spread(self, axis):
        piece = self.full.at[(self.other, *self.spot(axis))]
        self.rings += self.go(
            [(piece, piece, self.place.along(axis, step)[0]) for step in (1, 3)]
        )

    def fetched(self):
        place = self.place
        self.first.wait()
        self.spread(place.ylo)
        piece = self.full.at[(self.other, *self.spot(place.ylo))]
        self.second = self.go([(piece, piece, place.twin())])

    def passed(self):
        self.second[0].wait()
        self.spread(1 - self.place.ylo)

    def relay(self, nth):
        cut = -(-self.half // 256) * 128
        axis = (1 - nth) * self.place.ylo + nth * (1 - self.place.ylo)
        for copy in self.rings[2 * nth : 2 * nth + 2]:
            copy.wait()
        plans = []
        for way in range(2):
            start, size = (0, cut) if way == 0 else (cut, self.half - cut)
            piece = self.full.at[(self.other, *self.spot(axis, 3 - 2 * way, start, size))]
            plans.append((piece, piece, self.place.along(axis, 1 + 2 * way)[0]))
        self.relays += self.go(plans)

    def share(self):
        for copy in self.relays:
            copy.wait()
        piece = self.full.at[self.other]
        self.last = self.go([(piece, piece, self.place.sibling())])

    def end(self):
        self.kept.wait()
        self.side.wait()
        for copy in self.last:
            copy.wait()


class QuickGather(Gather):
    def begin(self):
        place = self.place
        spots = [self.spot(axis) for axis in range(2)]
        plans = [(self.own.at[s], self.full.at[(place.stripe, *s)], place.mirror()) for s in spots]
        plans.append((self.own, self.full.at[place.stripe], place.sibling()))
        *self.first, self.side = self.go(plans)
        self.kept.start()

    def fetched(self):
        for axis in range(2):
            self.first[axis].wait()
            piece = self.full.at[(self.other, *self.spot(axis))]
            self.relays += self.go(
                [(piece, piece, self.place.along(axis, step)[0]) for step in (1, 3, 2)]
            )

    def passed(self):
        pass

    def relay(self, nth):
        pass


def trans_dot(left, right):
    return lax.dot_general(left, right, (((0,), (0,)), ((), ())), preferred_element_type=f32)


def right_dot(left, right):
    return lax.dot_general(left, right, (((1,), (1,)), ((), ())), preferred_element_type=f32)


def dot(left, right):
    return jnp.dot(left, right, preferred_element_type=f32)


def norm_rows(values):
    centred = values - jnp.mean(values, axis=-1, keepdims=True)
    spread = jnp.mean(centred * centred, axis=-1, keepdims=True)
    rate = lax.rsqrt(spread + 1e-06)
    return centred * rate, rate


def norm_pull(grad, normed, rate):
    along = jnp.mean(grad * normed, axis=-1, keepdims=True)
    return rate * (grad - jnp.mean(grad, axis=-1, keepdims=True) - normed * along)


def over_rows(values):
    return jnp.sum(values, axis=0, keepdims=True)


def gelu_and_slope(v):
    square = v * v
    t = jnp.tanh(0.7978845608028654 * (v + 0.044715 * (square * v)))
    half = 0.5 * (1.0 + t)
    inner = 0.7978845608028654 * (1.0 + 0.134145 * square)
    return v * half, half + 0.5 * v * (1.0 - t * t) * inner


class Small:
    def __init__(self, ref):
        self.ref = ref

    def spot(self, layer, member, half):
        unit = 2 * member + half
        return unit // 3, 4 + 3 * layer + unit % 3

    def mod(self, layer, member):
        spots = [self.spot(layer, member, half) for half in range(2)]
        return jnp.concatenate([self.ref[s, r : r + 1, :] for s, r in spots], axis=1)

    def put_mod(self, layer, member, value):
        for half in range(2):
            s, r = self.spot(layer, member, half)
            self.ref[s, r : r + 1, :] = value[:, half * 384 : (half + 1) * 384]

    def bias(self, layer, s):
        return jnp.concatenate(
            [self.ref[s, 2 * layer + half : 2 * layer + half + 1, :] for half in range(2)], axis=1
        )

    def put_bias(self, layer, s, value):
        for half in range(2):
            r = 2 * layer + half
            self.ref[s, r : r + 1, :] = value[:, half * 384 : (half + 1) * 384]


def frame_major():
    for group in range(2):
        for frame in range(4):
            start = group * 128 + frame * 32
            yield slice(start, start + 32), frame, slice(group * 32, group * 32 + 32)


def head_mask(half):
    lane = lax.broadcasted_iota(jnp.int32, (1, 128), 1)
    return (lane >= 64 * half) & (lane < 64 * half + 64)


def same_patch():
    row = lax.broadcasted_iota(jnp.int32, (128, 128), 0)
    col = lax.broadcasted_iota(jnp.int32, (128, 128), 1)
    return lax.rem(row, 32) == lax.rem(col, 32)


def attend(qkv, attended, probs, spatial, first, last):
    size = ROWS if spatial else 128

    @pl.loop(first, last)
    def _(pair):
        def cols(member):
            return pl.ds(pl.multiple_of(member * WIDTH + pair * 128, 128), 128)

        for group in range(ROWS // size):
            here = slice(group * size, (group + 1) * size)
            query, key, value = (qkv[here, cols(member)] for member in range(3))
            query = query * jnp.asarray(HEAD**-0.5, bf16)
            outs = []
            for half in range(2):
                picked = jnp.where(head_mask(half), query, jnp.zeros_like(query))
                scores = right_dot(picked, key)
                if not spatial:
                    scores = jnp.where(same_patch(), scores, -1e30)
                expo = jnp.exp(scores - jnp.max(scores, axis=-1, keepdims=True))
                weight = (expo * (1.0 / jnp.sum(expo, axis=-1, keepdims=True))).astype(bf16)
                probs[pair * 2 + half, here, 0:size] = weight
                outs.append(dot(weight, value))
            attended[here, cols(0)] = jnp.where(head_mask(0), outs[0], outs[1]).astype(bf16)


def attend_back(qkv, probs, grad_att, grad_qkv, spatial, first, last):
    size = ROWS if spatial else 128
    scale = HEAD**-0.5

    @pl.loop(first, last)
    def _(pair):
        def cols(member):
            return pl.ds(pl.multiple_of(member * WIDTH + pair * 128, 128), 128)

        for group in range(ROWS // size):
            here = slice(group * size, (group + 1) * size)
            query, key, value = (qkv[here, cols(member)] for member in range(3))
            grad = grad_att[here, cols(0)]
            found = []
            for half in range(2):
                picked = jnp.where(head_mask(half), grad, jnp.zeros_like(grad))
                weight = probs[pair * 2 + half, here, 0:size]
                wide = weight.astype(f32)
                pull = wide * right_dot(picked, value)
                centre = jnp.sum(pull, axis=-1, keepdims=True)
                grad_scores = ((pull - wide * centre) * scale).astype(bf16)
                found.append(
                    (
                        dot(grad_scores, key),
                        trans_dot(grad_scores, query),
                        trans_dot(weight, grad),
                    )
                )
            for member in range(3):
                both = jnp.where(head_mask(0), found[0][member], found[1][member])
                grad_qkv[here, cols(member)] = both.astype(bf16)


class Weights(NamedTuple):
    qkv: Any
    out: Any
    up: Any
    down: Any


class Saved(NamedTuple):
    normed1: Any
    unit1: Any
    rate1: Any
    qkv: Any
    probs: Any
    attended: Any
    branch: Any
    unit2: Any
    rate2: Any
    normed2: Any
    slope: Any
    hidden: Any
    mlp: Any


FULL = Weights((4, 192, 2304), (4, 192, 768), (4, 192, 3072), (4, 768, 768))
SAVED = Saved(
    normed1=Buf((ROWS, WIDTH), bf16),
    unit1=Buf((ROWS, WIDTH), bf16),
    rate1=Buf((ROWS, 128), f32),
    qkv=Buf((ROWS, 3 * WIDTH), bf16),
    probs=Buf((12, ROWS, ROWS), bf16),
    attended=Buf((ROWS, WIDTH), bf16),
    branch=Buf((ROWS, WIDTH), bf16),
    unit2=Buf((ROWS, WIDTH), bf16),
    rate2=Buf((ROWS, 128), f32),
    normed2=Buf((ROWS, WIDTH), bf16),
    slope=Buf((ROWS, 4 * WIDTH), bf16),
    hidden=Buf((ROWS, 4 * WIDTH), bf16),
    mlp=Buf((ROWS, WIDTH), bf16),
)


class Keep:
    def __init__(self, near, far, layer, sem, inward):
        copies = []
        for at, (a, b) in enumerate(zip(near, far)):
            a, b = (b.at[layer], a) if inward else (a, b.at[layer])
            copies.append(pltpu.make_async_copy(a, b, sem.at[at]))
        self.copies = Saved(*copies)

    def start(self, pick):
        for copy in pick(self.copies):
            copy.start()

    def wait(self, pick):
        for copy in pick(self.copies):
            copy.wait()


def spread_lanes(value):
    return jnp.broadcast_to(value, (ROWS, 128))


def whole(ref, cols=slice(None)):
    value = ref[:, :, cols]
    return value.reshape(value.shape[0] * value.shape[1], value.shape[2])


def forward_block(layer, rows, mid, near, keep, small, weights, move):
    unit, rate = norm_rows(rows[...])
    near.unit1[...] = unit.astype(bf16)
    near.rate1[...] = spread_lanes(rate)
    shift, scale = small.mod(layer, 0), small.mod(layer, 1)
    near.normed1[...] = (unit * (1.0 + scale) + shift).astype(bf16)
    keep.start(lambda k: (k.unit1, k.rate1, k.normed1))
    if layer == 0:
        move()
    move()
    move()
    for j in range(3):
        cols = slice(j * WIDTH, (j + 1) * WIDTH)
        near.qkv[:, cols] = dot(near.normed1[...], whole(weights.qkv, cols)).astype(bf16)
        if j > 0:
            move()
    keep.start(lambda k: (k.qkv,))
    for pair in range(0, 6, 2):
        attend(near.qkv, near.attended, near.probs, layer == 0, pair, pair + 2)
        move()
    keep.start(lambda k: (k.probs, k.attended))
    move()
    branch = dot(near.attended[...], whole(weights.out))
    near.branch[...] = branch.astype(bf16)
    mid[...] = rows[...] + small.mod(layer, 2) * branch
    unit, rate = norm_rows(mid[...])
    near.unit2[...] = unit.astype(bf16)
    near.rate2[...] = spread_lanes(rate)
    shift, scale = small.mod(layer, 3), small.mod(layer, 4)
    near.normed2[...] = (unit * (1.0 + scale) + shift).astype(bf16)
    keep.start(lambda k: (k.branch, k.unit2, k.rate2, k.normed2))
    move()
    move()
    for j in range(4):
        cols = slice(j * WIDTH, (j + 1) * WIDTH)
        pre = dot(near.normed2[...], whole(weights.up, cols)) + small.bias(layer, j)
        hidden, slope = gelu_and_slope(pre)
        near.hidden[:, cols] = hidden.astype(bf16)
        near.slope[:, cols] = slope.astype(bf16)
        move()
    keep.start(lambda k: (k.hidden, k.slope))
    move()
    mlp = dot(near.hidden[...], whole(weights.down))
    near.mlp[...] = mlp.astype(bf16)
    keep.start(lambda k: (k.mlp,))
    rows[...] = mid[...] + small.mod(layer, 5) * mlp
    move()


def group_peers(place):
    return [place.in_group(step)[0] for step in (1, 2, 3)]


def ring_peers(place):
    return [place.ring(axis, step)[0] for axis in range(2) for step in (1, 2, 3)]


class Swap:
    def __init__(self, place, sems, source, result, local_sem):
        self.copies = []
        for step in (2, 1, 3):
            device, there = place.in_group(step)
            self.copies.append(sems.copy(source.at[there], result.at[place.stripe], device))
        mine = place.stripe
        self.copies.append(pltpu.make_async_copy(source.at[mine], result.at[mine], local_sem))

    def start(self):
        for copy in self.copies:
            copy.start()

    def wait(self):
        for copy in self.copies:
            copy.wait()


ARRIVALS = (
    ((0, 0), (1, 0),),
    ((2, 0), (3, 0), (4, 0), (5, 0), (6, 0), (7, 0),),
    ((0, 1), (1, 1),),
    (),
    ((2, 1), (0, 2), (0, 3), (3, 1), (1, 2), (1, 3), (4, 1), (5, 1), (2, 2), (2, 3), (0, 4), (1, 4), (6, 1), (3, 2), (3, 3), (4, 2), (2, 4), (7, 1), (5, 2), (0, 5), (4, 3), (1, 5), (5, 3), (6, 2), (0, 6),),
    (),
    ((3, 4),),
    ((6, 3), (7, 2), (4, 4),),
    ((2, 5), (5, 4),),
    ((7, 3),),
    ((3, 5), (6, 4),),
    ((1, 6),),
    (),
    ((2, 6),),
    ((7, 4),),
    ((4, 5), (5, 5),),
    ((6, 5),),
    ((7, 5),),
    ((3, 6),),
    (),
    (),
    (),
    ((4, 6),),
    (),
    (),
    (),
    (),
    (),
    (),
    ((5, 6),),
    (),
    ((6, 6),),
    (),
    (),
    (),
    (),
    ((7, 6),),
    (),
)


def forward_blocks(refs):
    place = Place()
    enter(group_peers(place) + [place.mirror(), place.twin()] + ring_peers(place))
    sems = Sems(refs.send, refs.recv)
    local = refs.local
    greet = []
    for step in (1, 2, 3):
        device, _ = place.in_group(step)
        greet.append(sems.copy(refs.small, refs.small_all.at[place.stripe], device))
    mine = refs.small_all.at[place.stripe]
    greet.append(pltpu.make_async_copy(refs.small, mine, local.at[0]))

    g, outward = [], []
    for layer in range(2):
        for own, full, far in zip(refs.shards, refs.full, refs.far):
            at = len(g)
            kind = Gather
            g.append(kind(place, sems, own.at[layer], full.at[layer], local.at[2 + at]))
            outward.append(
                pltpu.make_async_copy(full.at[layer], far.at[layer], local.at[10 + at])
            )
    points = iter(ARRIVALS)

    def move():
        for at, step in next(points):
            one = g[at]
            (
                one.begin, one.fetched, one.passed, lambda: one.relay(0), lambda: one.relay(1),
                one.share, one.end
            )[step]()
            if step == 6:
                outward[at].start()

    for copy in greet:
        copy.start()
    move()
    swap = Swap(place, sems, refs.tokens, refs.frame, local.at[1])
    swap.start()
    move()
    for copy in greet:
        copy.wait()
    swap.wait()
    move()
    small = Small(refs.small_all)
    rows = refs.rows
    for j in range(4):
        rows[j * 64 : (j + 1) * 64, :] = refs.frame[j].astype(f32)
    keeps = []
    for layer in range(2):
        keep = Keep(refs.near[layer], refs.saved, layer, refs.keep.at[layer], False)
        keeps.append(keep)
        weights = Weights(*[full.at[layer] for full in refs.full])

        forward_block(layer, rows, refs.mid, refs.near[layer], keep, small, weights, move)
        if layer == 0:
            for j in range(4):
                refs.turn[j] = rows[j * 64 : (j + 1) * 64, :].astype(bf16)
            swap = Swap(place, sems, refs.turn, refs.turned, local.at[18])
            swap.start()
            move()
            swap.wait()
            move()
            for here, f, patches in frame_major():
                rows[here, :] = refs.turned[f, patches, :].astype(f32)
    for here, f, patches in frame_major():
        refs.block_output[f, patches, :] = rows[here, :].astype(bf16)
    for copy in outward:
        copy.wait()
    for keep in keeps:
        keep.wait(lambda k: k)


def run_forward(small, tokens, shards):
    ins = dict(
        small=given(small),
        tokens=given(tokens),
        shards=Weights(*[given(w, pl.ANY) for w in shards]),
    )
    outs = dict(
        small_all=Buf((4, 16, 384), f32),
        block_output=Buf(tokens.shape, bf16),
        far=Weights(*[Buf((2, *shape), bf16, pl.ANY) for shape in FULL]),
        saved=Saved(*[Buf((2, *b.shape), b.dtype, pl.ANY) for b in SAVED]),
    )
    scratch = dict(
        full=Weights(*[Buf((2, *shape), bf16) for shape in FULL]),
        near=(SAVED, SAVED),
        rows=Buf((ROWS, WIDTH), f32),
        mid=Buf((ROWS, WIDTH), f32),
        frame=Buf(tokens.shape, bf16),
        turn=Buf(tokens.shape, bf16),
        turned=Buf(tokens.shape, bf16),
        send=dma(110),
        recv=dma(110),
        local=dma(20),
        keep=dma(2, len(SAVED)),
    )
    return call_kernel(forward_blocks, 0, ins, outs, scratch)


def backward_block(layer, grad, refs, small, pack, weights, at):
    near, grads, work, gpre, back, gqkv = (
        refs.near, refs.grads, refs.work, refs.gpre, refs.back, refs.gqkv
    )
    at.have(lambda k: (k.mlp, k.hidden))
    b = 1 - layer
    pack.put_mod(layer, 5, over_rows(grad[...] * near.mlp[...].astype(f32)))
    work[...] = (small.mod(layer, 5) * grad[...]).astype(bf16)
    at.move()
    for s in range(4):
        cols = slice(s * WIDTH, (s + 1) * WIDTH)
        grads[b, s // 2, s % 2] = trans_dot(near.hidden[:, cols], work[...]).astype(bf16)
    at.move()
    at.have(lambda k: (k.slope,), lambda w: (w.down,))
    for j in range(4):
        cols = slice(j * WIDTH, (j + 1) * WIDTH)
        pre = (right_dot(work[...], weights.down[j]) * near.slope[:, cols].astype(f32)).astype(bf16)
        gpre[:, cols] = pre
        pack.put_bias(layer, j, over_rows(pre.astype(f32)))
        if j % 2 == 1:
            at.move()
    at.done(lambda k: (k.mlp, k.hidden, k.slope), lambda w: (w.down,))
    at.have(lambda k: (k.unit2, k.rate2, k.normed2), lambda w: (w.up,))
    back[...] = right_dot(gpre[...], whole(weights.up))
    at.move()
    for j in range(4):
        found = trans_dot(near.normed2[...], gpre[:, j * WIDTH : (j + 1) * WIDTH]).astype(bf16)
        for s in range(4):
            rows = slice(j * 192, (j + 1) * 192)
            grads[1 - b, s // 2, s % 2, rows, :] = found[s * 192 : (s + 1) * 192, :]
    at.move()
    pack.put_mod(layer, 3, over_rows(back[...]))
    unit = near.unit2[...].astype(f32)
    pack.put_mod(layer, 4, over_rows(back[...] * unit))
    rate = near.rate2[:, 0:1]
    grad[...] += norm_pull(back[...] * (1.0 + small.mod(layer, 4)), unit, rate)
    at.move()
    at.done(lambda k: (k.unit2, k.rate2, k.normed2), lambda w: (w.up,))
    at.have(lambda k: (k.branch,), lambda w: (w.out,))
    pack.put_mod(layer, 2, over_rows(grad[...] * near.branch[...].astype(f32)))
    work[...] = (small.mod(layer, 2) * grad[...]).astype(bf16)
    refs.gatt[...] = right_dot(work[...], whole(weights.out)).astype(bf16)
    at.move()
    at.have(lambda k: (k.qkv, k.probs))
    for pair in range(6):
        attend_back(near.qkv, near.probs, refs.gatt, gqkv, layer == 0, pair, pair + 1)
        at.move()
    at.done(lambda k: (k.branch, k.qkv, k.probs), lambda w: (w.out,))
    at.have(lambda k: (k.normed1, k.attended))
    for j in range(4):
        if j < 3:
            found = trans_dot(near.normed1[...], gqkv[:, j * WIDTH : (j + 1) * WIDTH])
        else:
            found = trans_dot(near.attended[...], work[...])
        found = found.astype(bf16)
        for s in range(4):
            rows = slice(j * 192, (j + 1) * 192)
            grads[b, s // 2, s % 2, rows, :] = found[s * 192 : (s + 1) * 192, :]
    at.move()
    at.have(lambda k: (k.unit1, k.rate1), lambda w: (w.qkv,))
    back[...] = right_dot(gqkv[...], whole(weights.qkv))
    at.move()
    pack.put_mod(layer, 0, over_rows(back[...]))
    unit = near.unit1[...].astype(f32)
    pack.put_mod(layer, 1, over_rows(back[...] * unit))
    rate = near.rate1[:, 0:1]
    grad[...] += norm_pull(back[...] * (1.0 + small.mod(layer, 1)), unit, rate)
    at.done(lambda k: (k.normed1, k.attended, k.unit1, k.rate1), lambda w: (w.qkv,))
    at.move()


ORDER = (
    (),
    ((0, 0),),
    (),
    (),
    ((1, 0),),
    ((0, 1),),
    ((2, 0),),
    (),
    ((1, 1),),
    (),
    (),
    (),
    (),
    ((3, 0),),
    ((0, 2), (2, 1),),
    (),
    (),
    ((1, 2), (4, 0),),
    ((3, 1),),
    ((0, 3),),
    ((2, 2),),
    ((5, 0),),
    ((1, 3), (4, 1), (6, 0), (3, 2),),
    ((0, 4), (2, 3),),
    ((7, 0), (5, 1),),
    (),
    ((1, 4), (4, 2),),
    ((6, 1),),
    ((3, 3),),
    (),
    ((8, 0),),
    (),
    ((0, 5), (2, 4), (5, 2),),
    ((4, 3), (9, 0), (7, 1),),
    ((1, 5), (6, 2),),
    (),
    ((3, 4), (5, 3), (8, 1), (2, 5), (7, 2), (6, 3), (4, 4), (9, 1), (3, 5), (8, 2), (7, 3), (5, 4), (9, 2), (4, 5), (6, 4), (8, 3), (5, 5), (7, 4), (9, 3), (6, 5), (8, 4), (7, 5), (9, 4), (8, 5), (9, 5),),
)


class Progress:
    def __init__(self, reduce, keeps, fetches):
        self.reduce, self.keeps, self.fetches = reduce, keeps, fetches
        self.point, self.layer = 0, 1

    def have(self, saved, weights=lambda w: ()):
        self.keeps[self.layer].wait(saved)
        for copy in weights(self.fetches[self.layer]):
            copy.wait()

    def done(self, saved, weights=lambda w: ()):
        if self.layer == 1:
            self.keeps[0].start(saved)
            for copy in weights(self.fetches[0]):
                copy.start()

    def move(self):
        for stage, k in ORDER[self.point]:
            self.reduce.step(stage, k)
        self.point += 1


def backward_blocks(refs):
    place = Place()
    enter(group_peers(place) + [place.mirror(), place.twin()] + ring_peers(place))
    keeps = [Keep(refs.near, refs.saved, layer, refs.keep.at[layer], True) for layer in range(2)]
    fetches = []
    for layer in range(2):
        copies = [
            pltpu.make_async_copy(far.at[layer], near, refs.fetch.at[layer, at])
            for at, (far, near) in enumerate(zip(refs.far, refs.weights))
        ]
        fetches.append(Weights(*copies))
    keeps[1].start(lambda k: (k.mlp, k.hidden, k.slope))
    fetches[1].down.start()
    keeps[1].start(lambda k: (k.unit2, k.rate2, k.normed2, k.branch))
    fetches[1].up.start()
    fetches[1].out.start()
    keeps[1].start(lambda k: (k.qkv, k.probs, k.normed1, k.attended, k.unit1, k.rate1))
    fetches[1].qkv.start()

    grad = refs.grad
    weight = refs.loss_weight[0]
    for here, f, patches in frame_major():
        grad[here, :] = refs.cotangent[f, patches, :].astype(f32) * weight
    small, pack = Small(refs.small_all), Small(refs.pack)
    refs.pack[...] = refs.base[...]

    reduce = Reduce(place, refs, refs.sums_out)
    little = ReduceSmall(place, refs)
    at = Progress(reduce, keeps, fetches)
    swap_sems = Sems(refs.swap_send, refs.swap_recv)
    for layer in (1, 0):
        at.layer = layer
        backward_block(layer, grad, refs, small, pack, refs.weights, at)
        turn = refs.turn.at[layer]
        if layer == 1:
            for here, f, patches in frame_major():
                turn[f, patches, :] = grad[here, :].astype(bf16)
            swap = Swap(place, swap_sems, turn, refs.turned, refs.swap_local.at[0])
            swap.start()
            swap.wait()
            for j in range(4):
                grad[j * 64 : (j + 1) * 64, :] = refs.turned[j].astype(f32)
            at.move()
        else:
            for j in range(4):
                turn[j] = grad[j * 64 : (j + 1) * 64, :].astype(bf16)
            swap = Swap(place, swap_sems, turn, refs.grad_input, refs.swap_local.at[1])
            swap.start()
    at.move()
    rest = ORDER[at.point]
    for nth, (stage, k) in enumerate(rest):
        if nth % 5 == 0 and nth // 5 < 5:
            little.step(nth // 5)
        reduce.step(stage, k)
    swap.wait()
    reduce.end()


def run_backward(forward, cotangent, loss_weight, base):
    ins = dict(
        cotangent=given(cotangent),
        loss_weight=given(loss_weight, pltpu.SMEM),
        base=given(base),
        small_all=given(forward.small_all),
        far=Weights(*[given(w, pl.ANY) for w in forward.far]),
        saved=Saved(*[given(w, pl.ANY) for w in forward.saved]),
    )
    outs = dict(
        grad_input=Buf(cotangent.shape, bf16),
        everyone=Buf((2, 4, 4, 16, 384), bf16),
        sums_out=Weights(
            *[
                Buf(shape, bf16, pl.ANY)
                for shape in ((2, 192, 2304), (2, 192, 768), (2, 192, 3072), (2, 768, 768))
            ]
        ),
    )
    scratch = dict(
        grads=Buf((2, 2, 2, 768, 768), bf16),
        side=Buf((2, 2, 768, 768), bf16),
        relay=Buf((2, 2, 2, 2, 96, SIDE), bf16),
        ring=Buf((2, 2, 2, 2, 192, SIDE), bf16),
        sums=Buf((2, 2, 2, 192, SIDE), bf16),
        cross=Buf((2, 2, 192, SIDE), bf16),
        ours=Buf((2, 2, 192, SIDE), bf16),
        ring2=Buf((2, 2, 3, 48, SIDE), bf16),
        small=Buf((2, 2, 48, SIDE), bf16),
        twin=Buf((2, 2, 48, SIDE), bf16),
        final=Buf((CHUNKS, 768, 768), bf16),
        near=SAVED,
        weights=Weights(*[Buf(shape, bf16) for shape in FULL]),
        grad=Buf((ROWS, WIDTH), f32),
        back=Buf((ROWS, WIDTH), f32),
        work=Buf((ROWS, WIDTH), bf16),
        gatt=Buf((ROWS, WIDTH), bf16),
        gpre=Buf((ROWS, 4 * WIDTH), bf16),
        gqkv=Buf((ROWS, 3 * WIDTH), bf16),
        turn=Buf((2, *cotangent.shape), bf16),
        turned=Buf(cotangent.shape, bf16),
        pack=Buf((4, 16, 384), f32),
        pack_land=Buf((3, 16, 384), f32),
        send=dma(2, 32),
        recv=dma(2, 32),
        store=dma(CHUNKS, 4),
        keep=dma(2, len(SAVED)),
        fetch=dma(2, len(FULL)),
        little_send=dma(10),
        little_recv=dma(10),
        swap_send=dma(6),
        swap_recv=dma(6),
        swap_local=dma(2),
    )
    return call_kernel(backward_blocks, 4, ins, outs, scratch)


def finish(refs):
    copies = []

    def load(far, near):
        copies.append(pltpu.make_async_copy(far, near, refs.sems.at[len(copies)]))
        copies[-1].start()
        return copies[-1]

    loads = {at: load(refs.sums_in[at], refs.near[at]) for at in (1, 0, 2, 3)}
    stores = []
    for at in (1, 0, 2, 3):
        loads[at].wait()
        near, wide, far = refs.near[at], refs.wide[at], refs.sums_out[at]
        for layer in range(2):
            rows = near.shape[1]

            @pl.loop(0, rows // 32)
            def _(step, layer=layer, near=near, wide=wide):
                here = pl.ds(pl.multiple_of(step * 32, 32), 32)
                wide[layer, here, :] = near[layer, here, :].astype(f32)

            stores.append(load(wide.at[layer], far.at[layer]))
    refs.grad_input[...] = refs.grad[...].astype(f32)
    everyone = refs.everyone[...].astype(f32)
    embed = jnp.concatenate([everyone[:, 10, :], everyone[:, 11, :]], axis=1).astype(bf16)
    for layer in range(2):
        for part in range(3):
            cols = pl.ds(part * 384, 384)
            change = everyone[:, 4 + 3 * layer + part, :]
            refs.b_mod[layer : layer + 1, cols] = over_rows(change)
            refs.mod[layer, :, cols] = trans_dot(embed, change.astype(bf16))
        stores.append(load(refs.mod.at[layer], refs.w_mod.at[layer]))
        for half in range(2):
            value = over_rows(everyone[:, 2 * layer + half, :])
            refs.b_up[layer : layer + 1, pl.ds(half * 384, 384)] = value
    for copy in stores:
        copy.wait()


def run_finish(back):
    ins = dict(
        everyone=given(back.everyone.reshape(32, 16, 384)),
        grad=given(back.grad_input),
        sums_in=Weights(*[given(w, pl.ANY) for w in back.sums_out]),
    )
    shapes = [w.shape for w in back.sums_out]
    outs = dict(
        grad_input=Buf(back.grad_input.shape, f32),
        w_mod=Buf((2, 768, 1152), f32, pl.ANY),
        b_mod=Buf((2, 1152), f32),
        b_up=Buf((2, 768), f32),
        sums_out=Weights(*[Buf(shape, f32, pl.ANY) for shape in shapes]),
    )
    scratch = dict(
        near=Weights(*[Buf(shape, bf16) for shape in shapes]),
        wide=Weights(*[Buf(shape, f32) for shape in shapes]),
        mod=Buf((2, 768, 1152), f32),
        sems=dma(16),
    )
    return call_kernel(finish, None, ins, outs, scratch)


def silu_plain(values):
    return values / (1.0 + jnp.exp(-values))


def sinusoid(steps, width):
    half = width // 2
    freqs = jnp.exp(-math.log(10000.0) * jnp.arange(half).astype(f32) / half)
    angles = steps.astype(f32)[:, None] * freqs[None, :]
    return jnp.concatenate([jnp.cos(angles), jnp.sin(angles)], axis=1)


def shards(
    clip_tokens, timesteps, loss_weight, cotangent, w_mod, b_mod, w_qkv, w_out, w_up, b_up, w_down
):
    embed = silu_plain(sinusoid(timesteps, WIDTH)).astype(bf16)
    mod_part = jnp.einsum("d,ldm->lm", embed[0], w_mod, preferred_element_type=f32) + b_mod.astype(
        f32
    )
    small = jnp.concatenate([b_up.astype(f32).reshape(4, 384), mod_part.reshape(6, 384)])
    small = jnp.pad(small, ((0, 6), (0, 0)))
    base = jnp.broadcast_to(0.25 * embed.astype(f32).reshape(1, 2, 384), (4, 2, 384))
    base = jnp.pad(base, ((0, 0), (10, 4), (0, 0)))
    forward = run_forward(small, clip_tokens[0], (w_qkv, w_out, w_up, w_down))
    back = run_backward(forward, cotangent[0], loss_weight, base)
    end = run_finish(back)
    sums = end.sums_out
    return (
        forward.block_output[None], end.grad_input[None], end.w_mod, end.b_mod, sums.qkv,
        sums.out, sums.up, end.b_up, sums.down
    )


def solution(mesh):
    rows = P("clip", None, "stripe", None)
    middle, last, clips = P(None, "stripe", None), P(None, None, "stripe"), P("clip")
    vector = P(None, "stripe")
    weights = (last, vector, middle, middle, middle, vector, middle)
    return jax.shard_map(
        shards,
        mesh=mesh,
        in_specs=(rows, clips, clips, rows, *weights),
        out_specs=(rows, rows, *weights),
        check_vma=False,
    )
```

```python
import math
from types import SimpleNamespace
from typing import Any, NamedTuple

import jax
import jax.numpy as jnp
from jax import lax
from jax.experimental import pallas as pl
from jax.experimental.pallas import tpu as pltpu
from jax.sharding import PartitionSpec as P

HEAD = 64
MESH = pl.DeviceIdType.MESH
bf16 = jnp.bfloat16
f32 = jnp.float32
WIDTH = 768
ROWS = 256


class Place:
    def __init__(self):
        clip, stripe = lax.axis_index("clip"), lax.axis_index("stripe")
        self.clip, self.stripe = clip, stripe
        self.ylo = lax.div(clip, 16)
        self.x = lax.rem(lax.div(clip, 4), 4)
        self.z = lax.rem(clip, 4)
        self.yhi = lax.div(stripe, 2)
        self.core = lax.rem(stripe, 2)

    def at_x(self, x):
        return (self.ylo * 16 + x * 4 + self.z, self.stripe)

    def at_z(self, z):
        return (self.ylo * 16 + self.x * 4 + z, self.stripe)

    def ring(self, axis, step):
        there = lax.rem((self.x if axis == 0 else self.z) + step, 4)
        return (self.at_x(there) if axis == 0 else self.at_z(there)), there

    def along(self, axis, step):
        x = lax.rem(self.x + step * (1 - axis), 4)
        z = lax.rem(self.z + step * axis, 4)
        return (self.ylo * 16 + x * 4 + z, self.stripe), x + (z - x) * axis

    def on_ring(self, axis):
        return self.x if axis == 0 else self.z

    def sibling(self):
        return (self.clip, self.yhi * 2 + 1 - self.core)

    def mirror(self):
        return ((1 - self.ylo) * 16 + self.x * 4 + self.z, (1 - self.yhi) * 2 + self.core)

    def twin(self):
        return ((1 - self.ylo) * 16 + self.x * 4 + self.z, self.stripe)

    def in_group(self, step):
        there = lax.rem(self.stripe + step, 4)
        return (self.clip, there), there


def enter(devices):
    barrier = pltpu.get_barrier_semaphore()
    for device in devices:
        pl.semaphore_signal(barrier, inc=1, device_id=device, device_id_type=MESH)
    pl.semaphore_wait(barrier, len(devices))


class Sems:
    def __init__(self, send, recv):
        self.send, self.recv, self.used = send, recv, 0

    def copy(self, src, dst, device):
        at = self.used
        self.used += 1
        return pltpu.make_async_remote_copy(
            src_ref=src,
            dst_ref=dst,
            send_sem=self.send.at[at],
            recv_sem=self.recv.at[at],
            device_id=device,
            device_id_type=MESH,
        )


def rows_at(start, size, grain):
    return pl.ds(pl.multiple_of(start * grain, grain), size)


class Buf:
    def __init__(self, shape, dtype, space=pltpu.VMEM, array=None):
        self.shape, self.dtype, self.space, self.array = shape, dtype, space, array


def given(array, space=pltpu.VMEM):
    return Buf(array.shape, array.dtype, space, array)


def dma(*shape):
    return pltpu.SemaphoreType.DMA(shape)


def call_kernel(body, collective_id, ins, outs, scratch):
    leaves, trees = zip(*(jax.tree.flatten(part) for part in (ins, outs, scratch)))
    ends = [len(leaves[0]), len(leaves[0]) + len(leaves[1])]

    def kernel(*refs):
        parts = (refs[: ends[0]], refs[ends[0] : ends[1]], refs[ends[1] :])
        groups = [jax.tree.unflatten(tree, part) for tree, part in zip(trees, parts)]
        body(SimpleNamespace(**groups[0], **groups[1], **groups[2]))

    results = pl.pallas_call(
        kernel,
        out_shape=[jax.ShapeDtypeStruct(b.shape, b.dtype) for b in leaves[1]],
        in_specs=[pl.BlockSpec(memory_space=b.space) for b in leaves[0]],
        out_specs=[pl.BlockSpec(memory_space=b.space) for b in leaves[1]],
        scratch_shapes=[
            pltpu.VMEM(b.shape, b.dtype) if isinstance(b, Buf) else b for b in leaves[2]
        ],
        compiler_params=pltpu.CompilerParams(
            collective_id=collective_id,
            has_side_effects=collective_id is not None,
            vmem_limit_bytes=62 * 2**20,
        ),
        name=body.__name__,
    )(*[b.array for b in leaves[0]])
    return SimpleNamespace(**jax.tree.unflatten(trees[1], results))


CHUNKS = 6
STAGES = 10
SIDE = 384


def add_into(out, *terms, rows=64):
    if len(terms) == 2 and all(t.dtype == out.dtype for t in terms):

        @pl.loop(0, out.shape[0] // 96)
        def _(step):
            at = pl.ds(pl.multiple_of(step * 96, 96), 96)
            out[at, :] = terms[0][at, :] + terms[1][at, :]

        return
    height = out.shape[0]
    rows = math.gcd(rows, height)

    @pl.loop(0, height // rows)
    def _(step):
        at = pl.ds(pl.multiple_of(step * rows, rows), rows)
        total = terms[0][at, :].astype(f32)
        for term in terms[1:]:
            total = total + term[at, :].astype(f32)
        out[at, :] = total.astype(out.dtype)


class Reduce:
    def __init__(self, place, bufs, outs):
        self.place, self.bufs, self.outs = place, bufs, outs
        self.flight = {}

    def go(self, key, *plans):
        k, stage = key
        sems = Sems(self.bufs.send.at[k % 2], self.bufs.recv.at[k % 2])
        sems.used = (0, 2, 6, 10, 11, 17, 18, 24, 28)[stage]
        copies = [sems.copy(*plan) for plan in plans]
        for copy in copies:
            copy.start()
        self.flight[key] = copies

    def land(self, *key):
        for copy in self.flight.pop(key):
            copy.wait()

    def cols(self, axis):
        return pl.ds(axis * SIDE, SIDE)

    def own(self, k, axis, step, half=None):
        there = self.place.ring(axis, step)[1] * 192
        size = 192
        if half is not None:
            there, size = there + 96 * half, 96
        rows = rows_at(there // 32, size, 32)
        return self.bufs.grads.at[k % 2, :, self.place.core, rows, self.cols(axis)]

    def step(self, stage, k):
        place, b, bufs = self.place, k % 2, self.bufs
        here = k, stage
        if stage > 0:
            self.land(k, stage - 1)
        if stage == 0:
            other = 1 - place.core
            self.go(
                here,
                *[
                    (bufs.grads.at[b, h, other], bufs.side.at[b, h], place.sibling())
                    for h in range(2)
                ],
            )
        elif stage == 1:
            for h in range(2):
                part = bufs.grads.at[b, h, place.core]
                add_into(part, part, bufs.side.at[b, h])
            self.go(
                here,
                *[
                    (
                        self.own(k, axis, 2, way),
                        bufs.relay.at[b, axis, way],
                        place.ring(axis, 1 + 2 * way)[0],
                    )
                    for axis in range(2)
                    for way in range(2)
                ],
            )
        elif stage == 2:
            plans = []
            for axis in range(2):
                for way in range(2):
                    for h in range(2):
                        half = self.own(k, axis, 1 + 2 * way, way).at[h]
                        add_into(half, half, bufs.relay.at[b, axis, way, h], rows=96)
                    device, _ = place.ring(axis, 1 + 2 * way)
                    piece = self.own(k, axis, 1 + 2 * way)
                    plans.append((piece, bufs.ring.at[b, axis, way], device))
            self.go(here, *plans)
        elif stage == 3:
            for axis in range(2):
                for h in range(2):
                    add_into(
                        bufs.sums.at[b, h, axis],
                        self.own(k, axis, 0).at[h],
                        *[bufs.ring.at[b, axis, way, h] for way in range(2)],
                    )
            self.go(
                here, (bufs.sums.at[b, 1 - place.yhi], bufs.cross.at[b], place.mirror())
            )
        elif stage == 4:
            for axis in range(2):
                ours = bufs.ours.at[b, axis]
                add_into(ours, bufs.sums.at[b, place.yhi, axis], bufs.cross.at[b, axis])
            plans = []
            for step in (1, 3, 2):
                for axis in range(2):
                    device, there = place.ring(1 - axis, step)
                    piece = bufs.ours.at[b, axis, rows_at(there, 48, 48)]
                    plans.append((piece, bufs.ring2.at[b, axis, step - 1], device))
            self.go(here, *plans)
        elif stage == 5:
            for axis in range(2):
                mine = rows_at(place.on_ring(1 - axis), 48, 48)
                add_into(
                    bufs.small.at[b, axis],
                    bufs.ours.at[b, axis, mine],
                    *[bufs.ring2.at[b, axis, step] for step in range(3)],
                    rows=48,
                )
            self.go(here, (bufs.small.at[b], bufs.twin.at[b], place.twin()))
        elif stage == 6:
            plans = []
            for axis in range(2):
                start = place.on_ring(axis) * 12 + place.on_ring(1 - axis) * 3
                piece = bufs.final.at[k, rows_at(start, 48, 16), self.cols(axis)]
                piece[...] = bufs.small[b, axis] + bufs.twin[b, axis]
                for step in (1, 3, 2):
                    plans.append((piece, piece, place.ring(1 - axis, step)[0]))
            self.go(here, *plans)
        elif stage == 7:
            plans = []
            for axis in range(2):
                mine = rows_at(place.on_ring(axis), 192, 192)
                piece = bufs.final.at[k, mine, self.cols(axis)]
                for step in (1, 3):
                    plans.append((piece, piece, place.ring(axis, step)[0]))
            self.go(here, *plans)
        elif stage == 8:
            plans = []
            for axis in range(2):
                for way in range(2):
                    came = place.ring(axis, 3 - 2 * way)[1]
                    rows = rows_at(came * 2 + way, 96, 96)
                    piece = bufs.final.at[k, rows, self.cols(axis)]
                    plans.append((piece, piece, place.ring(axis, 1 + 2 * way)[0]))
            self.go(here, *plans)
        else:
            copies = []
            layer, member = 1 - k // 3, k % 3
            for j in range(4):
                block = bufs.final.at[k, pl.ds(j * 192, 192)]
                wide = pl.ds(j * 768, 768)
                if member == 0:
                    to = self.outs.down.at[layer, pl.ds(j * 192, 192)]
                elif member == 1:
                    to = self.outs.up.at[layer, :, wide]
                elif j < 3:
                    to = self.outs.qkv.at[layer, :, wide]
                else:
                    to = self.outs.out.at[layer]
                copies.append(pltpu.make_async_copy(block, to, bufs.store.at[k, j]))
            for copy in copies:
                copy.start()
            self.flight[here] = copies

    def end(self):
        for key in list(self.flight):
            self.land(*key)


class ReduceSmall:
    def __init__(self, place, bufs):
        self.place, self.bufs = place, bufs
        self.sems = Sems(bufs.little_send, bufs.little_recv)

    def go(self, copies):
        for copy in copies:
            copy.start()
        self.flight = copies

    def land(self):
        for copy in self.flight:
            copy.wait()

    def step(self, stage):
        place, bufs, sems = self.place, self.bufs, self.sems
        if stage == 0:
            copies = []
            for step in (1, 2, 3):
                device, there = place.in_group(step)
                copies.append(sems.copy(bufs.pack.at[there], bufs.pack_land.at[step - 1], device))
            self.go(copies)
        elif stage == 1:
            self.land()
            total = bufs.pack[place.stripe]
            for step in range(3):
                total = total + bufs.pack_land[step]
            mine = bufs.everyone.at[place.ylo, place.x, place.z]
            mine[...] = total.astype(bf16)
            self.go([sems.copy(mine, mine, place.ring(0, step)[0]) for step in (1, 2, 3)])
        elif stage == 2:
            self.land()
            mine = bufs.everyone.at[place.ylo, :, place.z]
            self.go([sems.copy(mine, mine, place.ring(1, step)[0]) for step in (1, 2, 3)])
        elif stage == 3:
            self.land()
            mine = bufs.everyone.at[place.ylo]
            self.go([sems.copy(mine, mine, place.twin())])
        elif stage == 4:
            self.land()


class Gather:
    STEPS = ("begin", "fetched", "passed", "relay", "share", "end")

    def __init__(self, place, sems, own, full, local_sem):
        self.place, self.sems, self.own, self.full = place, sems, own, full
        rows, columns = own.shape
        self.quarter, self.half = rows // 4, columns // 2
        self.other = (1 - place.yhi) * 2 + place.core
        self.kept = pltpu.make_async_copy(own, full.at[place.stripe], local_sem)
        self.rings, self.relays = [], []

    def spot(self, axis, step=0, start=0, size=None):
        rows = rows_at(self.place.along(axis, step)[1], self.quarter, self.quarter)
        cols = pl.ds(pl.multiple_of(axis * self.half + start, 128), size or self.half)
        return rows, cols

    def go(self, plans):
        copies = [self.sems.copy(*plan) for plan in plans]
        for copy in copies:
            copy.start()
        return copies

    def begin(self):
        place = self.place
        spot = self.spot(1 - place.ylo)
        self.first, self.side = self.go(
            [
                (self.own.at[spot], self.full.at[(place.stripe, *spot)], place.mirror()),
                (self.own, self.full.at[place.stripe], place.sibling()),
            ]
        )
        self.kept.start()

    def spread(self, axis):
        piece = self.full.at[(self.other, *self.spot(axis))]
        self.rings += self.go(
            [(piece, piece, self.place.along(axis, step)[0]) for step in (1, 3)]
        )

    def fetched(self):
        place = self.place
        self.first.wait()
        self.spread(place.ylo)
        piece = self.full.at[(self.other, *self.spot(place.ylo))]
        self.second = self.go([(piece, piece, place.twin())])

    def passed(self):
        self.second[0].wait()
        self.spread(1 - self.place.ylo)

    def relay(self, nth):
        cut = -(-self.half // 256) * 128
        axis = (1 - nth) * self.place.ylo + nth * (1 - self.place.ylo)
        for copy in self.rings[2 * nth : 2 * nth + 2]:
            copy.wait()
        plans = []
        for way in range(2):
            start, size = (0, cut) if way == 0 else (cut, self.half - cut)
            piece = self.full.at[(self.other, *self.spot(axis, 3 - 2 * way, start, size))]
            plans.append((piece, piece, self.place.along(axis, 1 + 2 * way)[0]))
        self.relays += self.go(plans)

    def share(self):
        for copy in self.relays:
            copy.wait()
        piece = self.full.at[self.other]
        self.last = self.go([(piece, piece, self.place.sibling())])

    def end(self):
        self.kept.wait()
        self.side.wait()
        for copy in self.last:
            copy.wait()


class QuickGather(Gather):
    def begin(self):
        place = self.place
        spots = [self.spot(axis) for axis in range(2)]
        plans = [(self.own.at[s], self.full.at[(place.stripe, *s)], place.mirror()) for s in spots]
        plans.append((self.own, self.full.at[place.stripe], place.sibling()))
        *self.first, self.side = self.go(plans)
        self.kept.start()

    def fetched(self):
        for axis in range(2):
            self.first[axis].wait()
            piece = self.full.at[(self.other, *self.spot(axis))]
            self.relays += self.go(
                [(piece, piece, self.place.along(axis, step)[0]) for step in (1, 3, 2)]
            )

    def passed(self):
        pass

    def relay(self, nth):
        pass


def trans_dot(left, right):
    return lax.dot_general(left, right, (((0,), (0,)), ((), ())), preferred_element_type=f32)


def right_dot(left, right):
    return lax.dot_general(left, right, (((1,), (1,)), ((), ())), preferred_element_type=f32)


def dot(left, right):
    return jnp.dot(left, right, preferred_element_type=f32)


def norm_rows(values):
    centred = values - jnp.mean(values, axis=-1, keepdims=True)
    spread = jnp.mean(centred * centred, axis=-1, keepdims=True)
    rate = lax.rsqrt(spread + 1e-06)
    return centred * rate, rate


def norm_pull(grad, normed, rate):
    along = jnp.mean(grad * normed, axis=-1, keepdims=True)
    return rate * (grad - jnp.mean(grad, axis=-1, keepdims=True) - normed * along)


def over_rows(values):
    return jnp.sum(values, axis=0, keepdims=True)


def gelu_and_slope(v):
    square = v * v
    t = jnp.tanh(0.7978845608028654 * (v + 0.044715 * (square * v)))
    half = 0.5 * (1.0 + t)
    inner = 0.7978845608028654 * (1.0 + 0.134145 * square)
    return v * half, half + 0.5 * v * (1.0 - t * t) * inner


class Small:
    def __init__(self, ref):
        self.ref = ref

    def spot(self, layer, member, half):
        unit = 2 * member + half
        return unit // 3, 4 + 3 * layer + unit % 3

    def mod(self, layer, member):
        spots = [self.spot(layer, member, half) for half in range(2)]
        return jnp.concatenate([self.ref[s, r : r + 1, :] for s, r in spots], axis=1)

    def put_mod(self, layer, member, value):
        for half in range(2):
            s, r = self.spot(layer, member, half)
            self.ref[s, r : r + 1, :] = value[:, half * 384 : (half + 1) * 384]

    def bias(self, layer, s):
        return jnp.concatenate(
            [self.ref[s, 2 * layer + half : 2 * layer + half + 1, :] for half in range(2)], axis=1
        )

    def put_bias(self, layer, s, value):
        for half in range(2):
            r = 2 * layer + half
            self.ref[s, r : r + 1, :] = value[:, half * 384 : (half + 1) * 384]


def frame_major():
    for group in range(2):
        for frame in range(4):
            start = group * 128 + frame * 32
            yield slice(start, start + 32), frame, slice(group * 32, group * 32 + 32)


def head_mask(half):
    lane = lax.broadcasted_iota(jnp.int32, (1, 128), 1)
    return (lane >= 64 * half) & (lane < 64 * half + 64)


def same_patch():
    row = lax.broadcasted_iota(jnp.int32, (128, 128), 0)
    col = lax.broadcasted_iota(jnp.int32, (128, 128), 1)
    return lax.rem(row, 32) == lax.rem(col, 32)


def attend(qkv, attended, probs, spatial, first, last):
    size = ROWS if spatial else 128

    @pl.loop(first, last)
    def _(pair):
        def cols(member):
            return pl.ds(pl.multiple_of(member * WIDTH + pair * 128, 128), 128)

        for group in range(ROWS // size):
            here = slice(group * size, (group + 1) * size)
            query, key, value = (qkv[here, cols(member)] for member in range(3))
            query = query * jnp.asarray(HEAD**-0.5, bf16)
            outs = []
            for half in range(2):
                picked = jnp.where(head_mask(half), query, jnp.zeros_like(query))
                scores = right_dot(picked, key)
                if not spatial:
                    scores = jnp.where(same_patch(), scores, -1e30)
                expo = jnp.exp(scores - jnp.max(scores, axis=-1, keepdims=True))
                weight = (expo * (1.0 / jnp.sum(expo, axis=-1, keepdims=True))).astype(bf16)
                probs[pair * 2 + half, here, 0:size] = weight
                outs.append(dot(weight, value))
            attended[here, cols(0)] = jnp.where(head_mask(0), outs[0], outs[1]).astype(bf16)


def attend_back(qkv, probs, grad_att, grad_qkv, spatial, first, last):
    size = ROWS if spatial else 128
    scale = HEAD**-0.5

    @pl.loop(first, last)
    def _(pair):
        def cols(member):
            return pl.ds(pl.multiple_of(member * WIDTH + pair * 128, 128), 128)

        for group in range(ROWS // size):
            here = slice(group * size, (group + 1) * size)
            query, key, value = (qkv[here, cols(member)] for member in range(3))
            grad = grad_att[here, cols(0)]
            found = []
            for half in range(2):
                picked = jnp.where(head_mask(half), grad, jnp.zeros_like(grad))
                weight = probs[pair * 2 + half, here, 0:size]
                wide = weight.astype(f32)
                pull = wide * right_dot(picked, value)
                centre = jnp.sum(pull, axis=-1, keepdims=True)
                grad_scores = ((pull - wide * centre) * scale).astype(bf16)
                found.append(
                    (
                        dot(grad_scores, key),
                        trans_dot(grad_scores, query),
                        trans_dot(weight, grad),
                    )
                )
            for member in range(3):
                both = jnp.where(head_mask(0), found[0][member], found[1][member])
                grad_qkv[here, cols(member)] = both.astype(bf16)


class Weights(NamedTuple):
    qkv: Any
    out: Any
    up: Any
    down: Any


class Saved(NamedTuple):
    normed1: Any
    unit1: Any
    rate1: Any
    qkv: Any
    probs: Any
    attended: Any
    branch: Any
    unit2: Any
    rate2: Any
    normed2: Any
    slope: Any
    hidden: Any
    mlp: Any


FULL = Weights((4, 192, 2304), (4, 192, 768), (4, 192, 3072), (4, 768, 768))
SAVED = Saved(
    normed1=Buf((ROWS, WIDTH), bf16),
    unit1=Buf((ROWS, WIDTH), bf16),
    rate1=Buf((ROWS, 128), f32),
    qkv=Buf((ROWS, 3 * WIDTH), bf16),
    probs=Buf((12, ROWS, ROWS), bf16),
    attended=Buf((ROWS, WIDTH), bf16),
    branch=Buf((ROWS, WIDTH), bf16),
    unit2=Buf((ROWS, WIDTH), bf16),
    rate2=Buf((ROWS, 128), f32),
    normed2=Buf((ROWS, WIDTH), bf16),
    slope=Buf((ROWS, 4 * WIDTH), bf16),
    hidden=Buf((ROWS, 4 * WIDTH), bf16),
    mlp=Buf((ROWS, WIDTH), bf16),
)


class Keep:
    def __init__(self, near, far, layer, sem, inward):
        copies = []
        for at, (a, b) in enumerate(zip(near, far)):
            a, b = (b.at[layer], a) if inward else (a, b.at[layer])
            copies.append(pltpu.make_async_copy(a, b, sem.at[at]))
        self.copies = Saved(*copies)

    def start(self, pick):
        for copy in pick(self.copies):
            copy.start()

    def wait(self, pick):
        for copy in pick(self.copies):
            copy.wait()


def spread_lanes(value):
    return jnp.broadcast_to(value, (ROWS, 128))


def whole(ref, cols=slice(None)):
    value = ref[:, :, cols]
    return value.reshape(value.shape[0] * value.shape[1], value.shape[2])


def forward_block(layer, rows, mid, near, keep, small, weights, move):
    unit, rate = norm_rows(rows[...])
    near.unit1[...] = unit.astype(bf16)
    near.rate1[...] = spread_lanes(rate)
    shift, scale = small.mod(layer, 0), small.mod(layer, 1)
    near.normed1[...] = (unit * (1.0 + scale) + shift).astype(bf16)
    keep.start(lambda k: (k.unit1, k.rate1, k.normed1))
    if layer == 0:
        move()
    move()
    move()
    for j in range(3):
        cols = slice(j * WIDTH, (j + 1) * WIDTH)
        near.qkv[:, cols] = dot(near.normed1[...], whole(weights.qkv, cols)).astype(bf16)
        if j > 0:
            move()
    keep.start(lambda k: (k.qkv,))
    for pair in range(0, 6, 2):
        attend(near.qkv, near.attended, near.probs, layer == 0, pair, pair + 2)
        move()
    keep.start(lambda k: (k.probs, k.attended))
    move()
    branch = dot(near.attended[...], whole(weights.out))
    near.branch[...] = branch.astype(bf16)
    mid[...] = rows[...] + small.mod(layer, 2) * branch
    unit, rate = norm_rows(mid[...])
    near.unit2[...] = unit.astype(bf16)
    near.rate2[...] = spread_lanes(rate)
    shift, scale = small.mod(layer, 3), small.mod(layer, 4)
    near.normed2[...] = (unit * (1.0 + scale) + shift).astype(bf16)
    keep.start(lambda k: (k.branch, k.unit2, k.rate2, k.normed2))
    move()
    move()
    for j in range(4):
        cols = slice(j * WIDTH, (j + 1) * WIDTH)
        pre = dot(near.normed2[...], whole(weights.up, cols)) + small.bias(layer, j)
        hidden, slope = gelu_and_slope(pre)
        near.hidden[:, cols] = hidden.astype(bf16)
        near.slope[:, cols] = slope.astype(bf16)
        move()
    keep.start(lambda k: (k.hidden, k.slope))
    move()
    mlp = dot(near.hidden[...], whole(weights.down))
    near.mlp[...] = mlp.astype(bf16)
    keep.start(lambda k: (k.mlp,))
    rows[...] = mid[...] + small.mod(layer, 5) * mlp
    move()


def group_peers(place):
    return [place.in_group(step)[0] for step in (1, 2, 3)]


def ring_peers(place):
    return [place.ring(axis, step)[0] for axis in range(2) for step in (1, 2, 3)]


class Swap:
    def __init__(self, place, sems, source, result, local_sem):
        self.copies = []
        for step in (2, 1, 3):
            device, there = place.in_group(step)
            self.copies.append(sems.copy(source.at[there], result.at[place.stripe], device))
        mine = place.stripe
        self.copies.append(pltpu.make_async_copy(source.at[mine], result.at[mine], local_sem))

    def start(self):
        for copy in self.copies:
            copy.start()

    def wait(self):
        for copy in self.copies:
            copy.wait()


ARRIVALS = (
    ((0, 0), (1, 0),),
    ((2, 0), (3, 0), (0, 1), (1, 1), (4, 0), (5, 0), (6, 0), (7, 0),),
    (),
    (),
    ((0, 5), (1, 5), (0, 6),),
    ((2, 1),),
    (),
    (),
    (),
    ((3, 1),),
    ((2, 5),),
    ((1, 6),),
    (),
    ((2, 6),),
    ((4, 1),),
    ((5, 1),),
    ((3, 5),),
    (),
    ((3, 6),),
    ((4, 5),),
    ((6, 1), (5, 5),),
    (),
    ((4, 6),),
    ((7, 1),),
    (),
    ((6, 5),),
    (),
    ((7, 5),),
    (),
    ((5, 6),),
    (),
    ((6, 6),),
    (),
    (),
    (),
    (),
    ((7, 6),),
    (),
)


def forward_blocks(refs):
    place = Place()
    enter(group_peers(place) + [place.mirror(), place.twin()] + ring_peers(place))
    sems = Sems(refs.send, refs.recv)
    local = refs.local
    greet = []
    for step in (1, 2, 3):
        device, _ = place.in_group(step)
        greet.append(sems.copy(refs.small, refs.small_all.at[place.stripe], device))
    mine = refs.small_all.at[place.stripe]
    greet.append(pltpu.make_async_copy(refs.small, mine, local.at[0]))

    g, outward = [], []
    for layer in range(2):
        for own, full, far in zip(refs.shards, refs.full, refs.far):
            at = len(g)
            kind = QuickGather
            g.append(kind(place, sems, own.at[layer], full.at[layer], local.at[2 + at]))
            outward.append(
                pltpu.make_async_copy(full.at[layer], far.at[layer], local.at[10 + at])
            )
    points = iter(ARRIVALS)

    def move():
        for at, step in next(points):
            one = g[at]
            (
                one.begin, one.fetched, one.passed, lambda: one.relay(0), lambda: one.relay(1),
                one.share, one.end
            )[step]()
            if step == 6:
                outward[at].start()

    for copy in greet:
        copy.start()
    move()
    swap = Swap(place, sems, refs.tokens, refs.frame, local.at[1])
    swap.start()
    move()
    for copy in greet:
        copy.wait()
    swap.wait()
    move()
    small = Small(refs.small_all)
    rows = refs.rows
    for j in range(4):
        rows[j * 64 : (j + 1) * 64, :] = refs.frame[j].astype(f32)
    keeps = []
    for layer in range(2):
        keep = Keep(refs.near[layer], refs.saved, layer, refs.keep.at[layer], False)
        keeps.append(keep)
        weights = Weights(*[full.at[layer] for full in refs.full])

        forward_block(layer, rows, refs.mid, refs.near[layer], keep, small, weights, move)
        if layer == 0:
            for j in range(4):
                refs.turn[j] = rows[j * 64 : (j + 1) * 64, :].astype(bf16)
            swap = Swap(place, sems, refs.turn, refs.turned, local.at[18])
            swap.start()
            move()
            swap.wait()
            move()
            for here, f, patches in frame_major():
                rows[here, :] = refs.turned[f, patches, :].astype(f32)
    for here, f, patches in frame_major():
        refs.block_output[f, patches, :] = rows[here, :].astype(bf16)
    for copy in outward:
        copy.wait()
    for keep in keeps:
        keep.wait(lambda k: k)


def run_forward(small, tokens, shards):
    ins = dict(
        small=given(small),
        tokens=given(tokens),
        shards=Weights(*[given(w, pl.ANY) for w in shards]),
    )
    outs = dict(
        small_all=Buf((4, 16, 384), f32),
        block_output=Buf(tokens.shape, bf16),
        far=Weights(*[Buf((2, *shape), bf16, pl.ANY) for shape in FULL]),
        saved=Saved(*[Buf((2, *b.shape), b.dtype, pl.ANY) for b in SAVED]),
    )
    scratch = dict(
        full=Weights(*[Buf((2, *shape), bf16) for shape in FULL]),
        near=(SAVED, SAVED),
        rows=Buf((ROWS, WIDTH), f32),
        mid=Buf((ROWS, WIDTH), f32),
        frame=Buf(tokens.shape, bf16),
        turn=Buf(tokens.shape, bf16),
        turned=Buf(tokens.shape, bf16),
        send=dma(110),
        recv=dma(110),
        local=dma(20),
        keep=dma(2, len(SAVED)),
    )
    return call_kernel(forward_blocks, 0, ins, outs, scratch)


def backward_block(layer, grad, refs, small, pack, weights, at, leave):
    near, grads, work, gpre, back, gqkv = (
        refs.near, refs.grads, refs.work, refs.gpre, refs.back, refs.gqkv
    )
    at.have(lambda k: (k.mlp, k.hidden))
    b = 1 - layer
    pack.put_mod(layer, 5, over_rows(grad[...] * near.mlp[...].astype(f32)))
    work[...] = (small.mod(layer, 5) * grad[...]).astype(bf16)
    at.move()
    for s in range(4):
        cols = slice(s * WIDTH, (s + 1) * WIDTH)
        grads[b, s // 2, s % 2] = trans_dot(near.hidden[:, cols], work[...]).astype(bf16)
    at.move()
    at.have(lambda k: (k.slope,), lambda w: (w.down,))
    for j in range(4):
        cols = slice(j * WIDTH, (j + 1) * WIDTH)
        pre = (right_dot(work[...], weights.down[j]) * near.slope[:, cols].astype(f32)).astype(bf16)
        gpre[:, cols] = pre
        pack.put_bias(layer, j, over_rows(pre.astype(f32)))
        if j % 2 == 1:
            at.move()
    at.done(lambda k: (k.mlp, k.hidden, k.slope), lambda w: (w.down,))
    at.have(lambda k: (k.unit2, k.rate2, k.normed2), lambda w: (w.up,))
    back[...] = right_dot(gpre[...], whole(weights.up))
    at.move()
    for j in range(4):
        found = trans_dot(near.normed2[...], gpre[:, j * WIDTH : (j + 1) * WIDTH]).astype(bf16)
        for s in range(4):
            rows = slice(j * 192, (j + 1) * 192)
            grads[1 - b, s // 2, s % 2, rows, :] = found[s * 192 : (s + 1) * 192, :]
    at.move()
    pack.put_mod(layer, 3, over_rows(back[...]))
    unit = near.unit2[...].astype(f32)
    pack.put_mod(layer, 4, over_rows(back[...] * unit))
    rate = near.rate2[:, 0:1]
    grad[...] += norm_pull(back[...] * (1.0 + small.mod(layer, 4)), unit, rate)
    at.move()
    at.done(lambda k: (k.unit2, k.rate2, k.normed2), lambda w: (w.up,))
    at.have(lambda k: (k.branch,), lambda w: (w.out,))
    pack.put_mod(layer, 2, over_rows(grad[...] * near.branch[...].astype(f32)))
    work[...] = (small.mod(layer, 2) * grad[...]).astype(bf16)
    refs.gatt[...] = right_dot(work[...], whole(weights.out)).astype(bf16)
    at.move()
    at.have(lambda k: (k.qkv, k.probs))
    for pair in range(6):
        attend_back(near.qkv, near.probs, refs.gatt, gqkv, layer == 0, pair, pair + 1)
        at.move()
    at.done(lambda k: (k.branch, k.qkv, k.probs), lambda w: (w.out,))
    def make():
        at.have(lambda k: (k.normed1, k.attended))
        for j in range(4):
            if j < 3:
                found = trans_dot(near.normed1[...], gqkv[:, j * WIDTH : (j + 1) * WIDTH])
            else:
                found = trans_dot(near.attended[...], work[...])
            found = found.astype(bf16)
            for s in range(4):
                rows = slice(j * 192, (j + 1) * 192)
                grads[b, s // 2, s % 2, rows, :] = found[s * 192 : (s + 1) * 192, :]
        at.move()

    if layer == 0:
        make()
    at.have(lambda k: (k.unit1, k.rate1), lambda w: (w.qkv,))
    back[...] = right_dot(gqkv[...], whole(weights.qkv))
    at.move()
    pack.put_mod(layer, 0, over_rows(back[...]))
    unit = near.unit1[...].astype(f32)
    pack.put_mod(layer, 1, over_rows(back[...] * unit))
    rate = near.rate1[:, 0:1]
    grad[...] += norm_pull(back[...] * (1.0 + small.mod(layer, 1)), unit, rate)
    leave()
    at.move()
    if layer == 1:
        make()
    at.done(lambda k: (k.normed1, k.attended, k.unit1, k.rate1), lambda w: (w.qkv,))


ORDER = (
    (),
    ((0, 0),),
    (),
    (),
    ((1, 0),),
    ((0, 1),),
    (),
    ((2, 0),),
    ((1, 1),),
    (),
    (),
    (),
    (),
    (),
    (),
    ((3, 0),),
    ((0, 2), (2, 1),),
    ((1, 2), (4, 0),),
    ((3, 1),),
    ((0, 3), (2, 2),),
    ((5, 0),),
    (),
    ((4, 1), (6, 0), (1, 3), (3, 2),),
    ((0, 4), (5, 1), (7, 0),),
    ((2, 3), (6, 1), (1, 4), (4, 2), (8, 0),),
    (),
    (),
    (),
    (),
    (),
    ((3, 3), (7, 1),),
    (),
    ((0, 5), (2, 4), (5, 2),),
    ((9, 0),),
    ((1, 5), (4, 3), (6, 2), (8, 1),),
    (),
    ((3, 4), (2, 5), (5, 3), (7, 2), (9, 1), (6, 3), (4, 4), (3, 5), (8, 2), (7, 3), (5, 4), (9, 2), (4, 5), (6, 4), (8, 3), (5, 5), (7, 4), (9, 3), (6, 5), (8, 4), (7, 5), (9, 4), (8, 5), (9, 5),),
)


class Progress:
    def __init__(self, reduce, keeps, fetches):
        self.reduce, self.keeps, self.fetches = reduce, keeps, fetches
        self.point, self.layer = 0, 1

    def have(self, saved, weights=lambda w: ()):
        self.keeps[self.layer].wait(saved)
        for copy in weights(self.fetches[self.layer]):
            copy.wait()

    def done(self, saved, weights=lambda w: ()):
        if self.layer == 1:
            self.keeps[0].start(saved)
            for copy in weights(self.fetches[0]):
                copy.start()

    def move(self):
        for stage, k in ORDER[self.point]:
            self.reduce.step(stage, k)
        self.point += 1


def backward_blocks(refs):
    place = Place()
    enter(group_peers(place) + [place.mirror(), place.twin()] + ring_peers(place))
    keeps = [Keep(refs.near, refs.saved, layer, refs.keep.at[layer], True) for layer in range(2)]
    fetches = []
    for layer in range(2):
        copies = [
            pltpu.make_async_copy(far.at[layer], near, refs.fetch.at[layer, at])
            for at, (far, near) in enumerate(zip(refs.far, refs.weights))
        ]
        fetches.append(Weights(*copies))
    keeps[1].start(lambda k: (k.mlp, k.hidden, k.slope))
    fetches[1].down.start()
    keeps[1].start(lambda k: (k.unit2, k.rate2, k.normed2, k.branch))
    fetches[1].up.start()
    fetches[1].out.start()
    keeps[1].start(lambda k: (k.qkv, k.probs, k.normed1, k.attended, k.unit1, k.rate1))
    fetches[1].qkv.start()

    grad = refs.grad
    weight = refs.loss_weight[0]
    for here, f, patches in frame_major():
        grad[here, :] = refs.cotangent[f, patches, :].astype(f32) * weight
    small, pack = Small(refs.small_all), Small(refs.pack)
    refs.pack[...] = refs.base[...]

    reduce = Reduce(place, refs, refs.sums_out)
    little = ReduceSmall(place, refs)
    at = Progress(reduce, keeps, fetches)
    swap_sems = Sems(refs.swap_send, refs.swap_recv)
    swaps = [
        Swap(place, swap_sems, refs.turn.at[layer], result, refs.swap_local.at[layer])
        for layer, result in ((1, refs.turned), (0, refs.grad_input))
    ]

    def leave_temporal():
        for here, f, patches in frame_major():
            refs.turn[1, f, patches, :] = grad[here, :].astype(bf16)
        swaps[0].start()

    def leave_spatial():
        for j in range(4):
            refs.turn[0, j] = grad[j * 64 : (j + 1) * 64, :].astype(bf16)
        swaps[1].start()

    backward_block(1, grad, refs, small, pack, refs.weights, at, leave_temporal)
    swaps[0].wait()
    for j in range(4):
        grad[j * 64 : (j + 1) * 64, :] = refs.turned[j].astype(f32)
    at.move()
    at.layer = 0
    backward_block(0, grad, refs, small, pack, refs.weights, at, leave_spatial)
    at.move()
    rest = ORDER[at.point]
    for nth, (stage, k) in enumerate(rest):
        if nth % 5 == 0 and nth // 5 < 5:
            little.step(nth // 5)
        reduce.step(stage, k)
    swaps[1].wait()
    reduce.end()


def run_backward(forward, cotangent, loss_weight, base):
    ins = dict(
        cotangent=given(cotangent),
        loss_weight=given(loss_weight, pltpu.SMEM),
        base=given(base),
        small_all=given(forward.small_all),
        far=Weights(*[given(w, pl.ANY) for w in forward.far]),
        saved=Saved(*[given(w, pl.ANY) for w in forward.saved]),
    )
    outs = dict(
        grad_input=Buf(cotangent.shape, bf16),
        everyone=Buf((2, 4, 4, 16, 384), bf16),
        sums_out=Weights(
            *[
                Buf(shape, bf16, pl.ANY)
                for shape in ((2, 192, 2304), (2, 192, 768), (2, 192, 3072), (2, 768, 768))
            ]
        ),
    )
    scratch = dict(
        grads=Buf((2, 2, 2, 768, 768), bf16),
        side=Buf((2, 2, 768, 768), bf16),
        relay=Buf((2, 2, 2, 2, 96, SIDE), bf16),
        ring=Buf((2, 2, 2, 2, 192, SIDE), bf16),
        sums=Buf((2, 2, 2, 192, SIDE), bf16),
        cross=Buf((2, 2, 192, SIDE), bf16),
        ours=Buf((2, 2, 192, SIDE), bf16),
        ring2=Buf((2, 2, 3, 48, SIDE), bf16),
        small=Buf((2, 2, 48, SIDE), bf16),
        twin=Buf((2, 2, 48, SIDE), bf16),
        final=Buf((CHUNKS, 768, 768), bf16),
        near=SAVED,
        weights=Weights(*[Buf(shape, bf16) for shape in FULL]),
        grad=Buf((ROWS, WIDTH), f32),
        back=Buf((ROWS, WIDTH), f32),
        work=Buf((ROWS, WIDTH), bf16),
        gatt=Buf((ROWS, WIDTH), bf16),
        gpre=Buf((ROWS, 4 * WIDTH), bf16),
        gqkv=Buf((ROWS, 3 * WIDTH), bf16),
        turn=Buf((2, *cotangent.shape), bf16),
        turned=Buf(cotangent.shape, bf16),
        pack=Buf((4, 16, 384), f32),
        pack_land=Buf((3, 16, 384), f32),
        send=dma(2, 32),
        recv=dma(2, 32),
        store=dma(CHUNKS, 4),
        keep=dma(2, len(SAVED)),
        fetch=dma(2, len(FULL)),
        little_send=dma(10),
        little_recv=dma(10),
        swap_send=dma(6),
        swap_recv=dma(6),
        swap_local=dma(2),
    )
    return call_kernel(backward_blocks, 4, ins, outs, scratch)


def finish(refs):
    copies = []

    def load(far, near):
        copies.append(pltpu.make_async_copy(far, near, refs.sems.at[len(copies)]))
        copies[-1].start()
        return copies[-1]

    loads = {at: load(refs.sums_in[at], refs.near[at]) for at in (1, 0, 2, 3)}
    stores = []
    for at in (1, 0, 2, 3):
        loads[at].wait()
        near, wide, far = refs.near[at], refs.wide[at], refs.sums_out[at]
        for layer in range(2):
            rows = near.shape[1]

            @pl.loop(0, rows // 32)
            def _(step, layer=layer, near=near, wide=wide):
                here = pl.ds(pl.multiple_of(step * 32, 32), 32)
                wide[layer, here, :] = near[layer, here, :].astype(f32)

            stores.append(load(wide.at[layer], far.at[layer]))
    refs.grad_input[...] = refs.grad[...].astype(f32)
    everyone = refs.everyone[...].astype(f32)
    embed = jnp.concatenate([everyone[:, 10, :], everyone[:, 11, :]], axis=1).astype(bf16)
    for layer in range(2):
        for part in range(3):
            cols = pl.ds(part * 384, 384)
            change = everyone[:, 4 + 3 * layer + part, :]
            refs.b_mod[layer : layer + 1, cols] = over_rows(change)
            refs.mod[layer, :, cols] = trans_dot(embed, change.astype(bf16))
        stores.append(load(refs.mod.at[layer], refs.w_mod.at[layer]))
        for half in range(2):
            value = over_rows(everyone[:, 2 * layer + half, :])
            refs.b_up[layer : layer + 1, pl.ds(half * 384, 384)] = value
    for copy in stores:
        copy.wait()


def run_finish(back):
    ins = dict(
        everyone=given(back.everyone.reshape(32, 16, 384)),
        grad=given(back.grad_input),
        sums_in=Weights(*[given(w, pl.ANY) for w in back.sums_out]),
    )
    shapes = [w.shape for w in back.sums_out]
    outs = dict(
        grad_input=Buf(back.grad_input.shape, f32),
        w_mod=Buf((2, 768, 1152), f32, pl.ANY),
        b_mod=Buf((2, 1152), f32),
        b_up=Buf((2, 768), f32),
        sums_out=Weights(*[Buf(shape, f32, pl.ANY) for shape in shapes]),
    )
    scratch = dict(
        near=Weights(*[Buf(shape, bf16) for shape in shapes]),
        wide=Weights(*[Buf(shape, f32) for shape in shapes]),
        mod=Buf((2, 768, 1152), f32),
        sems=dma(16),
    )
    return call_kernel(finish, None, ins, outs, scratch)


def silu_plain(values):
    return values / (1.0 + jnp.exp(-values))


def sinusoid(steps, width):
    half = width // 2
    freqs = jnp.exp(-math.log(10000.0) * jnp.arange(half).astype(f32) / half)
    angles = steps.astype(f32)[:, None] * freqs[None, :]
    return jnp.concatenate([jnp.cos(angles), jnp.sin(angles)], axis=1)


def shards(
    clip_tokens, timesteps, loss_weight, cotangent, w_mod, b_mod, w_qkv, w_out, w_up, b_up, w_down
):
    embed = silu_plain(sinusoid(timesteps, WIDTH)).astype(bf16)
    mod_part = jnp.einsum("d,ldm->lm", embed[0], w_mod, preferred_element_type=f32) + b_mod.astype(
        f32
    )
    small = jnp.concatenate([b_up.astype(f32).reshape(4, 384), mod_part.reshape(6, 384)])
    small = jnp.pad(small, ((0, 6), (0, 0)))
    base = jnp.broadcast_to(0.25 * embed.astype(f32).reshape(1, 2, 384), (4, 2, 384))
    base = jnp.pad(base, ((0, 0), (10, 4), (0, 0)))
    forward = run_forward(small, clip_tokens[0], (w_qkv, w_out, w_up, w_down))
    back = run_backward(forward, cotangent[0], loss_weight, base)
    end = run_finish(back)
    sums = end.sums_out
    return (
        forward.block_output[None], end.grad_input[None], end.w_mod, end.b_mod, sums.qkv,
        sums.out, sums.up, end.b_up, sums.down
    )


def solution(mesh):
    rows = P("clip", None, "stripe", None)
    middle, last, clips = P(None, "stripe", None), P(None, None, "stripe"), P("clip")
    vector = P(None, "stripe")
    weights = (last, vector, middle, middle, middle, vector, middle)
    return jax.shard_map(
        shards,
        mesh=mesh,
        in_specs=(rows, clips, clips, rows, *weights),
        out_specs=(rows, rows, *weights),
        check_vma=False,
    )
```

```python
import math
from types import SimpleNamespace
from typing import Any, NamedTuple

import jax
import jax.numpy as jnp
from jax import lax
from jax.experimental import pallas as pl
from jax.experimental.pallas import tpu as pltpu
from jax.sharding import PartitionSpec as P

HEAD = 64
MESH = pl.DeviceIdType.MESH
bf16 = jnp.bfloat16
f32 = jnp.float32
WIDTH = 768
ROWS = 256


class Place:
    def __init__(self):
        clip, stripe = lax.axis_index("clip"), lax.axis_index("stripe")
        self.clip, self.stripe = clip, stripe
        self.ylo = lax.div(clip, 16)
        self.x = lax.rem(lax.div(clip, 4), 4)
        self.z = lax.rem(clip, 4)
        self.yhi = lax.div(stripe, 2)
        self.core = lax.rem(stripe, 2)

    def at_x(self, x):
        return (self.ylo * 16 + x * 4 + self.z, self.stripe)

    def at_z(self, z):
        return (self.ylo * 16 + self.x * 4 + z, self.stripe)

    def ring(self, axis, step):
        there = lax.rem((self.x if axis == 0 else self.z) + step, 4)
        return (self.at_x(there) if axis == 0 else self.at_z(there)), there

    def along(self, axis, step):
        x = lax.rem(self.x + step * (1 - axis), 4)
        z = lax.rem(self.z + step * axis, 4)
        return (self.ylo * 16 + x * 4 + z, self.stripe), x + (z - x) * axis

    def on_ring(self, axis):
        return self.x if axis == 0 else self.z

    def sibling(self):
        return (self.clip, self.yhi * 2 + 1 - self.core)

    def mirror(self):
        return ((1 - self.ylo) * 16 + self.x * 4 + self.z, (1 - self.yhi) * 2 + self.core)

    def twin(self):
        return ((1 - self.ylo) * 16 + self.x * 4 + self.z, self.stripe)

    def in_group(self, step):
        there = lax.rem(self.stripe + step, 4)
        return (self.clip, there), there


def enter(devices):
    barrier = pltpu.get_barrier_semaphore()
    for device in devices:
        pl.semaphore_signal(barrier, inc=1, device_id=device, device_id_type=MESH)
    pl.semaphore_wait(barrier, len(devices))


class Sems:
    def __init__(self, send, recv):
        self.send, self.recv, self.used = send, recv, 0

    def copy(self, src, dst, device):
        at = self.used
        self.used += 1
        return pltpu.make_async_remote_copy(
            src_ref=src,
            dst_ref=dst,
            send_sem=self.send.at[at],
            recv_sem=self.recv.at[at],
            device_id=device,
            device_id_type=MESH,
        )


def rows_at(start, size, grain):
    return pl.ds(pl.multiple_of(start * grain, grain), size)


class Buf:
    def __init__(self, shape, dtype, space=pltpu.VMEM, array=None):
        self.shape, self.dtype, self.space, self.array = shape, dtype, space, array


def given(array, space=pltpu.VMEM):
    return Buf(array.shape, array.dtype, space, array)


def dma(*shape):
    return pltpu.SemaphoreType.DMA(shape)


def call_kernel(body, collective_id, ins, outs, scratch):
    leaves, trees = zip(*(jax.tree.flatten(part) for part in (ins, outs, scratch)))
    ends = [len(leaves[0]), len(leaves[0]) + len(leaves[1])]

    def kernel(*refs):
        parts = (refs[: ends[0]], refs[ends[0] : ends[1]], refs[ends[1] :])
        groups = [jax.tree.unflatten(tree, part) for tree, part in zip(trees, parts)]
        body(SimpleNamespace(**groups[0], **groups[1], **groups[2]))

    results = pl.pallas_call(
        kernel,
        out_shape=[jax.ShapeDtypeStruct(b.shape, b.dtype) for b in leaves[1]],
        in_specs=[pl.BlockSpec(memory_space=b.space) for b in leaves[0]],
        out_specs=[pl.BlockSpec(memory_space=b.space) for b in leaves[1]],
        scratch_shapes=[
            pltpu.VMEM(b.shape, b.dtype) if isinstance(b, Buf) else b for b in leaves[2]
        ],
        compiler_params=pltpu.CompilerParams(
            collective_id=collective_id,
            has_side_effects=collective_id is not None,
            vmem_limit_bytes=62 * 2**20,
        ),
        name=body.__name__,
    )(*[b.array for b in leaves[0]])
    return SimpleNamespace(**jax.tree.unflatten(trees[1], results))


CHUNKS = 6
STAGES = 10
SIDE = 384


def add_into(out, *terms, rows=64):
    if len(terms) == 2 and all(t.dtype == out.dtype for t in terms):

        @pl.loop(0, out.shape[0] // 96)
        def _(step):
            at = pl.ds(pl.multiple_of(step * 96, 96), 96)
            out[at, :] = terms[0][at, :] + terms[1][at, :]

        return
    height = out.shape[0]
    rows = math.gcd(rows, height)

    @pl.loop(0, height // rows)
    def _(step):
        at = pl.ds(pl.multiple_of(step * rows, rows), rows)
        total = terms[0][at, :].astype(f32)
        for term in terms[1:]:
            total = total + term[at, :].astype(f32)
        out[at, :] = total.astype(out.dtype)


class Reduce:
    def __init__(self, place, bufs, outs):
        self.place, self.bufs, self.outs = place, bufs, outs
        self.flight = {}

    def go(self, key, *plans):
        k, stage = key
        sems = Sems(self.bufs.send.at[k % 2], self.bufs.recv.at[k % 2])
        sems.used = (0, 2, 6, 10, 11, 17, 18, 24, 28)[stage]
        copies = [sems.copy(*plan) for plan in plans]
        for copy in copies:
            copy.start()
        self.flight[key] = copies

    def land(self, *key):
        for copy in self.flight.pop(key):
            copy.wait()

    def cols(self, axis):
        return pl.ds(axis * SIDE, SIDE)

    def own(self, k, axis, step, half=None):
        there = self.place.ring(axis, step)[1] * 192
        size = 192
        if half is not None:
            there, size = there + 96 * half, 96
        rows = rows_at(there // 32, size, 32)
        return self.bufs.grads.at[k % 2, :, self.place.core, rows, self.cols(axis)]

    def step(self, stage, k):
        place, b, bufs = self.place, k % 2, self.bufs
        here = k, stage
        if stage > 0:
            self.land(k, stage - 1)
        if stage == 0:
            other = 1 - place.core
            self.go(
                here,
                *[
                    (bufs.grads.at[b, h, other], bufs.side.at[b, h], place.sibling())
                    for h in range(2)
                ],
            )
        elif stage == 1:
            for h in range(2):
                part = bufs.grads.at[b, h, place.core]
                add_into(part, part, bufs.side.at[b, h])
            self.go(
                here,
                *[
                    (
                        self.own(k, axis, 2, way),
                        bufs.relay.at[b, axis, way],
                        place.ring(axis, 1 + 2 * way)[0],
                    )
                    for axis in range(2)
                    for way in range(2)
                ],
            )
        elif stage == 2:
            plans = []
            for axis in range(2):
                for way in range(2):
                    for h in range(2):
                        half = self.own(k, axis, 1 + 2 * way, way).at[h]
                        add_into(half, half, bufs.relay.at[b, axis, way, h], rows=96)
                    device, _ = place.ring(axis, 1 + 2 * way)
                    piece = self.own(k, axis, 1 + 2 * way)
                    plans.append((piece, bufs.ring.at[b, axis, way], device))
            self.go(here, *plans)
        elif stage == 3:
            for axis in range(2):
                for h in range(2):
                    add_into(
                        bufs.sums.at[b, h, axis],
                        self.own(k, axis, 0).at[h],
                        *[bufs.ring.at[b, axis, way, h] for way in range(2)],
                    )
            self.go(
                here, (bufs.sums.at[b, 1 - place.yhi], bufs.cross.at[b], place.mirror())
            )
        elif stage == 4:
            for axis in range(2):
                ours = bufs.ours.at[b, axis]
                add_into(ours, bufs.sums.at[b, place.yhi, axis], bufs.cross.at[b, axis])
            plans = []
            for step in (1, 3, 2):
                for axis in range(2):
                    device, there = place.ring(1 - axis, step)
                    piece = bufs.ours.at[b, axis, rows_at(there, 48, 48)]
                    plans.append((piece, bufs.ring2.at[b, axis, step - 1], device))
            self.go(here, *plans)
        elif stage == 5:
            for axis in range(2):
                mine = rows_at(place.on_ring(1 - axis), 48, 48)
                add_into(
                    bufs.small.at[b, axis],
                    bufs.ours.at[b, axis, mine],
                    *[bufs.ring2.at[b, axis, step] for step in range(3)],
                    rows=48,
                )
            self.go(here, (bufs.small.at[b], bufs.twin.at[b], place.twin()))
        elif stage == 6:
            plans = []
            for axis in range(2):
                start = place.on_ring(axis) * 12 + place.on_ring(1 - axis) * 3
                piece = bufs.final.at[k, rows_at(start, 48, 16), self.cols(axis)]
                piece[...] = bufs.small[b, axis] + bufs.twin[b, axis]
                for step in (1, 3, 2):
                    plans.append((piece, piece, place.ring(1 - axis, step)[0]))
            self.go(here, *plans)
        elif stage == 7:
            plans = []
            for axis in range(2):
                mine = rows_at(place.on_ring(axis), 192, 192)
                piece = bufs.final.at[k, mine, self.cols(axis)]
                for step in (1, 3):
                    plans.append((piece, piece, place.ring(axis, step)[0]))
            self.go(here, *plans)
        elif stage == 8:
            plans = []
            for axis in range(2):
                for way in range(2):
                    came = place.ring(axis, 3 - 2 * way)[1]
                    rows = rows_at(came * 2 + way, 96, 96)
                    piece = bufs.final.at[k, rows, self.cols(axis)]
                    plans.append((piece, piece, place.ring(axis, 1 + 2 * way)[0]))
            self.go(here, *plans)
        else:
            copies = []
            layer, member = 1 - k // 3, k % 3
            for j in range(4):
                block = bufs.final.at[k, pl.ds(j * 192, 192)]
                wide = pl.ds(j * 768, 768)
                if member == 0:
                    to = self.outs.down.at[layer, pl.ds(j * 192, 192)]
                elif member == 1:
                    to = self.outs.up.at[layer, :, wide]
                elif j < 3:
                    to = self.outs.qkv.at[layer, :, wide]
                else:
                    to = self.outs.out.at[layer]
                copies.append(pltpu.make_async_copy(block, to, bufs.store.at[k, j]))
            for copy in copies:
                copy.start()
            self.flight[here] = copies

    def end(self):
        for key in list(self.flight):
            self.land(*key)


class ReduceSmall:
    def __init__(self, place, bufs):
        self.place, self.bufs = place, bufs
        self.sems = Sems(bufs.little_send, bufs.little_recv)

    def go(self, copies):
        for copy in copies:
            copy.start()
        self.flight = copies

    def land(self):
        for copy in self.flight:
            copy.wait()

    def step(self, stage):
        place, bufs, sems = self.place, self.bufs, self.sems
        if stage == 0:
            copies = []
            for step in (1, 2, 3):
                device, there = place.in_group(step)
                copies.append(sems.copy(bufs.pack.at[there], bufs.pack_land.at[step - 1], device))
            self.go(copies)
        elif stage == 1:
            self.land()
            total = bufs.pack[place.stripe]
            for step in range(3):
                total = total + bufs.pack_land[step]
            mine = bufs.everyone.at[place.ylo, place.x, place.z]
            mine[...] = total.astype(bf16)
            self.go([sems.copy(mine, mine, place.ring(0, step)[0]) for step in (1, 2, 3)])
        elif stage == 2:
            self.land()
            mine = bufs.everyone.at[place.ylo, :, place.z]
            self.go([sems.copy(mine, mine, place.ring(1, step)[0]) for step in (1, 2, 3)])
        elif stage == 3:
            self.land()
            mine = bufs.everyone.at[place.ylo]
            self.go([sems.copy(mine, mine, place.twin())])
        elif stage == 4:
            self.land()


class Gather:
    STEPS = ("begin", "fetched", "passed", "relay", "share", "end")

    def __init__(self, place, sems, own, full, local_sem):
        self.place, self.sems, self.own, self.full = place, sems, own, full
        rows, columns = own.shape
        self.quarter, self.half = rows // 4, columns // 2
        self.other = (1 - place.yhi) * 2 + place.core
        self.kept = pltpu.make_async_copy(own, full.at[place.stripe], local_sem)
        self.rings, self.relays = [], []

    def spot(self, axis, step=0, start=0, size=None):
        rows = rows_at(self.place.along(axis, step)[1], self.quarter, self.quarter)
        cols = pl.ds(pl.multiple_of(axis * self.half + start, 128), size or self.half)
        return rows, cols

    def go(self, plans):
        copies = [self.sems.copy(*plan) for plan in plans]
        for copy in copies:
            copy.start()
        return copies

    def begin(self):
        place = self.place
        spot = self.spot(1 - place.ylo)
        self.first, self.side = self.go(
            [
                (self.own.at[spot], self.full.at[(place.stripe, *spot)], place.mirror()),
                (self.own, self.full.at[place.stripe], place.sibling()),
            ]
        )
        self.kept.start()

    def spread(self, axis):
        piece = self.full.at[(self.other, *self.spot(axis))]
        self.rings += self.go(
            [(piece, piece, self.place.along(axis, step)[0]) for step in (1, 3)]
        )

    def fetched(self):
        place = self.place
        self.first.wait()
        self.spread(place.ylo)
        piece = self.full.at[(self.other, *self.spot(place.ylo))]
        self.second = self.go([(piece, piece, place.twin())])

    def passed(self):
        self.second[0].wait()
        self.spread(1 - self.place.ylo)

    def relay(self, nth):
        cut = -(-self.half // 256) * 128
        axis = (1 - nth) * self.place.ylo + nth * (1 - self.place.ylo)
        for copy in self.rings[2 * nth : 2 * nth + 2]:
            copy.wait()
        plans = []
        for way in range(2):
            start, size = (0, cut) if way == 0 else (cut, self.half - cut)
            piece = self.full.at[(self.other, *self.spot(axis, 3 - 2 * way, start, size))]
            plans.append((piece, piece, self.place.along(axis, 1 + 2 * way)[0]))
        self.relays += self.go(plans)

    def share(self):
        for copy in self.relays:
            copy.wait()
        piece = self.full.at[self.other]
        self.last = self.go([(piece, piece, self.place.sibling())])

    def end(self):
        self.kept.wait()
        self.side.wait()
        for copy in self.last:
            copy.wait()


class QuickGather(Gather):
    def begin(self):
        place = self.place
        spots = [self.spot(axis) for axis in range(2)]
        plans = [(self.own.at[s], self.full.at[(place.stripe, *s)], place.mirror()) for s in spots]
        plans.append((self.own, self.full.at[place.stripe], place.sibling()))
        *self.first, self.side = self.go(plans)
        self.kept.start()

    def fetched(self):
        for axis in range(2):
            self.first[axis].wait()
            piece = self.full.at[(self.other, *self.spot(axis))]
            self.relays += self.go(
                [(piece, piece, self.place.along(axis, step)[0]) for step in (1, 3, 2)]
            )

    def passed(self):
        pass

    def relay(self, nth):
        pass


def trans_dot(left, right):
    return lax.dot_general(left, right, (((0,), (0,)), ((), ())), preferred_element_type=f32)


def right_dot(left, right):
    return lax.dot_general(left, right, (((1,), (1,)), ((), ())), preferred_element_type=f32)


def dot(left, right):
    return jnp.dot(left, right, preferred_element_type=f32)


def norm_rows(values):
    centred = values - jnp.mean(values, axis=-1, keepdims=True)
    spread = jnp.mean(centred * centred, axis=-1, keepdims=True)
    rate = lax.rsqrt(spread + 1e-06)
    return centred * rate, rate


def norm_pull(grad, normed, rate):
    along = jnp.mean(grad * normed, axis=-1, keepdims=True)
    return rate * (grad - jnp.mean(grad, axis=-1, keepdims=True) - normed * along)


def over_rows(values):
    return jnp.sum(values, axis=0, keepdims=True)


def gelu_and_slope(v):
    square = v * v
    t = jnp.tanh(0.7978845608028654 * (v + 0.044715 * (square * v)))
    half = 0.5 * (1.0 + t)
    inner = 0.7978845608028654 * (1.0 + 0.134145 * square)
    return v * half, half + 0.5 * v * (1.0 - t * t) * inner


class Small:
    def __init__(self, ref):
        self.ref = ref

    def spot(self, layer, member, half):
        unit = 2 * member + half
        return unit // 3, 4 + 3 * layer + unit % 3

    def mod(self, layer, member):
        spots = [self.spot(layer, member, half) for half in range(2)]
        return jnp.concatenate([self.ref[s, r : r + 1, :] for s, r in spots], axis=1)

    def put_mod(self, layer, member, value):
        for half in range(2):
            s, r = self.spot(layer, member, half)
            self.ref[s, r : r + 1, :] = value[:, half * 384 : (half + 1) * 384]

    def bias(self, layer, s):
        return jnp.concatenate(
            [self.ref[s, 2 * layer + half : 2 * layer + half + 1, :] for half in range(2)], axis=1
        )

    def put_bias(self, layer, s, value):
        for half in range(2):
            r = 2 * layer + half
            self.ref[s, r : r + 1, :] = value[:, half * 384 : (half + 1) * 384]


def frame_major():
    for group in range(2):
        for frame in range(4):
            start = group * 128 + frame * 32
            yield slice(start, start + 32), frame, slice(group * 32, group * 32 + 32)


def head_mask(half):
    lane = lax.broadcasted_iota(jnp.int32, (1, 128), 1)
    return (lane >= 64 * half) & (lane < 64 * half + 64)


def same_patch():
    row = lax.broadcasted_iota(jnp.int32, (128, 128), 0)
    col = lax.broadcasted_iota(jnp.int32, (128, 128), 1)
    return lax.rem(row, 32) == lax.rem(col, 32)


def attend(qkv, attended, probs, spatial, first, last):
    size = ROWS if spatial else 128

    @pl.loop(first, last, unroll=True)
    def _(pair):
        def cols(member):
            return pl.ds(pl.multiple_of(member * WIDTH + pair * 128, 128), 128)

        for group in range(ROWS // size):
            here = slice(group * size, (group + 1) * size)
            query, key, value = (qkv[here, cols(member)] for member in range(3))
            query = query * jnp.asarray(HEAD**-0.5, bf16)
            outs = []
            for half in range(2):
                picked = jnp.where(head_mask(half), query, jnp.zeros_like(query))
                scores = right_dot(picked, key)
                if not spatial:
                    scores = jnp.where(same_patch(), scores, -1e30)
                expo = jnp.exp(scores - jnp.max(scores, axis=-1, keepdims=True))
                weight = (expo * (1.0 / jnp.sum(expo, axis=-1, keepdims=True))).astype(bf16)
                probs[pair * 2 + half, here, 0:size] = weight
                outs.append(dot(weight, value))
            attended[here, cols(0)] = jnp.where(head_mask(0), outs[0], outs[1]).astype(bf16)


def attend_back(qkv, probs, grad_att, grad_qkv, spatial, first, last):
    size = ROWS if spatial else 128
    scale = HEAD**-0.5

    @pl.loop(first, last, unroll=True)
    def _(pair):
        def cols(member):
            return pl.ds(pl.multiple_of(member * WIDTH + pair * 128, 128), 128)

        for group in range(ROWS // size):
            here = slice(group * size, (group + 1) * size)
            query, key, value = (qkv[here, cols(member)] for member in range(3))
            grad = grad_att[here, cols(0)]
            found = []
            for half in range(2):
                picked = jnp.where(head_mask(half), grad, jnp.zeros_like(grad))
                weight = probs[pair * 2 + half, here, 0:size]
                wide = weight.astype(f32)
                pull = wide * right_dot(picked, value)
                centre = jnp.sum(pull, axis=-1, keepdims=True)
                grad_scores = ((pull - wide * centre) * scale).astype(bf16)
                found.append(
                    (
                        dot(grad_scores, key),
                        trans_dot(grad_scores, query),
                        trans_dot(weight, grad),
                    )
                )
            for member in range(3):
                both = jnp.where(head_mask(0), found[0][member], found[1][member])
                grad_qkv[here, cols(member)] = both.astype(bf16)


class Weights(NamedTuple):
    qkv: Any
    out: Any
    up: Any
    down: Any


class Saved(NamedTuple):
    normed1: Any
    unit1: Any
    rate1: Any
    qkv: Any
    probs: Any
    attended: Any
    branch: Any
    unit2: Any
    rate2: Any
    normed2: Any
    slope: Any
    hidden: Any
    mlp: Any


FULL = Weights((4, 192, 2304), (4, 192, 768), (4, 192, 3072), (4, 768, 768))
SAVED = Saved(
    normed1=Buf((ROWS, WIDTH), bf16),
    unit1=Buf((ROWS, WIDTH), bf16),
    rate1=Buf((ROWS, 128), f32),
    qkv=Buf((ROWS, 3 * WIDTH), bf16),
    probs=Buf((12, ROWS, ROWS), bf16),
    attended=Buf((ROWS, WIDTH), bf16),
    branch=Buf((ROWS, WIDTH), bf16),
    unit2=Buf((ROWS, WIDTH), bf16),
    rate2=Buf((ROWS, 128), f32),
    normed2=Buf((ROWS, WIDTH), bf16),
    slope=Buf((ROWS, 4 * WIDTH), bf16),
    hidden=Buf((ROWS, 4 * WIDTH), bf16),
    mlp=Buf((ROWS, WIDTH), bf16),
)


class Keep:
    def __init__(self, near, far, layer, sem, inward):
        copies = []
        for at, (a, b) in enumerate(zip(near, far)):
            a, b = (b.at[layer], a) if inward else (a, b.at[layer])
            copies.append(pltpu.make_async_copy(a, b, sem.at[at]))
        self.copies = Saved(*copies)

    def start(self, pick):
        for copy in pick(self.copies):
            copy.start()

    def wait(self, pick):
        for copy in pick(self.copies):
            copy.wait()


def spread_lanes(value):
    return jnp.broadcast_to(value, (ROWS, 128))


def whole(ref, cols=slice(None)):
    value = ref[:, :, cols]
    return value.reshape(value.shape[0] * value.shape[1], value.shape[2])


def forward_block(layer, rows, mid, near, keep, small, weights, move):
    unit, rate = norm_rows(rows[...])
    near.unit1[...] = unit.astype(bf16)
    near.rate1[...] = spread_lanes(rate)
    shift, scale = small.mod(layer, 0), small.mod(layer, 1)
    near.normed1[...] = (unit * (1.0 + scale) + shift).astype(bf16)
    keep.start(lambda k: (k.unit1, k.rate1, k.normed1))
    if layer == 0:
        move()
    move()
    move()
    for j in range(3):
        cols = slice(j * WIDTH, (j + 1) * WIDTH)
        near.qkv[:, cols] = dot(near.normed1[...], whole(weights.qkv, cols)).astype(bf16)
        if j > 0:
            move()
    keep.start(lambda k: (k.qkv,))
    for pair in range(0, 6, 3):
        attend(near.qkv, near.attended, near.probs, layer == 0, pair, pair + 3)
        move()
    move()
    keep.start(lambda k: (k.probs, k.attended))
    move()
    branch = dot(near.attended[...], whole(weights.out))
    near.branch[...] = branch.astype(bf16)
    mid[...] = rows[...] + small.mod(layer, 2) * branch
    unit, rate = norm_rows(mid[...])
    near.unit2[...] = unit.astype(bf16)
    near.rate2[...] = spread_lanes(rate)
    shift, scale = small.mod(layer, 3), small.mod(layer, 4)
    near.normed2[...] = (unit * (1.0 + scale) + shift).astype(bf16)
    keep.start(lambda k: (k.branch, k.unit2, k.rate2, k.normed2))
    move()
    move()
    for j in range(4):
        cols = slice(j * WIDTH, (j + 1) * WIDTH)
        pre = dot(near.normed2[...], whole(weights.up, cols)) + small.bias(layer, j)
        hidden, slope = gelu_and_slope(pre)
        near.hidden[:, cols] = hidden.astype(bf16)
        near.slope[:, cols] = slope.astype(bf16)
        move()
    keep.start(lambda k: (k.hidden, k.slope))
    move()
    mlp = dot(near.hidden[...], whole(weights.down))
    near.mlp[...] = mlp.astype(bf16)
    keep.start(lambda k: (k.mlp,))
    rows[...] = mid[...] + small.mod(layer, 5) * mlp
    move()


def group_peers(place):
    return [place.in_group(step)[0] for step in (1, 2, 3)]


def ring_peers(place):
    return [place.ring(axis, step)[0] for axis in range(2) for step in (1, 2, 3)]


class Swap:
    def __init__(self, place, sems, source, result, local_sem):
        self.copies = []
        for step in (2, 1, 3):
            device, there = place.in_group(step)
            self.copies.append(sems.copy(source.at[there], result.at[place.stripe], device))
        mine = place.stripe
        self.copies.append(pltpu.make_async_copy(source.at[mine], result.at[mine], local_sem))

    def start(self):
        for copy in self.copies:
            copy.start()

    def wait(self):
        for copy in self.copies:
            copy.wait()


ARRIVALS = (
    ((0, 0), (1, 0),),
    ((2, 0), (3, 0), (0, 1), (1, 1), (4, 0), (5, 0), (6, 0), (7, 0),),
    (),
    (),
    ((0, 5), (1, 5), (0, 6),),
    ((2, 1),),
    (),
    (),
    (),
    ((3, 1),),
    ((2, 5),),
    ((1, 6),),
    (),
    ((2, 6),),
    ((4, 1),),
    ((5, 1),),
    ((3, 5),),
    (),
    ((3, 6),),
    ((4, 5),),
    ((6, 1), (5, 5),),
    (),
    ((4, 6),),
    ((7, 1),),
    (),
    ((6, 5),),
    (),
    ((7, 5),),
    (),
    ((5, 6),),
    (),
    ((6, 6),),
    (),
    (),
    (),
    (),
    ((7, 6),),
    (),
)


def forward_blocks(refs):
    place = Place()
    enter(group_peers(place) + [place.mirror(), place.twin()] + ring_peers(place))
    sems = Sems(refs.send, refs.recv)
    local = refs.local
    greet = []
    for step in (1, 2, 3):
        device, _ = place.in_group(step)
        greet.append(sems.copy(refs.small, refs.small_all.at[place.stripe], device))
    mine = refs.small_all.at[place.stripe]
    greet.append(pltpu.make_async_copy(refs.small, mine, local.at[0]))

    g, outward = [], []
    for layer in range(2):
        for own, full, far in zip(refs.shards, refs.full, refs.far):
            at = len(g)
            kind = QuickGather
            g.append(kind(place, sems, own.at[layer], full.at[layer], local.at[2 + at]))
            outward.append(
                pltpu.make_async_copy(full.at[layer], far.at[layer], local.at[10 + at])
            )
    points = iter(ARRIVALS)

    def move():
        for at, step in next(points):
            one = g[at]
            (
                one.begin, one.fetched, one.passed, lambda: one.relay(0), lambda: one.relay(1),
                one.share, one.end
            )[step]()
            if step == 6:
                outward[at].start()

    for copy in greet:
        copy.start()
    move()
    swap = Swap(place, sems, refs.tokens, refs.frame, local.at[1])
    swap.start()
    move()
    for copy in greet:
        copy.wait()
    swap.wait()
    move()
    small = Small(refs.small_all)
    rows = refs.rows
    for j in range(4):
        rows[j * 64 : (j + 1) * 64, :] = refs.frame[j].astype(f32)
    keeps = []
    for layer in range(2):
        keep = Keep(refs.near[layer], refs.saved, layer, refs.keep.at[layer], False)
        keeps.append(keep)
        weights = Weights(*[full.at[layer] for full in refs.full])

        forward_block(layer, rows, refs.mid, refs.near[layer], keep, small, weights, move)
        if layer == 0:
            for j in range(4):
                refs.turn[j] = rows[j * 64 : (j + 1) * 64, :].astype(bf16)
            swap = Swap(place, sems, refs.turn, refs.turned, local.at[18])
            swap.start()
            move()
            swap.wait()
            move()
            for here, f, patches in frame_major():
                rows[here, :] = refs.turned[f, patches, :].astype(f32)
    for here, f, patches in frame_major():
        refs.block_output[f, patches, :] = rows[here, :].astype(bf16)
    for copy in outward:
        copy.wait()
    for keep in keeps:
        keep.wait(lambda k: k)


def run_forward(small, tokens, shards):
    ins = dict(
        small=given(small),
        tokens=given(tokens),
        shards=Weights(*[given(w, pl.ANY) for w in shards]),
    )
    outs = dict(
        small_all=Buf((4, 16, 384), f32),
        block_output=Buf(tokens.shape, bf16),
        far=Weights(*[Buf((2, *shape), bf16, pl.ANY) for shape in FULL]),
        saved=Saved(*[Buf((2, *b.shape), b.dtype, pl.ANY) for b in SAVED]),
    )
    scratch = dict(
        full=Weights(*[Buf((2, *shape), bf16) for shape in FULL]),
        near=(SAVED, SAVED),
        rows=Buf((ROWS, WIDTH), f32),
        mid=Buf((ROWS, WIDTH), f32),
        frame=Buf(tokens.shape, bf16),
        turn=Buf(tokens.shape, bf16),
        turned=Buf(tokens.shape, bf16),
        send=dma(110),
        recv=dma(110),
        local=dma(20),
        keep=dma(2, len(SAVED)),
    )
    return call_kernel(forward_blocks, 0, ins, outs, scratch)


def backward_block(layer, grad, refs, small, pack, weights, at, leave):
    near, grads, work, gpre, back, gqkv = (
        refs.near, refs.grads, refs.work, refs.gpre, refs.back, refs.gqkv
    )
    at.have(lambda k: (k.mlp, k.hidden))
    b = 1 - layer
    pack.put_mod(layer, 5, over_rows(grad[...] * near.mlp[...].astype(f32)))
    work[...] = (small.mod(layer, 5) * grad[...]).astype(bf16)
    at.move()
    for s in range(4):
        cols = slice(s * WIDTH, (s + 1) * WIDTH)
        grads[b, s // 2, s % 2] = trans_dot(near.hidden[:, cols], work[...]).astype(bf16)
    at.move()
    at.have(lambda k: (k.slope,), lambda w: (w.down,))
    for j in range(4):
        cols = slice(j * WIDTH, (j + 1) * WIDTH)
        pre = (right_dot(work[...], weights.down[j]) * near.slope[:, cols].astype(f32)).astype(bf16)
        gpre[:, cols] = pre
        pack.put_bias(layer, j, over_rows(pre.astype(f32)))
        if j % 2 == 1:
            at.move()
    at.done(lambda k: (k.mlp, k.hidden, k.slope), lambda w: (w.down,))
    at.have(lambda k: (k.unit2, k.rate2, k.normed2), lambda w: (w.up,))
    back[...] = right_dot(gpre[...], whole(weights.up))
    at.move()
    for j in range(4):
        found = trans_dot(near.normed2[...], gpre[:, j * WIDTH : (j + 1) * WIDTH]).astype(bf16)
        for s in range(4):
            rows = slice(j * 192, (j + 1) * 192)
            grads[1 - b, s // 2, s % 2, rows, :] = found[s * 192 : (s + 1) * 192, :]
    at.move()
    pack.put_mod(layer, 3, over_rows(back[...]))
    unit = near.unit2[...].astype(f32)
    pack.put_mod(layer, 4, over_rows(back[...] * unit))
    rate = near.rate2[:, 0:1]
    grad[...] += norm_pull(back[...] * (1.0 + small.mod(layer, 4)), unit, rate)
    at.move()
    at.done(lambda k: (k.unit2, k.rate2, k.normed2), lambda w: (w.up,))
    at.have(lambda k: (k.branch,), lambda w: (w.out,))
    pack.put_mod(layer, 2, over_rows(grad[...] * near.branch[...].astype(f32)))
    work[...] = (small.mod(layer, 2) * grad[...]).astype(bf16)
    refs.gatt[...] = right_dot(work[...], whole(weights.out)).astype(bf16)
    at.move()
    at.have(lambda k: (k.qkv, k.probs))
    for pair in range(0, 6, 2):
        attend_back(near.qkv, near.probs, refs.gatt, gqkv, layer == 0, pair, pair + 2)
        at.move()
        at.move()
    at.done(lambda k: (k.branch, k.qkv, k.probs), lambda w: (w.out,))
    def make():
        at.have(lambda k: (k.normed1, k.attended))
        for j in range(4):
            if j < 3:
                found = trans_dot(near.normed1[...], gqkv[:, j * WIDTH : (j + 1) * WIDTH])
            else:
                found = trans_dot(near.attended[...], work[...])
            found = found.astype(bf16)
            for s in range(4):
                rows = slice(j * 192, (j + 1) * 192)
                grads[b, s // 2, s % 2, rows, :] = found[s * 192 : (s + 1) * 192, :]
        at.move()

    if layer == 0:
        make()
    at.have(lambda k: (k.unit1, k.rate1), lambda w: (w.qkv,))
    back[...] = right_dot(gqkv[...], whole(weights.qkv))
    at.move()
    pack.put_mod(layer, 0, over_rows(back[...]))
    unit = near.unit1[...].astype(f32)
    pack.put_mod(layer, 1, over_rows(back[...] * unit))
    rate = near.rate1[:, 0:1]
    grad[...] += norm_pull(back[...] * (1.0 + small.mod(layer, 1)), unit, rate)
    leave()
    at.move()
    if layer == 1:
        make()
    at.done(lambda k: (k.normed1, k.attended, k.unit1, k.rate1), lambda w: (w.qkv,))


ORDER = (
    (),
    ((0, 0),),
    (),
    (),
    ((1, 0),),
    ((0, 1),),
    (),
    (),
    ((2, 0), (1, 1),),
    (),
    (),
    (),
    (),
    (),
    (),
    ((3, 0),),
    ((0, 2), (2, 1),),
    ((1, 2), (4, 0),),
    ((3, 1),),
    ((0, 3), (2, 2),),
    ((5, 0),),
    (),
    ((4, 1), (6, 0), (1, 3), (3, 2),),
    ((0, 4), (7, 0), (5, 1),),
    ((2, 3),),
    ((1, 4), (4, 2), (8, 0), (6, 1),),
    (),
    (),
    (),
    (),
    (),
    ((3, 3),),
    ((0, 5), (2, 4), (5, 2),),
    ((9, 0),),
    (),
    ((1, 5), (7, 1), (4, 3), (6, 2),),
    ((3, 4), (2, 5), (8, 1), (5, 3), (7, 2), (4, 4), (6, 3), (3, 5), (9, 1), (8, 2), (5, 4), (7, 3), (9, 2), (4, 5), (6, 4), (8, 3), (5, 5), (7, 4), (9, 3), (6, 5), (8, 4), (7, 5), (9, 4), (8, 5), (9, 5),),
)


class Progress:
    def __init__(self, reduce, keeps, fetches):
        self.reduce, self.keeps, self.fetches = reduce, keeps, fetches
        self.point, self.layer = 0, 1

    def have(self, saved, weights=lambda w: ()):
        self.keeps[self.layer].wait(saved)
        for copy in weights(self.fetches[self.layer]):
            copy.wait()

    def done(self, saved, weights=lambda w: ()):
        if self.layer == 1:
            self.keeps[0].start(saved)
            for copy in weights(self.fetches[0]):
                copy.start()

    def move(self):
        for stage, k in ORDER[self.point]:
            self.reduce.step(stage, k)
        self.point += 1


def backward_blocks(refs):
    place = Place()
    enter(group_peers(place) + [place.mirror(), place.twin()] + ring_peers(place))
    keeps = [Keep(refs.near, refs.saved, layer, refs.keep.at[layer], True) for layer in range(2)]
    fetches = []
    for layer in range(2):
        copies = [
            pltpu.make_async_copy(far.at[layer], near, refs.fetch.at[layer, at])
            for at, (far, near) in enumerate(zip(refs.far, refs.weights))
        ]
        fetches.append(Weights(*copies))
    keeps[1].start(lambda k: (k.mlp, k.hidden, k.slope))
    fetches[1].down.start()
    keeps[1].start(lambda k: (k.unit2, k.rate2, k.normed2, k.branch))
    fetches[1].up.start()
    fetches[1].out.start()
    keeps[1].start(lambda k: (k.qkv, k.probs, k.normed1, k.attended, k.unit1, k.rate1))
    fetches[1].qkv.start()

    grad = refs.grad
    weight = refs.loss_weight[0]
    for here, f, patches in frame_major():
        grad[here, :] = refs.cotangent[f, patches, :].astype(f32) * weight
    small, pack = Small(refs.small_all), Small(refs.pack)
    refs.pack[...] = refs.base[...]

    reduce = Reduce(place, refs, refs.sums_out)
    little = ReduceSmall(place, refs)
    at = Progress(reduce, keeps, fetches)
    swap_sems = Sems(refs.swap_send, refs.swap_recv)
    swaps = [
        Swap(place, swap_sems, refs.turn.at[layer], result, refs.swap_local.at[layer])
        for layer, result in ((1, refs.turned), (0, refs.grad_input))
    ]

    def leave_temporal():
        for here, f, patches in frame_major():
            refs.turn[1, f, patches, :] = grad[here, :].astype(bf16)
        swaps[0].start()

    def leave_spatial():
        for j in range(4):
            refs.turn[0, j] = grad[j * 64 : (j + 1) * 64, :].astype(bf16)
        swaps[1].start()

    backward_block(1, grad, refs, small, pack, refs.weights, at, leave_temporal)
    swaps[0].wait()
    for j in range(4):
        grad[j * 64 : (j + 1) * 64, :] = refs.turned[j].astype(f32)
    at.move()
    at.layer = 0
    backward_block(0, grad, refs, small, pack, refs.weights, at, leave_spatial)
    at.move()
    rest = ORDER[at.point]
    for nth, (stage, k) in enumerate(rest):
        if nth % 5 == 0 and nth // 5 < 5:
            little.step(nth // 5)
        reduce.step(stage, k)
    swaps[1].wait()
    reduce.end()


def run_backward(forward, cotangent, loss_weight, base):
    ins = dict(
        cotangent=given(cotangent),
        loss_weight=given(loss_weight, pltpu.SMEM),
        base=given(base),
        small_all=given(forward.small_all),
        far=Weights(*[given(w, pl.ANY) for w in forward.far]),
        saved=Saved(*[given(w, pl.ANY) for w in forward.saved]),
    )
    outs = dict(
        grad_input=Buf(cotangent.shape, bf16),
        everyone=Buf((2, 4, 4, 16, 384), bf16),
        sums_out=Weights(
            *[
                Buf(shape, bf16, pl.ANY)
                for shape in ((2, 192, 2304), (2, 192, 768), (2, 192, 3072), (2, 768, 768))
            ]
        ),
    )
    scratch = dict(
        grads=Buf((2, 2, 2, 768, 768), bf16),
        side=Buf((2, 2, 768, 768), bf16),
        relay=Buf((2, 2, 2, 2, 96, SIDE), bf16),
        ring=Buf((2, 2, 2, 2, 192, SIDE), bf16),
        sums=Buf((2, 2, 2, 192, SIDE), bf16),
        cross=Buf((2, 2, 192, SIDE), bf16),
        ours=Buf((2, 2, 192, SIDE), bf16),
        ring2=Buf((2, 2, 3, 48, SIDE), bf16),
        small=Buf((2, 2, 48, SIDE), bf16),
        twin=Buf((2, 2, 48, SIDE), bf16),
        final=Buf((CHUNKS, 768, 768), bf16),
        near=SAVED,
        weights=Weights(*[Buf(shape, bf16) for shape in FULL]),
        grad=Buf((ROWS, WIDTH), f32),
        back=Buf((ROWS, WIDTH), f32),
        work=Buf((ROWS, WIDTH), bf16),
        gatt=Buf((ROWS, WIDTH), bf16),
        gpre=Buf((ROWS, 4 * WIDTH), bf16),
        gqkv=Buf((ROWS, 3 * WIDTH), bf16),
        turn=Buf((2, *cotangent.shape), bf16),
        turned=Buf(cotangent.shape, bf16),
        pack=Buf((4, 16, 384), f32),
        pack_land=Buf((3, 16, 384), f32),
        send=dma(2, 32),
        recv=dma(2, 32),
        store=dma(CHUNKS, 4),
        keep=dma(2, len(SAVED)),
        fetch=dma(2, len(FULL)),
        little_send=dma(10),
        little_recv=dma(10),
        swap_send=dma(6),
        swap_recv=dma(6),
        swap_local=dma(2),
    )
    return call_kernel(backward_blocks, 4, ins, outs, scratch)


def finish(refs):
    copies = []

    def load(far, near):
        copies.append(pltpu.make_async_copy(far, near, refs.sems.at[len(copies)]))
        copies[-1].start()
        return copies[-1]

    loads = {at: load(refs.sums_in[at], refs.near[at]) for at in (1, 0, 2, 3)}
    stores = []
    for at in (1, 0, 2, 3):
        loads[at].wait()
        near, wide, far = refs.near[at], refs.wide[at], refs.sums_out[at]
        for layer in range(2):
            rows = near.shape[1]

            @pl.loop(0, rows // 32)
            def _(step, layer=layer, near=near, wide=wide):
                here = pl.ds(pl.multiple_of(step * 32, 32), 32)
                wide[layer, here, :] = near[layer, here, :].astype(f32)

            stores.append(load(wide.at[layer], far.at[layer]))
    refs.grad_input[...] = refs.grad[...].astype(f32)
    everyone = refs.everyone[...].astype(f32)
    embed = jnp.concatenate([everyone[:, 10, :], everyone[:, 11, :]], axis=1).astype(bf16)
    for layer in range(2):
        for part in range(3):
            cols = pl.ds(part * 384, 384)
            change = everyone[:, 4 + 3 * layer + part, :]
            refs.b_mod[layer : layer + 1, cols] = over_rows(change)
            refs.mod[layer, :, cols] = trans_dot(embed, change.astype(bf16))
        stores.append(load(refs.mod.at[layer], refs.w_mod.at[layer]))
        for half in range(2):
            value = over_rows(everyone[:, 2 * layer + half, :])
            refs.b_up[layer : layer + 1, pl.ds(half * 384, 384)] = value
    for copy in stores:
        copy.wait()


def run_finish(back):
    ins = dict(
        everyone=given(back.everyone.reshape(32, 16, 384)),
        grad=given(back.grad_input),
        sums_in=Weights(*[given(w, pl.ANY) for w in back.sums_out]),
    )
    shapes = [w.shape for w in back.sums_out]
    outs = dict(
        grad_input=Buf(back.grad_input.shape, f32),
        w_mod=Buf((2, 768, 1152), f32, pl.ANY),
        b_mod=Buf((2, 1152), f32),
        b_up=Buf((2, 768), f32),
        sums_out=Weights(*[Buf(shape, f32, pl.ANY) for shape in shapes]),
    )
    scratch = dict(
        near=Weights(*[Buf(shape, bf16) for shape in shapes]),
        wide=Weights(*[Buf(shape, f32) for shape in shapes]),
        mod=Buf((2, 768, 1152), f32),
        sems=dma(16),
    )
    return call_kernel(finish, None, ins, outs, scratch)


def silu_plain(values):
    return values / (1.0 + jnp.exp(-values))


def sinusoid(steps, width):
    half = width // 2
    freqs = jnp.exp(-math.log(10000.0) * jnp.arange(half).astype(f32) / half)
    angles = steps.astype(f32)[:, None] * freqs[None, :]
    return jnp.concatenate([jnp.cos(angles), jnp.sin(angles)], axis=1)


def shards(
    clip_tokens, timesteps, loss_weight, cotangent, w_mod, b_mod, w_qkv, w_out, w_up, b_up, w_down
):
    embed = silu_plain(sinusoid(timesteps, WIDTH)).astype(bf16)
    mod_part = jnp.einsum("d,ldm->lm", embed[0], w_mod, preferred_element_type=f32) + b_mod.astype(
        f32
    )
    small = jnp.concatenate([b_up.astype(f32).reshape(4, 384), mod_part.reshape(6, 384)])
    small = jnp.pad(small, ((0, 6), (0, 0)))
    base = jnp.broadcast_to(0.25 * embed.astype(f32).reshape(1, 2, 384), (4, 2, 384))
    base = jnp.pad(base, ((0, 0), (10, 4), (0, 0)))
    forward = run_forward(small, clip_tokens[0], (w_qkv, w_out, w_up, w_down))
    back = run_backward(forward, cotangent[0], loss_weight, base)
    end = run_finish(back)
    sums = end.sums_out
    return (
        forward.block_output[None], end.grad_input[None], end.w_mod, end.b_mod, sums.qkv,
        sums.out, sums.up, end.b_up, sums.down
    )


def solution(mesh):
    rows = P("clip", None, "stripe", None)
    middle, last, clips = P(None, "stripe", None), P(None, None, "stripe"), P("clip")
    vector = P(None, "stripe")
    weights = (last, vector, middle, middle, middle, vector, middle)
    return jax.shard_map(
        shards,
        mesh=mesh,
        in_specs=(rows, clips, clips, rows, *weights),
        out_specs=(rows, rows, *weights),
        check_vma=False,
    )
```
